32 devices in a mesh: dp: 16 (over z, y, x), seq: 2 (over core).
Axes of the slice: x: 2, y: 2, z: 4, core: 2. Of those that a mesh axis runs over, the one named last changes fastest.
Arguments:
- tokens: bfloat16 [16, 1536, 1024], P('dp', 'seq'), may hold values from -6 to 6
- segment_ids: int32 [16, 1536], P('dp'), may hold values from 0 to 5, never falling along the last dimension, each value on 1 to 768 neighbouring positions
- cotangent: bfloat16 [16, 1536, 1024], P('dp', 'seq'), may hold values from -6 to 6
- attention_weights: float32 [4, 1024, 1024], P(None, 'dp'), may hold values from -0.1875 to 0.1875
- feed_weights: float32 [3, 4096, 1024], P(None, 'dp'), may hold values from -0.1875 to 0.1875
- attention_scales: float32 [3, 1024], P(None, 'dp'), may hold values from 0.2 to 1.6, as said below
- feed_scales: float32 [2, 4096], P(None, 'dp'), may hold values from 0.5 to 2
- attention_first: float32 [4, 1024, 1024], P(None, 'dp'), may hold values from -8192 to 8192
- attention_second: float32 [4, 1024, 1024], P(None, 'dp'), may hold values from 235929 to 235929600
- feed_first: float32 [3, 4096, 1024], P(None, 'dp'), may hold values from -8192 to 8192
- feed_second: float32 [3, 4096, 1024], P(None, 'dp'), may hold values from 235929 to 235929600
- attention_scale_first: float32 [3, 1024], P(None, 'dp'), may hold values from -8192 to 8192
- attention_scale_second: float32 [3, 1024], P(None, 'dp'), may hold values from 235929 to 235929600
- feed_scale_first: float32 [2, 4096], P(None, 'dp'), may hold values from -8192 to 8192
- feed_scale_second: float32 [2, 4096], P(None, 'dp'), may hold values from 235929 to 235929600
Outputs:
- output: float32 [16, 1536, 1024], P('dp', 'seq')
- input_grad: float32 [16, 1536, 1024], P('dp', 'seq')
- attention_grad: float32 [4, 1024, 1024], P(None, 'dp')
- feed_grad: float32 [3, 4096, 1024], P(None, 'dp')
- attention_scale_grad: float32 [3, 1024], P(None, 'dp')
- feed_scale_grad: float32 [2, 4096], P(None, 'dp')
- attention_change: float32 [4, 1024, 1024], P(None, 'dp')
- feed_change: float32 [3, 4096, 1024], P(None, 'dp')
- attention_scale_change: float32 [3, 1024], P(None, 'dp')
- feed_scale_change: float32 [2, 4096], P(None, 'dp')
The draws below stay inside these ranges and needn't reach their ends.
Inputs may be any that keep to these rules, and one draw needn't show every extreme that they name: `segment_ids`: along a row the ids never fall; each document has 1 to 768 tokens and in every row one has exactly 768. `attention_scales`: the first row lies in 0.9 to 1.6, the other two in 0.2 to 0.8.
All inputs are finite; a program needn't handle non-finite values.
Results may differ from the reference program's by a relative error of at most 0.017.
The reference program's roundings to bfloat16 on the way count: a program that leaves them out, or rounds other values in their place, can miss the bound.
Values may be sent and summed in bfloat16 or wider, within the bound.
No kernel may reach another device: no remote copies, remote signals or barrier semaphores. Data moves between devices by JAX's collectives and lax.ppermute only.
A program may use at most 320 MiB of HBM per device.

```python
import math
import jax
import jax.numpy as jnp
import numpy as np
from jax import lax

D = 1024
FF = 4096
HEADS = 16
HEAD_DIM = 64
LEN = 1536
DOCS = 6
DOC_MOST = 768
ROWS = 16


def draw_attention_scales(key, part):
    first_key, rest_key = jax.random.split(key)
    query_gain = jax.random.uniform(first_key, (1, D), jnp.float32, 0.9, 1.6)
    mixing = jnp.exp(jax.random.uniform(rest_key, (2, D), jnp.float32, math.log(0.2), math.log(0.8)))
    return jnp.concatenate([query_gain, mixing], axis=0)


def levels(stream_key, shape, shards, low, largest):
    def one(dim, blocks):
        draws = jax.random.uniform(jax.random.fold_in(jax.random.fold_in(stream_key, 6), dim), (blocks,), jnp.float32, low / len(shards), largest / len(shards))
        return jnp.repeat(jnp.exp(draws), shape[dim] // blocks).reshape((-1,) + (1,) * (len(shape) - dim - 1))

    gain = one(*shards[0])
    for cut in shards[1:]:
        gain = gain * one(*cut)
    return gain


def profile(amount, total, limit, slope):
    weights = [(1 << 20) // math.isqrt(standing ** slope) + 1 for standing in range(2, amount + 1)]
    spare, given = total - limit - (amount - 1), [1] * (amount - 1)
    while spare > 0:
        candidates = [i for i in range(amount - 1) if given[i] < limit]
        pool, remaining = sum([weights[i] for i in candidates]), spare
        for i in candidates:
            more = min(limit - given[i], max(1, remaining * weights[i] // pool), spare)
            given[i] = given[i] + more
            spare = spare - more
    return np.array([limit] + given)


def ragged_sizes(stream_key, amount, total, most, lean):
    if amount == 2:
        one = jax.random.randint(stream_key, (), max(1, total - most), min(most, total - 1) + 1)
        return jnp.stack([one, total - one])
    sizes = jnp.asarray(profile(amount, total, most, lean), jnp.int32)
    couples = (amount - 1) // 2
    donor, receiver = sizes[1:1 + 2 * couples:2], sizes[2:2 + 2 * couples:2]
    margin = jnp.minimum(donor - 1, most - receiver)
    passed = jax.random.randint(jax.random.fold_in(stream_key, 1), (couples,), 0, 1 << 20) % (margin + 1)
    sizes = sizes.at[1:1 + 2 * couples:2].set(donor - passed).at[2:2 + 2 * couples:2].set(receiver + passed)
    return sizes[jax.random.permutation(jax.random.fold_in(stream_key, 2), amount)]


def noise(own_key, shape, deviation, reach, cuts=(), kind=jnp.bfloat16):
    level = levels(own_key, shape, cuts, -0.22, 0.18) if cuts else 1.0
    values = jax.random.normal(own_key, shape, jnp.float32) * deviation * level
    return jnp.minimum(jnp.maximum(values, -reach), reach).astype(kind)


def setup_inputs(seed: int = 0) -> dict:
    key_of = jax.random.split(jax.random.key(seed), 16)
    return {
        "tokens": noise(key_of[0], (ROWS, LEN, D), 1.0, 6.0, ((0, 16), (1, 2))),
        "segment_ids": jax.vmap(lambda own: jnp.searchsorted(jnp.cumsum(ragged_sizes(own, DOCS, LEN, DOC_MOST, 2)), jnp.arange(LEN), side="right"))(jax.random.split(key_of[1], ROWS)).reshape((ROWS, LEN)).astype(jnp.int32),
        "cotangent": noise(key_of[2], (ROWS, LEN, D), 1.0, 6.0, ((0, 16), (1, 2))),
        "attention_weights": noise(key_of[3], (4, D, D), D ** -0.5, 0.1875, ((1, 16),), jnp.float32),
        "feed_weights": noise(key_of[4], (3, FF, D), D ** -0.5, 0.1875, ((1, 16),), jnp.float32),
        "attention_scales": draw_attention_scales(jax.random.fold_in(key_of[15], 71), 0),
        "feed_scales": jnp.clip(jnp.exp(math.log(2.0) - 1.3862944 * jax.random.uniform(key_of[6], (2, FF), jnp.float32) ** levels(key_of[6], (2, FF), ((1, 16),), -0.2, 0.2)), 0.5, 2.0),
        "attention_first": noise(key_of[7], (4, D, D), LEN, 8192.0, ((1, 16),), jnp.float32),
        "attention_second": jnp.clip(jnp.exp(math.log(235929600) - 6.9077578 * jax.random.uniform(key_of[8], (4, D, D), jnp.float32) ** levels(key_of[8], (4, D, D), ((1, 16),), -0.2, 0.2)), 235929.0, 235929600),
        "feed_first": noise(key_of[9], (3, FF, D), LEN, 8192.0, ((1, 16),), jnp.float32),
        "feed_second": jnp.clip(jnp.exp(math.log(235929600) - 6.9077578 * jax.random.uniform(key_of[10], (3, FF, D), jnp.float32) ** levels(key_of[10], (3, FF, D), ((1, 16),), -0.2, 0.2)), 235929.0, 235929600),
        "attention_scale_first": noise(key_of[11], (3, D), LEN, 8192.0, ((1, 16),), jnp.float32),
        "attention_scale_second": jnp.clip(jnp.exp(math.log(235929600) - 6.9077578 * jax.random.uniform(key_of[12], (3, D), jnp.float32) ** levels(key_of[12], (3, D), ((1, 16),), -0.2, 0.2)), 235929.0, 235929600),
        "feed_scale_first": noise(key_of[13], (2, FF), LEN, 8192.0, ((1, 16),), jnp.float32),
        "feed_scale_second": jnp.clip(jnp.exp(math.log(235929600) - 6.9077578 * jax.random.uniform(key_of[14], (2, FF), jnp.float32) ** levels(key_of[14], (2, FF), ((1, 16),), -0.2, 0.2)), 235929.0, 235929600),
    }


norm_eps = 1e-06
neg_big = -1e+30
rope_base = 10000.0
learn_rate = 0.003
beta_one = 0.9
beta_two = 0.95
adam_eps = 1e-08
corr_one = 1.0 - 0.9 ** 10
corr_two = 1.0 - 0.95 ** 10
highest = lax.Precision.HIGHEST

@jax.custom_vjp
def low(v):
    return lax.optimization_barrier(v.astype(jnp.bfloat16)).astype(jnp.float32)

@jax.custom_vjp
def low_back(v):
    return v

def low_keep(v):
    return (low(v), None)

def low_pass(kept, grad):
    return (grad,)

def back_keep(v):
    return (v, None)

def back_low(kept, grad):
    return (low(grad),)
low.defvjp(low_keep, low_pass)
low_back.defvjp(back_keep, back_low)

def rms_unit(values):
    return values * lax.rsqrt(lax.optimization_barrier(jnp.mean(values * values, axis=-1, keepdims=True)) + norm_eps)

def blend(residual, branch, mixing):
    return rms_unit(residual + mixing * (rms_unit(branch) - residual))

def doc_positions(segments):
    length = segments.shape[-1]
    places = jnp.arange(length, dtype=jnp.int32)
    first_flag = jnp.ones(segments.shape[:-1] + (1,), dtype=jnp.bool_)
    change = jnp.concatenate([first_flag, segments[..., 1:] != segments[..., :-1]], axis=-1)
    starts = jnp.where(change, places, 0).astype(jnp.int32)
    return (places - lax.cummax(starts, axis=segments.ndim - 1)).astype(jnp.int32)

def rotate(values, positions):
    half_dim = values.shape[-1] // 2
    frequency = jnp.exp(jnp.arange(half_dim, dtype=jnp.float32) * (-2.0 * math.log(rope_base) / values.shape[-1]))
    angles = positions.astype(jnp.float32)[..., None, None] * frequency
    cosine_values = jnp.cos(angles)
    sine_values = jnp.sin(angles)
    first_half = values[..., :half_dim]
    second_half = values[..., half_dim:]
    return jnp.concatenate([first_half * cosine_values - second_half * sine_values, first_half * sine_values + second_half * cosine_values], axis=-1)

def heads_unit(projected, positions, scale_row):
    shaped = projected.reshape(projected.shape[:-1] + (HEADS, HEAD_DIM))
    turned = rotate(shaped, positions)
    unit_heads = turned * lax.rsqrt(lax.optimization_barrier(jnp.sum(turned * turned, axis=-1, keepdims=True)) + norm_eps)
    return (unit_heads * scale_row.reshape(HEADS, HEAD_DIM)).reshape(projected.shape)

def swiglu(upward, gating, up_scale, gate_scale):
    return upward * up_scale * jax.nn.silu(gating * gate_scale)

def adam_change(weight, gradient, moment_one, moment_two, renormalize):
    moment_one_new = beta_one * moment_one + (1.0 - beta_one) * gradient
    moment_two_new = beta_two * moment_two + (1.0 - beta_two) * gradient * gradient
    stepped = weight - learn_rate * (moment_one_new / corr_one) / (jnp.sqrt(moment_two_new / corr_two) + adam_eps)
    if renormalize:
        stepped = stepped * lax.rsqrt(lax.optimization_barrier(jnp.sum(stepped * stepped, axis=-1, keepdims=True)) + norm_eps)
    return stepped - weight

def row_layer(inputs, segments, attend_round, feed_round, attend_scale, feed_scale):
    positions = doc_positions(segments)
    query_raw = low_back(jnp.dot(inputs, attend_round[0].T, precision=highest))
    key_raw = low_back(jnp.dot(inputs, attend_round[1].T, precision=highest))
    value_round = low(low_back(jnp.dot(inputs, attend_round[2].T, precision=highest)))
    query_unit = low(heads_unit(query_raw, positions, attend_scale[0]))
    key_unit = low(heads_unit(key_raw, positions, attend_scale[0]))
    places = jnp.arange(segments.shape[0], dtype=jnp.int32)
    allowed = (segments[:, None] == segments[None, :]) & (places[None, :] <= places[:, None])
    score_gain = math.sqrt(HEAD_DIM)

    def one_head(head):
        offset = head * HEAD_DIM
        query_head = lax.dynamic_slice_in_dim(query_unit, offset, HEAD_DIM, 1)
        key_head = lax.dynamic_slice_in_dim(key_unit, offset, HEAD_DIM, 1)
        value_head = lax.dynamic_slice_in_dim(value_round, offset, HEAD_DIM, 1)
        scores = low_back(score_gain * jnp.dot(query_head, key_head.T, precision=highest))
        scores = jnp.where(allowed, scores, neg_big)
        exponent = jnp.exp(scores - lax.optimization_barrier(jnp.max(scores, axis=-1, keepdims=True)))
        probability = low(exponent / lax.optimization_barrier(jnp.sum(exponent, axis=-1, keepdims=True)))
        return jnp.dot(probability, value_head, precision=highest)
    per_head = lax.map(jax.checkpoint(one_head), jnp.arange(HEADS, dtype=jnp.int32))
    mixture = low(low_back(jnp.transpose(per_head, (1, 0, 2)).reshape(inputs.shape)))
    branch = low_back(jnp.dot(mixture, attend_round[3], precision=highest))
    hidden = blend(inputs, branch, attend_scale[1])
    hidden_round = low(hidden)
    upward = low_back(jnp.dot(hidden_round, feed_round[0].T, precision=highest))
    gating = low_back(jnp.dot(hidden_round, feed_round[1].T, precision=highest))
    product = low(swiglu(upward, gating, feed_scale[0], feed_scale[1]))
    downward = low_back(jnp.dot(product, feed_round[2], precision=highest))
    return blend(hidden, downward, attend_scale[2])

def reference(tokens, segment_ids, cotangent, attention_weights, feed_weights, attention_scales, feed_scales, attention_first, attention_second, feed_first, feed_second, attention_scale_first, attention_scale_second, feed_scale_first, feed_scale_second):
    inputs = tokens.astype(jnp.float32)

    def layer(layer_inputs, attend_weights, forward_weights, attend_scales, forward_scales):
        attend_round = low(attend_weights)
        feed_round = low(forward_weights)
        attend_scale = low(attend_scales)
        feed_scale = low(forward_scales)

        def one_row(carry, row_pair):
            return (carry, row_layer(row_pair[0], row_pair[1], attend_round, feed_round, attend_scale, feed_scale))
        _, outputs = lax.scan(jax.checkpoint(one_row), jnp.zeros((), jnp.float32), (layer_inputs, segment_ids))
        return outputs
    output, pullback = jax.vjp(layer, inputs, attention_weights, feed_weights, attention_scales, feed_scales)
    input_grad, attention_grad, feed_grad, attention_scale_grad, feed_scale_grad = pullback(cotangent.astype(jnp.float32))
    attention_change = adam_change(attention_weights, attention_grad, attention_first, attention_second, True)
    feed_change = adam_change(feed_weights, feed_grad, feed_first, feed_second, True)
    attention_scale_change = adam_change(attention_scales, attention_scale_grad, attention_scale_first, attention_scale_second, False)
    feed_scale_change = adam_change(feed_scales, feed_scale_grad, feed_scale_first, feed_scale_second, False)
    return (output, input_grad, attention_grad, feed_grad, attention_scale_grad, feed_scale_grad, attention_change, feed_change, attention_scale_change, feed_scale_change)
```

```python
import functools
import math

import jax
import jax.numpy as jnp
from jax import lax
from jax.experimental import pallas as pl
from jax.experimental.pallas import tpu as pltpu
from jax.sharding import PartitionSpec as P

HEADS = 16
HEAD_DIM = 64
PAIR = 2 * HEAD_DIM
BLOCK = 256

norm_eps = 1e-06
rope_base = 10000.0
learn_rate = 0.003
beta_one = 0.9
beta_two = 0.95
adam_eps = 1e-08
corr_one = 1.0 - 0.9**10
corr_two = 1.0 - 0.95**10
apart = 1024.0

bf16 = jnp.bfloat16
f32 = jnp.float32
NT = (((1,), (1,)), ((), ()))
NN = (((1,), (0,)), ((), ()))
TN = (((0,), (0,)), ((), ()))
MIB = 1024 * 1024


def dot(a, b, dims=NN, precision=None):
    return lax.dot_general(a, b, dims, precision=precision, preferred_element_type=f32)


def swap(x):
    return lax.ppermute(x, "seq", [(0, 1), (1, 0)])


def via(x, bits):
    count = lax.axis_size("dp")
    return lax.ppermute(x, "dp", [(i, i ^ bits) for i in range(count)])


def halves(x, axis):
    return lax.slice_in_dim(x, 0, 2, axis=axis), lax.slice_in_dim(x, 2, 4, axis=axis)


def gather_chunks(block, axis):
    own = jnp.stack([block] + [via(block, 4 * k) for k in (1, 2, 3)], axis)
    by_x = via(own, 1)
    by_y = via(own, 2)
    diagonal = jnp.concatenate([via(halves(by_y, axis)[0], 1), via(halves(by_x, axis)[1], 2)], axis)
    return [own, by_x, by_y, diagonal]


def plus(a, b):
    return (a.astype(f32) + b.astype(f32)).astype(bf16)


def reduce_chunks(chunks, axis):
    own, by_x, by_y, diagonal = chunks
    first, second = halves(diagonal, axis)
    to_y, to_x = via(first, 1), via(second, 2)
    y_first, y_second = halves(by_y, axis)
    x_first, x_second = halves(by_x, axis)
    by_y = jnp.concatenate([plus(y_first, to_y), y_second], axis)
    by_x = jnp.concatenate([x_first, plus(x_second, to_x)], axis)
    total = own.astype(f32) + via(by_x, 1).astype(f32) + via(by_y, 2).astype(f32)
    part = [lax.index_in_dim(total, k, axis, keepdims=False) for k in range(4)]
    result = part[0]
    for k in (1, 2, 3):
        result = result + via(part[k].astype(bf16), 4 * k).astype(f32)
    return result


def slot_of(offset):
    return (offset & 3) * 4 + (offset >> 2)


def offset_of(slot):
    return (slot >> 2) + 4 * (slot & 3)


def lane_index(shape):
    return lax.broadcasted_iota(jnp.int32, shape, len(shape) - 1)


def partner_lanes(x):
    low_part = (lane_index(x.shape) & 32) == 0
    return jnp.where(low_part, pltpu.roll(x, PAIR - 32, 1), pltpu.roll(x, 32, 1))


def head_sums(x):
    first = lane_index(x.shape) < HEAD_DIM
    one = jnp.sum(jnp.where(first, x, 0.0), axis=1, keepdims=True)
    two = jnp.sum(jnp.where(first, 0.0, x), axis=1, keepdims=True)
    return jnp.where(first, one, two)


def turned_unit(raw, cosine, sine):
    turned = raw * cosine + partner_lanes(raw) * sine
    scale = lax.rsqrt(head_sums(turned * turned) + norm_eps)
    return turned * scale, scale


def local_rows(block, half_blocks, rank):
    count = 2 * half_blocks
    return pl.multiple_of(lax.rem(block + half_blocks * rank, count) * BLOCK, BLOCK)


def attend_kernel(
    info, x_ref, w_ref, cos_ref, sin_ref, scale_ref, qa_ref, ka_ref,
    raw_ref, q_ref, k_ref, v_ref, mix_ref, inv_ref,
    q_aug, k_aug, p_scr,
):
    blocks = x_ref.shape[0] // BLOCK
    rank = info[blocks]
    first = lane_index((BLOCK, PAIR)) < HEAD_DIM

    def project(t, carry):
        rows = pl.ds(pl.multiple_of(t * BLOCK, BLOCK), BLOCK)
        raw = dot(x_ref[rows, :], w_ref[0], NT)
        raw_ref[rows, :] = raw[:, : 2 * PAIR]
        v_ref[rows, :] = raw[:, 2 * PAIR :].astype(bf16)
        cosine, sine = cos_ref[rows, :], sin_ref[rows, :]
        scale = scale_ref[0]
        q = (turned_unit(raw[:, :PAIR], cosine, sine)[0] * scale).astype(bf16)
        k = (turned_unit(raw[:, PAIR : 2 * PAIR], cosine, sine)[0] * scale).astype(bf16)
        q_ref[rows, :] = q
        k_ref[rows, :] = k
        q8 = q * jnp.asarray(8.0, bf16)
        qa, ka = qa_ref[rows, :], ka_ref[rows, :]
        q_aug[0, rows, :] = jnp.where(first, q8, qa)
        q_aug[1, rows, :] = jnp.where(first, qa, q8)
        k_aug[0, rows, :] = jnp.where(first, k, ka)
        k_aug[1, rows, :] = jnp.where(first, ka, k)
        return carry

    lax.fori_loop(0, blocks, project, 0)

    row = lax.broadcasted_iota(jnp.int32, (BLOCK, BLOCK), 0)
    col = lax.broadcasted_iota(jnp.int32, (BLOCK, BLOCK), 1)
    causal = col <= row
    ones = jnp.ones((8, PAIR), f32)

    def query_block(g, carry):
        q_rows = pl.ds(local_rows(g, blocks // 2, rank), BLOCK)
        count = g - info[g] + 1

        def variant(nk):
            mixed = []
            k_rows = [pl.ds(local_rows(g - (nk - 1) + j, blocks // 2, rank), BLOCK) for j in range(nk)]
            for h in range(2):
                q = q_aug[h, q_rows, :]
                lacc = None
                for j in range(nk):
                    p = jnp.exp(dot(q, k_aug[h, k_rows[j], :], NT))
                    if j == nk - 1:
                        p = jnp.where(causal, p, 0.0)
                    p_scr[h, j] = p
                    part = p[:, :PAIR] + p[:, PAIR:]
                    lacc = part if lacc is None else lacc + part
                inverse = 1.0 / jnp.sum(lacc, axis=1, keepdims=True)
                sums = dot(ones, lacc, NT, lax.Precision.HIGHEST)
                inv_ref[0, h : h + 1, q_rows] = 1.0 / sums[:1]
                acc = None
                for j in range(nk):
                    part = dot((p_scr[h, j] * inverse).astype(bf16), v_ref[k_rows[j], :])
                    acc = part if acc is None else acc + part
                mixed.append(acc)
            mix_ref[q_rows, :] = jnp.where(first, mixed[0], mixed[1]).astype(bf16)

        for nk in range(1, 5):
            pl.when(count == nk if nk < 4 else count >= 4)(functools.partial(variant, nk))
        return carry

    lax.fori_loop(0, blocks, query_block, 0)


def whole(shape):
    return pl.BlockSpec(shape, lambda p: (0,) * len(shape))


def attend_forward(info, x_all, w_pairs, cosine, sine, scale, qa, ka):
    tokens, width = x_all.shape
    pairs = w_pairs.shape[0]
    feats = pairs * PAIR
    by_pair = pl.BlockSpec((tokens, PAIR), lambda p: (0, p))
    return pl.pallas_call(
        attend_kernel,
        grid=(pairs,),
        in_specs=[
            pl.BlockSpec(memory_space=pltpu.SMEM),
            whole((tokens, width)),
            pl.BlockSpec((1, 3 * PAIR, width), lambda p: (p, 0, 0)),
            whole((tokens, PAIR)),
            whole((tokens, PAIR)),
            pl.BlockSpec((1, 1, PAIR), lambda p: (p, 0, 0)),
            whole((tokens, PAIR)),
            whole((tokens, PAIR)),
        ],
        out_specs=[
            pl.BlockSpec((tokens, 2 * PAIR), lambda p: (0, p)),
            by_pair,
            by_pair,
            by_pair,
            by_pair,
            pl.BlockSpec((1, 8, tokens), lambda p: (p, 0, 0)),
        ],
        out_shape=[
            jax.ShapeDtypeStruct((tokens, 2 * feats), f32),
            jax.ShapeDtypeStruct((tokens, feats), bf16),
            jax.ShapeDtypeStruct((tokens, feats), bf16),
            jax.ShapeDtypeStruct((tokens, feats), bf16),
            jax.ShapeDtypeStruct((tokens, feats), bf16),
            jax.ShapeDtypeStruct((pairs, 8, tokens), f32),
        ],
        scratch_shapes=[
            pltpu.VMEM((2, tokens, PAIR), bf16),
            pltpu.VMEM((2, tokens, PAIR), bf16),
            pltpu.VMEM((2, 4, BLOCK, BLOCK), f32),
        ],
        compiler_params=pltpu.CompilerParams(vmem_limit_bytes=40 * MIB),
        cost_estimate=pl.CostEstimate(flops=12_000_000_000, bytes_accessed=24_000_000, transcendentals=0),
        name="attend_forward",
    )(info, x_all, w_pairs, cosine, sine, scale, qa, ka)


def attend_back_kernel(
    info, q_ref, k_ref, v_ref, do_ref, mix_ref, inv_ref, raw_ref, cos_ref, sin_ref, scale_ref, qa_ref, ka_ref,
    grad_ref, gscale_ref,
    q_aug, k_aug, do_h, q_h, kt_h, delta, dq_acc, dk_acc, dv_acc,
):
    blocks = q_ref.shape[0] // BLOCK
    rank = info[blocks]
    first = lane_index((BLOCK, PAIR)) < HEAD_DIM
    zero = jnp.zeros((BLOCK, PAIR), bf16)
    eight = jnp.asarray(8.0, bf16)
    head_row = lax.broadcasted_iota(jnp.int32, (8, PAIR), 0)
    head_lane = lane_index((8, PAIR)) // HEAD_DIM
    head_mask = jnp.where(head_row == head_lane, 1.0, 0.0).astype(f32)

    def prepare(t, carry):
        start = pl.multiple_of(t * BLOCK, BLOCK)
        rows = pl.ds(start, BLOCK)
        q8 = q_ref[rows, :] * eight
        k = k_ref[rows, :]
        qa, ka = qa_ref[rows, :], ka_ref[rows, :]
        q_aug[0, rows, :] = jnp.where(first, q8, qa)
        q_aug[1, rows, :] = jnp.where(first, qa, q8)
        k_aug[0, rows, :] = jnp.where(first, k, ka)
        k_aug[1, rows, :] = jnp.where(first, ka, k)
        q_h[0, rows, :] = jnp.where(first, q8, zero)
        q_h[1, rows, :] = jnp.where(first, zero, q8)
        k8 = (k * eight).astype(f32)
        kt_h[0, :, rows] = jnp.where(first, k8, 0.0).T.astype(bf16)
        kt_h[1, :, rows] = jnp.where(first, 0.0, k8).T.astype(bf16)
        grad = do_ref[rows, :]
        do_h[0, rows, :] = jnp.where(first, grad, zero)
        do_h[1, rows, :] = jnp.where(first, zero, grad)
        inner = grad.astype(f32) * mix_ref[rows, :].astype(f32)
        delta[:, rows] = dot(head_mask, inner, NT, lax.Precision.HIGHEST)
        dk_acc[rows, :] = jnp.zeros((BLOCK, PAIR), f32)
        dv_acc[rows, :] = jnp.zeros((BLOCK, PAIR), f32)
        return carry

    lax.fori_loop(0, blocks, prepare, 0)

    row = lax.broadcasted_iota(jnp.int32, (BLOCK, BLOCK), 0)
    col = lax.broadcasted_iota(jnp.int32, (BLOCK, BLOCK), 1)
    causal = row <= col

    def query_block(g, carry):
        q_rows = pl.ds(local_rows(g, blocks // 2, rank), BLOCK)
        count = g - info[g] + 1

        def variant(nk):
            dq_t = None
            for j in range(nk):
                k_rows = pl.ds(local_rows(g - (nk - 1) + j, blocks // 2, rank), BLOCK)
                dk = dv = None
                for h in range(2):
                    scores = dot(k_aug[h, k_rows, :], q_aug[h, q_rows, :], NT)
                    p = jnp.exp(scores) * inv_ref[0, h : h + 1, q_rows]
                    if j == nk - 1:
                        p = jnp.where(causal, p, 0.0)
                    dp = dot(v_ref[k_rows, :], do_h[h, q_rows, :], NT)
                    ds = (p * (dp - delta[h : h + 1, q_rows])).astype(bf16)
                    dv_part = dot(p.astype(bf16), do_h[h, q_rows, :])
                    dk_part = dot(ds, q_h[h, q_rows, :])
                    dq_part = dot(kt_h[h, :, k_rows], ds)
                    dv = dv_part if dv is None else dv + dv_part
                    dk = dk_part if dk is None else dk + dk_part
                    dq_t = dq_part if dq_t is None else dq_t + dq_part
                dv_acc[k_rows, :] += dv
                dk_acc[k_rows, :] += dk
            dq_acc[q_rows, :] = dq_t.T

        for nk in range(1, 5):
            pl.when(count == nk if nk < 4 else count >= 4)(functools.partial(variant, nk))
        return carry

    lax.fori_loop(0, blocks, query_block, 0)

    def unturn(t, total):
        rows = pl.ds(pl.multiple_of(t * BLOCK, BLOCK), BLOCK)
        cosine, sine = cos_ref[rows, :], sin_ref[rows, :]
        scale = scale_ref[0]
        for which, acc in ((0, dq_acc), (1, dk_acc)):
            raw = raw_ref[rows, which * PAIR : (which + 1) * PAIR]
            unit, size = turned_unit(raw, cosine, sine)
            grad = acc[rows, :]
            total = total + jnp.sum((grad * unit).reshape(BLOCK // 8, 8, PAIR), axis=0)
            grad_unit = grad * scale
            grad_turned = size * (grad_unit - unit * head_sums(unit * grad_unit))
            grad_raw = grad_turned * cosine - partner_lanes(grad_turned) * sine
            grad_ref[rows, which * PAIR : (which + 1) * PAIR] = grad_raw.astype(bf16)
        grad_ref[rows, 2 * PAIR :] = dv_acc[rows, :].astype(bf16)
        return total

    total = lax.fori_loop(0, blocks, unturn, jnp.zeros((8, PAIR), f32))
    gscale_ref[0] = total


def attend_backward(info, q, k, v, grad_mixture, mixture, inverse, raw, cosine, sine, scale, qa, ka):
    tokens, feats = q.shape
    pairs = feats // PAIR
    by_pair = pl.BlockSpec((tokens, PAIR), lambda p: (0, p))
    half = pltpu.VMEM((2, tokens, PAIR), bf16)
    acc = pltpu.VMEM((tokens, PAIR), f32)
    return pl.pallas_call(
        attend_back_kernel,
        grid=(pairs,),
        in_specs=[
            pl.BlockSpec(memory_space=pltpu.SMEM),
            by_pair,
            by_pair,
            by_pair,
            by_pair,
            by_pair,
            pl.BlockSpec((1, 8, tokens), lambda p: (p, 0, 0)),
            pl.BlockSpec((tokens, 2 * PAIR), lambda p: (0, p)),
            whole((tokens, PAIR)),
            whole((tokens, PAIR)),
            pl.BlockSpec((1, 1, PAIR), lambda p: (p, 0, 0)),
            whole((tokens, PAIR)),
            whole((tokens, PAIR)),
        ],
        out_specs=[
            pl.BlockSpec((tokens, 3 * PAIR), lambda p: (0, p)),
            pl.BlockSpec((1, 8, PAIR), lambda p: (p, 0, 0)),
        ],
        out_shape=[
            jax.ShapeDtypeStruct((tokens, 3 * feats), bf16),
            jax.ShapeDtypeStruct((pairs, 8, PAIR), f32),
        ],
        scratch_shapes=[
            half,
            half,
            half,
            half,
            pltpu.VMEM((2, PAIR, tokens), bf16),
            pltpu.VMEM((8, tokens), f32),
            acc,
            acc,
            acc,
        ],
        compiler_params=pltpu.CompilerParams(vmem_limit_bytes=40 * MIB),
        cost_estimate=pl.CostEstimate(flops=24_000_000_000, bytes_accessed=24_000_000, transcendentals=0),
        name="attend_backward",
    )(info, q, k, v, grad_mixture, mixture, inverse, raw, cosine, sine, scale, qa, ka)


def up_gate_kernel(h_ref, w_ref, scale_ref, ug_ref, product_ref):
    units = product_ref.shape[1]
    both = dot(h_ref[...], w_ref[...], NT)
    ug_ref[...] = both.astype(bf16)
    upward = both[:, :units] * scale_ref[:, :units]
    gated = both[:, units:] * scale_ref[:, units:]
    product_ref[...] = (upward * gated / (1.0 + jnp.exp(-gated))).astype(bf16)


def tile_of(tokens):
    return 512 if tokens % 512 == 0 else 256


def up_gate(hidden, w, scale):
    tokens, width = hidden.shape
    units = w.shape[0] // 2
    tile = tile_of(tokens)
    return pl.pallas_call(
        up_gate_kernel,
        grid=(tokens // tile,),
        in_specs=[
            pl.BlockSpec((tile, width), lambda t: (t, 0)),
            whole((2 * units, width)),
            whole((1, 2 * units)),
        ],
        out_specs=[
            pl.BlockSpec((tile, 2 * units), lambda t: (t, 0)),
            pl.BlockSpec((tile, units), lambda t: (t, 0)),
        ],
        out_shape=[
            jax.ShapeDtypeStruct((tokens, 2 * units), bf16),
            jax.ShapeDtypeStruct((tokens, units), bf16),
        ],
        compiler_params=pltpu.CompilerParams(vmem_limit_bytes=32 * MIB),
        cost_estimate=pl.CostEstimate(
            flops=4 * tokens * width * units, bytes_accessed=14_000_000, transcendentals=tokens * units
        ),
        name="up_gate",
    )(hidden, w, scale)


def gate_back_kernel(grad_ref, w_ref, ug_ref, scale_ref, gug_ref, gscale_ref):
    units = w_ref.shape[0]
    grad = dot(grad_ref[...], w_ref[...], NT)
    up = ug_ref[:, :units].astype(f32)
    gate = ug_ref[:, units:].astype(f32)
    up_scale, gate_scale = scale_ref[:, :units], scale_ref[:, units:]
    gated = gate * gate_scale
    sig = 1.0 / (1.0 + jnp.exp(-gated))
    silu = gated * sig
    through = grad * silu
    grad_gated = grad * (up * up_scale) * (sig + silu * (1.0 - sig))
    gug_ref[:, :units] = (through * up_scale).astype(bf16)
    gug_ref[:, units:] = (grad_gated * gate_scale).astype(bf16)

    @pl.when(pl.program_id(0) == 0)
    def _():
        gscale_ref[...] = jnp.zeros_like(gscale_ref)

    rows = grad.shape[0] // 8
    gscale_ref[:, :units] += jnp.sum((through * up).reshape(rows, 8, units), axis=0)
    gscale_ref[:, units:] += jnp.sum((grad_gated * gate).reshape(rows, 8, units), axis=0)


def gate_back(grad, w, ug, scale):
    tokens, width = grad.shape
    units = w.shape[0]
    tile = tile_of(tokens)
    return pl.pallas_call(
        gate_back_kernel,
        grid=(tokens // tile,),
        in_specs=[
            pl.BlockSpec((tile, width), lambda t: (t, 0)),
            whole((units, width)),
            pl.BlockSpec((tile, 2 * units), lambda t: (t, 0)),
            whole((1, 2 * units)),
        ],
        out_specs=[
            pl.BlockSpec((tile, 2 * units), lambda t: (t, 0)),
            whole((8, 2 * units)),
        ],
        out_shape=[
            jax.ShapeDtypeStruct((tokens, 2 * units), bf16),
            jax.ShapeDtypeStruct((8, 2 * units), f32),
        ],
        compiler_params=pltpu.CompilerParams(vmem_limit_bytes=32 * MIB),
        cost_estimate=pl.CostEstimate(
            flops=2 * tokens * width * units, bytes_accessed=14_000_000, transcendentals=tokens * units
        ),
        name="gate_back",
    )(grad, w, ug, scale)


def sum_dots_kernel(count, *refs):
    total = dot(refs[0][...], refs[count][...])
    for c in range(1, count):
        total = total + dot(refs[c][...], refs[count + c][...])
    refs[-1][...] = total.astype(refs[-1].dtype)


def sum_dots(lefts, rights, start, rows, dtype):
    tile = 256
    depth, width = rights[0].shape
    count = len(lefts)
    return pl.pallas_call(
        functools.partial(sum_dots_kernel, count),
        grid=(rows // tile,),
        in_specs=[pl.BlockSpec((tile, depth), lambda t: (t + start // tile, 0))] * count
        + [whole((depth, width))] * count,
        out_specs=pl.BlockSpec((tile, width), lambda t: (t, 0)),
        out_shape=jax.ShapeDtypeStruct((rows, width), dtype),
        compiler_params=pltpu.CompilerParams(vmem_limit_bytes=40 * MIB),
        cost_estimate=pl.CostEstimate(
            flops=2 * rows * width * depth * count, bytes_accessed=10_000_000, transcendentals=0
        ),
        name="sum_dots",
    )(*lefts, *rights)


def rms_unit(values):
    return values * lax.rsqrt(jnp.mean(values * values, axis=-1, keepdims=True) + norm_eps)


def blend(residual, branch, mixing):
    return rms_unit(residual + mixing * (rms_unit(branch) - residual))


def adam_change(weight, gradient, moment_one, moment_two, renormalize):
    moment_one_new = beta_one * moment_one + (1.0 - beta_one) * gradient
    moment_two_new = beta_two * moment_two + (1.0 - beta_two) * gradient * gradient
    stepped = weight - learn_rate * (moment_one_new / corr_one) / (
        jnp.sqrt(moment_two_new / corr_two) + adam_eps
    )
    if renormalize:
        stepped = stepped * lax.rsqrt(jnp.sum(stepped * stepped, axis=-1, keepdims=True) + norm_eps)
    return stepped - weight


def own_half(x, rank, axis):
    size = x.shape[axis] // 2
    return lax.dynamic_slice_in_dim(x, rank * size, size, axis)


def gather_sixteen(rank, attention_weights, feed_weights, attention_scales, feed_scales):
    place = lax.axis_index("dp")
    width = attention_weights.shape[-1]
    part = own_half(attention_weights, rank, 1).astype(bf16)
    rows = part.shape[1]
    part = part.reshape(4 * rows, width)
    extra = jnp.concatenate(
        [attention_scales.reshape(-1), own_half(feed_scales, rank, 1).reshape(-1)]
    ).astype(bf16)
    used = extra.shape[0]
    extra = jnp.pad(extra[None], ((0, 7), (0, width - used)))
    chunks = gather_chunks(jnp.concatenate([part, extra], axis=0), 0)
    feed_part = own_half(feed_weights, rank, 1).astype(bf16)
    ug_chunks = gather_chunks(feed_part[:2], 1)
    d_chunks = gather_chunks(feed_part[2], 0)

    lower, upper = [], []
    for chunk in chunks:
        mine = chunk[:, : 4 * rows]
        other = swap(mine)
        lower.append(jnp.where(rank == 0, mine, other))
        upper.append(jnp.where(rank == 0, other, mine))
    shape = (HEADS, 4, rows, width)
    full = jnp.stack(
        [jnp.concatenate(lower, 0).reshape(shape), jnp.concatenate(upper, 0).reshape(shape)], 2
    )
    half = HEADS // 2
    mine = lax.dynamic_slice_in_dim(full, rank * half, half, 0)
    other = lax.dynamic_slice_in_dim(full, (1 - rank) * half, half, 0)
    w_pairs = jnp.swapaxes(mine[:, :3].reshape(half // 2, 2, 3, HEAD_DIM, width), 1, 2)
    w_pairs = w_pairs.reshape(half // 2, 3 * PAIR, width)
    wo_mine = mine[:, 3].reshape(half * HEAD_DIM, width)
    wo_other = other[:, 3].reshape(half * HEAD_DIM, width)

    extras = jnp.concatenate([chunk[:, 4 * rows] for chunk in chunks], 0)[:, :used].astype(f32)
    qk_scale = lax.dynamic_slice_in_dim(extras[:, :HEAD_DIM], rank * half, half, 0)
    alpha = jnp.take(
        extras[:, HEAD_DIM : 3 * HEAD_DIM], slot_of(jnp.arange(HEADS, dtype=jnp.int32) ^ place), axis=0
    )
    alpha = jnp.swapaxes(alpha.reshape(HEADS, 2, HEAD_DIM), 0, 1).reshape(2, width)
    feed_scale = extras[:, 3 * HEAD_DIM :].reshape(4, 4, 2, -1)
    feed = [
        (
            ug_chunks[c].reshape(-1, width),
            d_chunks[c].reshape(-1, width),
            jnp.swapaxes(feed_scale[c], 0, 1).reshape(1, -1),
        )
        for c in range(4)
    ]
    return w_pairs, wo_mine, wo_other, qk_scale.reshape(half // 2, 1, PAIR), alpha, feed


def reduce_feed_sixteen(rank, grad_ug, grad_d):
    rows = grad_d[0].shape[0] // 4
    width = grad_d[0].shape[1]
    down = reduce_chunks([g.reshape(4, rows, width) for g in grad_d], 0)
    both = reduce_chunks([g.reshape(2, 4, rows, width) for g in grad_ug], 1)
    total = jnp.concatenate([both, down[None]], 0)
    other = swap(total)
    return jnp.concatenate(
        [jnp.where(rank == 0, total, other), jnp.where(rank == 0, other, total)], 1
    )


def reduce_attend_sixteen(rank, grad_pairs, grad_wo, grad_qk, grad_alpha, grad_feed_scale):
    place = lax.axis_index("dp")
    width = grad_wo.shape[-1]
    half = HEADS // 2
    rows = HEAD_DIM // 2
    qkv = grad_pairs.reshape(half // 2, 3, 2, 2, rows, width)
    qkv = jnp.transpose(qkv, (3, 0, 2, 1, 4, 5)).reshape(2, half, 3 * rows, width)
    wo = jnp.swapaxes(grad_wo.reshape(half, 2, rows, width), 0, 1)
    both = jnp.concatenate([qkv, wo], 2)
    keep = lax.dynamic_index_in_dim(both, rank, 0, keepdims=False)
    other = swap(lax.dynamic_index_in_dim(both, 1 - rank, 0, keepdims=False))
    near = jnp.where(rank == 0, keep, other)
    far = jnp.where(rank == 0, other, keep)

    qk = jnp.zeros((HEADS, HEAD_DIM), f32)
    qk = lax.dynamic_update_slice(qk, grad_qk.reshape(half, HEAD_DIM), (rank * half, 0))
    alpha = jnp.swapaxes(grad_alpha.reshape(2, HEADS, HEAD_DIM), 0, 1).reshape(HEADS, 2 * HEAD_DIM)
    alpha = jnp.take(alpha, place ^ offset_of(jnp.arange(HEADS, dtype=jnp.int32)), axis=0)
    feed = jnp.concatenate(
        [jnp.swapaxes(g.reshape(2, 4, -1), 0, 1).reshape(4, -1) for g in grad_feed_scale], 0
    )
    extra = jnp.concatenate([qk, alpha, feed], 1).astype(bf16)
    used = extra.shape[1]
    extra = jnp.pad(extra[:, None], ((0, 0), (0, 7), (0, width - used)))
    chunks = [
        jnp.concatenate([side[at : at + 4], extra[slot : slot + 4]], 1)
        for side, at, slot in ((near, 0, 0), (near, 4, 4), (far, 0, 8), (far, 4, 12))
    ]
    total = reduce_chunks(chunks, 0)
    other = swap(total)
    low = jnp.where(rank == 0, total, other)
    high = jnp.where(rank == 0, other, total)
    grad_w = jnp.concatenate(
        [low[: 4 * rows].reshape(4, rows, width), high[: 4 * rows].reshape(4, rows, width)], 1
    )
    at = 3 * HEAD_DIM
    grad_s = (low[4 * rows, :at] + high[4 * rows, :at]).reshape(3, HEAD_DIM)
    grad_fs = jnp.concatenate(
        [low[4 * rows, at:used].reshape(2, -1), high[4 * rows, at:used].reshape(2, -1)], 1
    )
    return grad_w, grad_s, grad_fs


def gather_any(rank, attention_weights, feed_weights, attention_scales, feed_scales):
    width = attention_weights.shape[-1]
    full = lax.all_gather(attention_weights.astype(bf16), "dp", axis=1, tiled=True)
    scales = lax.all_gather(attention_scales.astype(bf16), "dp", axis=1, tiled=True).astype(f32)
    half = full.shape[1] // 2
    mine = lax.dynamic_slice_in_dim(full, rank * half, half, 1)
    pairs = half // PAIR
    w_pairs = jnp.swapaxes(mine[:3].reshape(3, pairs, PAIR, width), 0, 1).reshape(pairs, 3 * PAIR, width)
    wo_other = lax.dynamic_slice_in_dim(full[3], (1 - rank) * half, half, 0)
    qk_scale = lax.dynamic_slice_in_dim(scales[0], rank * half, half, 0)
    feed = lax.all_gather(own_half(feed_weights, rank, 1).astype(bf16), "dp", axis=1, tiled=True)
    feed_s = lax.all_gather(own_half(feed_scales, rank, 1).astype(bf16), "dp", axis=1, tiled=True)
    units = feed.shape[1] // 4
    chunks = []
    for c in range(4):
        part = feed[:, c * units : (c + 1) * units]
        scale = feed_s[:, c * units : (c + 1) * units].astype(f32)
        chunks.append((part[:2].reshape(-1, width), part[2], scale.reshape(1, -1)))
    return w_pairs, mine[3], wo_other, qk_scale.reshape(pairs, 1, PAIR), scales[1:], chunks


def reduce_feed_any(rank, grad_ug, grad_d):
    units, width = grad_d[0].shape
    parts = [
        jnp.concatenate([u.reshape(2, units, width), d[None]], 0) for u, d in zip(grad_ug, grad_d)
    ]
    total = jnp.concatenate(parts, 1)
    total = lax.psum_scatter(total, "dp", scatter_dimension=1, tiled=True).astype(f32)
    other = swap(total)
    return jnp.concatenate(
        [jnp.where(rank == 0, total, other), jnp.where(rank == 0, other, total)], 1
    )


def reduce_attend_any(rank, grad_pairs, grad_wo, grad_qk, grad_alpha, grad_feed_scale):
    pairs, width = grad_pairs.shape[0] // (3 * PAIR), grad_wo.shape[-1]
    half = pairs * PAIR
    qkv = jnp.swapaxes(grad_pairs.reshape(pairs, 3, PAIR, width), 0, 1).reshape(3, half, width)
    both = jnp.concatenate([qkv, grad_wo[None]], 0)
    full = lax.dynamic_update_slice(jnp.zeros((4, 2 * half, width), bf16), both, (0, rank * half, 0))
    total = lax.psum_scatter(full, "dp", scatter_dimension=1, tiled=True).astype(f32)
    grad_w = total + swap(total)
    qk = lax.dynamic_update_slice(jnp.zeros((1, 2 * half), f32), grad_qk.reshape(1, half), (0, rank * half))
    scales = jnp.concatenate([qk, grad_alpha], 0)
    grad_s = lax.psum_scatter(scales, "dp", scatter_dimension=1, tiled=True)
    grad_s = grad_s + swap(grad_s)
    feed = jnp.concatenate([g.reshape(2, -1) for g in grad_feed_scale], 1)
    feed = lax.psum_scatter(feed, "dp", scatter_dimension=1, tiled=True)
    other = swap(feed)
    grad_fs = jnp.concatenate(
        [jnp.where(rank == 0, feed, other), jnp.where(rank == 0, other, feed)], 1
    )
    return grad_w, grad_s, grad_fs


def local(
    tokens,
    segment_ids,
    cotangent,
    attention_weights,
    feed_weights,
    attention_scales,
    feed_scales,
    attention_first,
    attention_second,
    feed_first,
    feed_second,
    attention_scale_first,
    attention_scale_second,
    feed_scale_first,
    feed_scale_second,
):
    sixteen = lax.axis_size("dp") == HEADS
    count, width = tokens.shape[0] * tokens.shape[1], tokens.shape[-1]
    rank = lax.axis_index("seq")
    x = tokens.reshape(count, width)
    x_all = jnp.concatenate([x, swap(x)], axis=0)

    w_pairs, wo_mine, wo_other, qk_scale, alpha, feed = (gather_sixteen if sixteen else gather_any)(
        rank, attention_weights, feed_weights, attention_scales, feed_scales
    )

    segments = segment_ids.reshape(-1)
    docs = jnp.arange(8, dtype=jnp.int32)
    begins = jnp.sum((segments[None, :] < docs[:, None]).astype(jnp.int32), axis=1)
    is_doc = segments[:, None] == docs[None, :]
    starts = jnp.sum(jnp.where(is_doc, begins[None, :], 0), axis=1)
    info = jnp.concatenate([starts[::BLOCK] // BLOCK, rank[None].astype(jnp.int32)])
    place = jnp.arange(2 * count, dtype=jnp.int32)

    def arranged(values):
        own = lax.dynamic_slice_in_dim(values, rank * count, count, 0)
        other = lax.dynamic_slice_in_dim(values, (1 - rank) * count, count, 0)
        return jnp.concatenate([own, other], 0)

    positions = arranged(place - starts).astype(f32)
    frequency = jnp.exp(
        jnp.arange(HEAD_DIM // 2, dtype=f32) * (-2.0 * math.log(rope_base) / HEAD_DIM)
    )
    angles = positions[:, None] * jnp.tile(frequency, 4)[None, :]
    cosine = jnp.cos(angles)
    sign = jnp.where((jnp.arange(PAIR) & 32) == 0, -1.0, 1.0).astype(f32)
    sine = jnp.sin(angles) * sign[None, :]
    lanes = jnp.arange(PAIR, dtype=jnp.int32) & (HEAD_DIM - 1)
    own_doc = arranged(segments)[:, None] == lanes[None, :]
    query_mark = own_doc.astype(bf16)
    key_mark = jnp.where(own_doc | (lanes >= 8)[None, :], 0.0, -apart).astype(bf16)

    raw, query, key, value, mixture, inverse = attend_forward(
        info, x_all, w_pairs, cosine, sine, qk_scale, query_mark, key_mark
    )
    mixed_other = swap(mixture[count:])
    branch = dot(mixture[:count], wo_mine) + dot(mixed_other, wo_other)
    hidden, hidden_back = jax.vjp(blend, x.astype(f32), branch, alpha[0])
    hidden_round = hidden.astype(bf16)
    hidden_all = jnp.concatenate([hidden_round, swap(hidden_round)], 0)

    ugs, products = [], []
    for w_ug, _, scale in feed:
        ug, product = up_gate(hidden_all, w_ug, scale)
        ugs.append(ug)
        products.append(product)
    w_ds = [w for _, w, _ in feed]
    down_other = sum_dots(products, w_ds, count, count, bf16)
    down_own = sum_dots(products, w_ds, 0, count, f32)
    downward = down_own + swap(down_other).astype(f32)
    output, output_back = jax.vjp(blend, hidden, downward, alpha[1])

    grad_out = cotangent.reshape(count, width).astype(f32)
    grad_hidden_res, grad_downward, grad_alpha_feed = output_back(grad_out)
    grad_down_round = grad_downward.astype(bf16)
    grad_down = jnp.concatenate([grad_down_round, swap(grad_down_round)], 0)
    grad_d = [dot(product, grad_down, TN).astype(bf16) for product in products]
    gugs, grad_feed_scale = [], []
    for (w_ug, w_d, scale), ug in zip(feed, ugs):
        gug, gscale = gate_back(grad_down, w_d, ug, scale)
        gugs.append(gug)
        grad_feed_scale.append(jnp.sum(gscale, axis=0))
    grad_ug = [dot(gug, hidden_all, TN).astype(bf16) for gug in gugs]
    w_ugs = [w for w, _, _ in feed]
    back_other = sum_dots(gugs, w_ugs, count, count, bf16)
    back_own = sum_dots(gugs, w_ugs, 0, count, f32)
    grad_hidden = grad_hidden_res + back_own + swap(back_other).astype(f32)
    feed_grad = (reduce_feed_sixteen if sixteen else reduce_feed_any)(rank, grad_ug, grad_d)

    grad_input_res, grad_branch, grad_alpha_attend = hidden_back(grad_hidden)
    grad_branch_round = grad_branch.astype(bf16)
    grad_branch_all = jnp.concatenate([grad_branch_round, swap(grad_branch_round)], 0)
    grad_mixture = dot(grad_branch_all, wo_mine, NT).astype(bf16)
    grad_wo = dot(mixture, grad_branch_all, TN).astype(bf16)
    grad_qkv, grad_qk = attend_backward(
        info, query, key, value, grad_mixture, mixture, inverse, raw, cosine, sine, qk_scale, query_mark, key_mark
    )
    grad_pairs = dot(grad_qkv, x_all, TN).astype(bf16)
    w_flat = w_pairs.reshape(-1, width)
    input_other = dot(grad_qkv[count:], w_flat).astype(bf16)
    input_own = dot(grad_qkv[:count], w_flat)
    input_grad = grad_input_res + input_own + swap(input_other).astype(f32)

    attend_grad, attend_grad_s, feed_grad_s = (reduce_attend_sixteen if sixteen else reduce_attend_any)(
        rank,
        grad_pairs,
        grad_wo,
        jnp.sum(grad_qk, axis=1),
        jnp.stack([grad_alpha_attend, grad_alpha_feed]),
        grad_feed_scale,
    )
    attention_change = adam_change(
        attention_weights, attend_grad, attention_first, attention_second, True
    )
    feed_change = adam_change(feed_weights, feed_grad, feed_first, feed_second, True)
    attention_scale_change = adam_change(
        attention_scales, attend_grad_s, attention_scale_first, attention_scale_second, False
    )
    feed_scale_change = adam_change(
        feed_scales, feed_grad_s, feed_scale_first, feed_scale_second, False
    )
    return (
        output.reshape(tokens.shape),
        input_grad.reshape(tokens.shape),
        attend_grad,
        feed_grad,
        attend_grad_s,
        feed_grad_s,
        attention_change,
        feed_change,
        attention_scale_change,
        feed_scale_change,
    )


def solution(mesh):
    rows = P("dp", "seq", None)
    matrix = P(None, "dp", None)
    scale = P(None, "dp")
    return jax.shard_map(
        local,
        mesh=mesh,
        in_specs=(rows, P("dp", None), rows, matrix, matrix, scale, scale)
        + (matrix,) * 4
        + (scale,) * 4,
        out_specs=(rows, rows, matrix, matrix, scale, scale, matrix, matrix, scale, scale),
        check_vma=False,
    )
```

```python
import functools
import math

import jax
import jax.numpy as jnp
from jax import lax
from jax.experimental import pallas as pl
from jax.experimental.pallas import tpu as pltpu
from jax.sharding import PartitionSpec as P

HEADS = 16
HEAD_DIM = 64
PAIR = 2 * HEAD_DIM
BLOCK = 256

norm_eps = 1e-06
rope_base = 10000.0
learn_rate = 0.003
beta_one = 0.9
beta_two = 0.95
adam_eps = 1e-08
corr_one = 1.0 - 0.9**10
corr_two = 1.0 - 0.95**10
apart = 1024.0

bf16 = jnp.bfloat16
f32 = jnp.float32
NT = (((1,), (1,)), ((), ()))
NN = (((1,), (0,)), ((), ()))
TN = (((0,), (0,)), ((), ()))
MIB = 1024 * 1024
SMALL = pl.CostEstimate(flops=1, bytes_accessed=1, transcendentals=0)
ROOM = pltpu.CompilerParams(vmem_limit_bytes=40 * MIB)


def made(shape, dtype):
    return pltpu.HBM(shape, dtype)


def dot(a, b, dims=NN, precision=None):
    return lax.dot_general(a, b, dims, precision=precision, preferred_element_type=f32)


def tie(*values):
    return lax.optimization_barrier(values)


def swap(x):
    return lax.ppermute(x, "seq", [(0, 1), (1, 0)])


def via(x, bits):
    count = lax.axis_size("dp")
    return lax.ppermute(x, "dp", [(i, i ^ bits) for i in range(count)])


def by_z(block):
    return [via(block, 4 * k) for k in (1, 2, 3)]


def join_kernel(steps, *refs):
    for k in range(len(refs) - 1):

        @pl.when(pl.program_id(0) // steps == k)
        def _():
            refs[-1][...] = refs[k][...]


def join(*parts):
    rows, width = parts[0].shape
    steps = max(1, rows // 256)
    tile = rows // steps

    def spec(k):
        return pl.BlockSpec((tile, width), lambda t: (jnp.clip(t - k * steps, 0, steps - 1), 0))

    return pl.pallas_call(
        functools.partial(join_kernel, steps),
        grid=(len(parts) * steps,),
        in_specs=[spec(k) for k in range(len(parts))],
        out_specs=pl.BlockSpec((tile, width), lambda t: (t, 0)),
        out_shape=made((len(parts) * rows, width), parts[0].dtype),
        compiler_params=ROOM,
        cost_estimate=SMALL,
        name="join",
    )(*parts)


def fill_kernel(whole_ref, part_ref, out_ref):
    out_ref[...] = part_ref[...]


def fill(target, part):
    rows, width = part.shape
    tile = rows // 2
    return pl.pallas_call(
        fill_kernel,
        grid=(2,),
        in_specs=[pl.BlockSpec(memory_space=pl.ANY), pl.BlockSpec((tile, width), lambda t: (t, 0))],
        out_specs=pl.BlockSpec((tile, width), lambda t: (t + 2, 0)),
        out_shape=made(target.shape, target.dtype),
        input_output_aliases={0: 0},
        compiler_params=ROOM,
        cost_estimate=SMALL,
        name="fill",
    )(target, part)


def add_half_kernel(a_ref, b_ref, o_ref):
    o_ref[...] = (a_ref[...].astype(f32) + b_ref[...].astype(f32)).astype(bf16)


def add_half(x, part, lower):
    rows, width = part.shape
    tile = rows // 2
    at = 2 if lower else 0
    return pl.pallas_call(
        add_half_kernel,
        grid=(2,),
        in_specs=[
            pl.BlockSpec((tile, width), lambda t: (t + at, 0)),
            pl.BlockSpec((tile, width), lambda t: (t, 0)),
        ],
        out_specs=pl.BlockSpec((tile, width), lambda t: (t + at, 0)),
        out_shape=made(x.shape, x.dtype),
        input_output_aliases={0: 0},
        compiler_params=ROOM,
        cost_estimate=SMALL,
        name="add_half",
    )(x, part)


def upper_half(x):
    return x[: x.shape[0] // 2]


def lower_half(x):
    return x[x.shape[0] // 2 :]


def diagonal_in(by_x, by_y):
    return [via(upper_half(by_y), 1), via(lower_half(by_x), 2)]


def diagonal_out(diagonal):
    return [via(upper_half(diagonal), 1), via(lower_half(diagonal), 2)]


def with_diagonal(by_x, by_y, parts):
    to_y, to_x = parts
    return add_half(by_x, to_x, True), add_half(by_y, to_y, False)


def column_kernel(own_ref, x_ref, y_ref, *outs):
    total = own_ref[...].astype(f32) + x_ref[...].astype(f32) + y_ref[...].astype(f32)
    for k in range(4):

        @pl.when(pl.program_id(0) == k)
        def _():
            outs[k][...] = total.astype(outs[k].dtype)


def column_sum(own, from_x, from_y):
    rows, width = own.shape[0] // 4, own.shape[1]
    block = pl.BlockSpec((rows, width), lambda t: (t, 0))
    mine, *parts = pl.pallas_call(
        column_kernel,
        grid=(4,),
        in_specs=[block] * 3,
        out_specs=[whole((rows, width))] * 4,
        out_shape=[made((rows, width), f32)] + [made((rows, width), bf16)] * 3,
        compiler_params=ROOM,
        cost_estimate=SMALL,
        name="column_sum",
    )(own, from_x, from_y)
    return mine, parts


def z_out(parts):
    return [via(part, 4 * k) for part, k in zip(parts, (1, 2, 3))]


def z_sum(mine, parts):
    for part in parts:
        mine = mine + part.astype(f32)
    return mine


def slot_of(offset):
    return (offset & 3) * 4 + (offset >> 2)


def offset_of(slot):
    return (slot >> 2) + 4 * (slot & 3)


def of_first(shape, dim):
    return (lax.broadcasted_iota(jnp.int32, shape, dim) & 32) == 0


def head_sums(x, same):
    high = x.astype(bf16)
    low = (x - high.astype(f32)).astype(bf16)
    return dot(high, same) + dot(low, same)


def same_head():
    same = of_first((PAIR, PAIR), 0) == of_first((PAIR, PAIR), 1)
    return jnp.where(same, 1.0, 0.0).astype(bf16)


def turned_unit(raw, cosine, sine, same):
    turned = raw * cosine + pltpu.roll(raw, HEAD_DIM, 1) * sine
    scale = lax.rsqrt(head_sums(turned * turned, same) + norm_eps)
    return turned * scale, scale


def local_rows(block, half_blocks, rank):
    count = 2 * half_blocks
    return pl.multiple_of(lax.rem(block + half_blocks * rank, count) * BLOCK, BLOCK)


def attend_kernel(
    info, x_ref, mine_ref, other_ref, cos_ref, sin_ref, scale_ref, qa_ref, ka_ref,
    w_ref, wo_ref, raw_ref, q_ref, k_ref, v_ref, mix_ref, inv_ref,
    q_aug, k_aug,
):
    blocks = x_ref.shape[0] // BLOCK
    rank = info[blocks]
    part = HEAD_DIM // 2

    def assemble(first_ref, second_ref):
        for head in range(2):
            for m in range(4):
                source = slice(head * 4 * part + m * part, head * 4 * part + (m + 1) * part)
                for t, ref in enumerate((first_ref, second_ref)):
                    at = t * HEAD_DIM + head * part
                    if m < 3:
                        w_ref[0, m * PAIR + at : m * PAIR + at + part, :] = ref[source, :]
                    else:
                        wo_ref[at : at + part, :] = ref[source, :]

    pl.when(rank == 0)(functools.partial(assemble, mine_ref, other_ref))
    pl.when(rank != 0)(functools.partial(assemble, other_ref, mine_ref))
    first = of_first((BLOCK, PAIR), 1)
    tall = 2 * BLOCK if blocks % 2 == 0 else BLOCK
    first_tall = of_first((tall, PAIR), 1)
    same = same_head()

    def project(t, carry):
        rows = pl.ds(pl.multiple_of(t * tall, tall), tall)
        raw = dot(x_ref[rows, :], w_ref[0], NT)
        raw_ref[rows, :] = raw[:, : 2 * PAIR]
        v_ref[rows, :] = raw[:, 2 * PAIR :].astype(bf16)
        cosine, sine = cos_ref[rows, :], sin_ref[rows, :]
        scale = scale_ref[0]
        q = (turned_unit(raw[:, :PAIR], cosine, sine, same)[0] * scale).astype(bf16)
        k = (turned_unit(raw[:, PAIR : 2 * PAIR], cosine, sine, same)[0] * scale).astype(bf16)
        q_ref[rows, :] = q
        k_ref[rows, :] = k
        q8 = q * jnp.asarray(8.0, bf16)
        qa, ka = qa_ref[rows, :], ka_ref[rows, :]
        q_aug[0, rows, :] = jnp.where(first_tall, q8, qa)
        q_aug[1, rows, :] = jnp.where(first_tall, qa, q8)
        k_aug[0, rows, :] = jnp.where(first_tall, k, ka)
        k_aug[1, rows, :] = jnp.where(first_tall, ka, k)
        return carry

    lax.fori_loop(0, blocks * BLOCK // tall, project, 0)

    row = lax.broadcasted_iota(jnp.int32, (BLOCK, BLOCK), 0)
    col = lax.broadcasted_iota(jnp.int32, (BLOCK, BLOCK), 1)
    causal = col <= row

    def query_block(g, carry):
        q_rows = pl.ds(local_rows(g, blocks // 2, rank), BLOCK)
        count = g - info[g] + 1

        def variant(nk):
            mixed = []
            k_rows = [pl.ds(local_rows(g - (nk - 1) + j, blocks // 2, rank), BLOCK) for j in range(nk)]
            for h in range(2):
                q = q_aug[h, q_rows, :]
                lacc = acc = None
                for j in range(nk):
                    p = jnp.exp(dot(q, k_aug[h, k_rows[j], :], NT))
                    if j == nk - 1:
                        p = jnp.where(causal, p, 0.0)
                    part = p[:, :PAIR] + p[:, PAIR:]
                    lacc = part if lacc is None else lacc + part
                    part = dot(p.astype(bf16), v_ref[k_rows[j], :])
                    acc = part if acc is None else acc + part
                inverse = 1.0 / jnp.sum(lacc, axis=1, keepdims=True)
                inv_ref[0, h : h + 1, q_rows] = 1.0 / jnp.sum(lacc.T, axis=0, keepdims=True)
                mixed.append(acc * inverse)
            mix_ref[q_rows, :] = jnp.where(first, mixed[0], mixed[1]).astype(bf16)

        for nk in range(1, 5):
            pl.when(count == nk if nk < 4 else count >= 4)(functools.partial(variant, nk))
        return carry

    lax.fori_loop(0, blocks, query_block, 0)


def whole(shape):
    return pl.BlockSpec(shape, lambda p: (0,) * len(shape))


def attend_forward(info, x_all, mine, other, cosine, sine, scale, qa, ka):
    tokens, width = x_all.shape
    pairs = mine.shape[0] // (4 * HEAD_DIM)
    feats = pairs * PAIR
    by_pair = pl.BlockSpec((tokens, PAIR), lambda p: (0, p))
    return pl.pallas_call(
        attend_kernel,
        grid=(pairs,),
        in_specs=[
            pl.BlockSpec(memory_space=pltpu.SMEM),
            whole((tokens, width)),
            pl.BlockSpec((4 * HEAD_DIM, width), lambda p: (p, 0)),
            pl.BlockSpec((4 * HEAD_DIM, width), lambda p: (p, 0)),
            whole((tokens, PAIR)),
            whole((tokens, PAIR)),
            pl.BlockSpec((1, 1, PAIR), lambda p: (p, 0, 0)),
            whole((tokens, PAIR)),
            whole((tokens, PAIR)),
        ],
        out_specs=[
            pl.BlockSpec((1, 3 * PAIR, width), lambda p: (p, 0, 0)),
            pl.BlockSpec((PAIR, width), lambda p: (p, 0)),
            pl.BlockSpec((tokens, 2 * PAIR), lambda p: (0, p)),
            by_pair,
            by_pair,
            by_pair,
            by_pair,
            pl.BlockSpec((1, 8, tokens), lambda p: (p, 0, 0)),
        ],
        out_shape=[
            made((pairs, 3 * PAIR, width), bf16),
            made((feats, width), bf16),
            made((tokens, 2 * feats), f32),
            made((tokens, feats), bf16),
            made((tokens, feats), bf16),
            made((tokens, feats), bf16),
            made((tokens, feats), bf16),
            made((pairs, 8, tokens), f32),
        ],
        scratch_shapes=[
            pltpu.VMEM((2, tokens, PAIR), bf16),
            pltpu.VMEM((2, tokens, PAIR), bf16),
        ],
        compiler_params=ROOM,
        cost_estimate=SMALL,
        name="attend_forward",
    )(info, x_all, mine, other, cosine, sine, scale, qa, ka)


def attend_back_kernel(
    info, q_ref, k_ref, v_ref, gb_ref, x_ref, wo_ref, mix_ref, inv_ref, raw_ref, cos_ref, sin_ref, scale_ref,
    qa_ref, ka_ref,
    grad_ref, keep_ref, send_ref, gscale_ref,
    q_aug, k_aug, do_h, q_h, kt_h, delta, dq_acc, dk_acc, dv_acc, dw_acc,
):
    blocks = q_ref.shape[0] // BLOCK
    rank = info[blocks]
    first = of_first((BLOCK, PAIR), 1)
    first_rows = of_first((PAIR, BLOCK), 0)
    zero = jnp.zeros((BLOCK, PAIR), bf16)
    eight = jnp.asarray(8.0, bf16)
    same = same_head()

    def prepare(t, carry):
        start = pl.multiple_of(t * BLOCK, BLOCK)
        rows = pl.ds(start, BLOCK)
        q8 = q_ref[rows, :] * eight
        k = k_ref[rows, :]
        qa, ka = qa_ref[rows, :], ka_ref[rows, :]
        q_aug[0, rows, :] = jnp.where(first, q8, qa)
        q_aug[1, rows, :] = jnp.where(first, qa, q8)
        k_aug[0, rows, :] = jnp.where(first, k, ka)
        k_aug[1, rows, :] = jnp.where(first, ka, k)
        q_h[0, rows, :] = jnp.where(first, q8, zero)
        q_h[1, rows, :] = jnp.where(first, zero, q8)
        k_t = (k * eight).astype(f32).T
        kt_h[0, :, rows] = jnp.where(first_rows, k_t, 0.0).astype(bf16)
        kt_h[1, :, rows] = jnp.where(first_rows, 0.0, k_t).astype(bf16)
        grad = dot(gb_ref[rows, :], wo_ref[...], NT).astype(bf16)
        do_h[0, rows, :] = jnp.where(first, grad, zero)
        do_h[1, rows, :] = jnp.where(first, zero, grad)
        inner = (grad.astype(f32) * mix_ref[rows, :].astype(f32)).T
        inner = inner[:HEAD_DIM] + inner[HEAD_DIM:]
        delta[0:1, rows] = jnp.sum(inner[: HEAD_DIM // 2], axis=0, keepdims=True)
        delta[1:2, rows] = jnp.sum(inner[HEAD_DIM // 2 :], axis=0, keepdims=True)
        dk_acc[rows, :] = jnp.zeros((BLOCK, PAIR), f32)
        dv_acc[rows, :] = jnp.zeros((BLOCK, PAIR), f32)
        return carry

    lax.fori_loop(0, blocks, prepare, 0)

    row = lax.broadcasted_iota(jnp.int32, (BLOCK, BLOCK), 0)
    col = lax.broadcasted_iota(jnp.int32, (BLOCK, BLOCK), 1)
    causal = row <= col

    def query_block(g, carry):
        q_rows = pl.ds(local_rows(g, blocks // 2, rank), BLOCK)
        count = g - info[g] + 1

        def variant(nk):
            dq_t = None
            for j in range(nk):
                k_rows = pl.ds(local_rows(g - (nk - 1) + j, blocks // 2, rank), BLOCK)
                dk = dv = None
                for h in range(2):
                    scores = dot(k_aug[h, k_rows, :], q_aug[h, q_rows, :], NT)
                    p = jnp.exp(scores) * inv_ref[0, h : h + 1, q_rows]
                    if j == nk - 1:
                        p = jnp.where(causal, p, 0.0)
                    dp = dot(v_ref[k_rows, :], do_h[h, q_rows, :], NT)
                    ds = (p * (dp - delta[h : h + 1, q_rows])).astype(bf16)
                    dv_part = dot(p.astype(bf16), do_h[h, q_rows, :])
                    dk_part = dot(ds, q_h[h, q_rows, :])
                    dq_part = dot(kt_h[h, :, k_rows], ds)
                    dv = dv_part if dv is None else dv + dv_part
                    dk = dk_part if dk is None else dk + dk_part
                    dq_t = dq_part if dq_t is None else dq_t + dq_part
                dv_acc[k_rows, :] += dv
                dk_acc[k_rows, :] += dk
            dq_acc[q_rows, :] = dq_t.T

        for nk in range(1, 5):
            pl.when(count == nk if nk < 4 else count >= 4)(functools.partial(variant, nk))
        return carry

    lax.fori_loop(0, blocks, query_block, 0)

    tall = 2 * BLOCK if blocks % 2 == 0 else BLOCK

    def unturn(t, total):
        rows = pl.ds(pl.multiple_of(t * tall, tall), tall)
        cosine, sine = cos_ref[rows, :], sin_ref[rows, :]
        scale = scale_ref[0]
        for which, acc in ((0, dq_acc), (1, dk_acc)):
            raw = raw_ref[rows, which * PAIR : (which + 1) * PAIR]
            unit, size = turned_unit(raw, cosine, sine, same)
            grad = acc[rows, :]
            total = total + jnp.sum((grad * unit).reshape(tall // 8, 8, PAIR), axis=0)
            grad_unit = grad * scale
            grad_turned = size * (grad_unit - unit * head_sums(unit * grad_unit, same))
            grad_raw = grad_turned * cosine - pltpu.roll(grad_turned, HEAD_DIM, 1) * sine
            grad_ref[rows, which * PAIR : (which + 1) * PAIR] = grad_raw.astype(bf16)
        grad_ref[rows, 2 * PAIR :] = dv_acc[rows, :].astype(bf16)
        return total

    total = lax.fori_loop(0, blocks * BLOCK // tall, unturn, jnp.zeros((8, PAIR), f32))
    gscale_ref[0] = total

    dw_acc[...] = jnp.zeros_like(dw_acc)

    def row_grads(t, carry):
        rows = pl.ds(pl.multiple_of(t * tall, tall), tall)
        dw_acc[: 3 * PAIR, :] += dot(grad_ref[rows, :], x_ref[rows, :], TN)
        dw_acc[3 * PAIR :, :] += dot(mix_ref[rows, :], gb_ref[rows, :], TN)
        return carry

    lax.fori_loop(0, blocks * BLOCK // tall, row_grads, 0)
    part = HEAD_DIM // 2

    def deal(first_out, second_out):
        for t, out in enumerate((first_out, second_out)):
            for head in range(2):
                for m in range(4):
                    at = m * PAIR + t * HEAD_DIM + head * part
                    to = (head * 4 + m) * part
                    out[to : to + part, :] = dw_acc[at : at + part, :].astype(bf16)

    pl.when(rank == 0)(functools.partial(deal, keep_ref, send_ref))
    pl.when(rank != 0)(functools.partial(deal, send_ref, keep_ref))


def attend_backward(info, q, k, v, grad_branch, x, wo, mixture, inverse, raw, cosine, sine, scale, qa, ka):
    tokens, feats = q.shape
    width = x.shape[1]
    pairs = feats // PAIR
    by_pair = pl.BlockSpec((tokens, PAIR), lambda p: (0, p))
    half = pltpu.VMEM((2, tokens, PAIR), bf16)
    acc = pltpu.VMEM((tokens, PAIR), f32)
    return pl.pallas_call(
        attend_back_kernel,
        grid=(pairs,),
        in_specs=[
            pl.BlockSpec(memory_space=pltpu.SMEM),
            by_pair,
            by_pair,
            by_pair,
            whole((tokens, width)),
            whole((tokens, width)),
            pl.BlockSpec((PAIR, width), lambda p: (p, 0)),
            by_pair,
            pl.BlockSpec((1, 8, tokens), lambda p: (p, 0, 0)),
            pl.BlockSpec((tokens, 2 * PAIR), lambda p: (0, p)),
            whole((tokens, PAIR)),
            whole((tokens, PAIR)),
            pl.BlockSpec((1, 1, PAIR), lambda p: (p, 0, 0)),
            whole((tokens, PAIR)),
            whole((tokens, PAIR)),
        ],
        out_specs=[
            pl.BlockSpec((tokens, 3 * PAIR), lambda p: (0, p)),
            pl.BlockSpec((2 * PAIR, width), lambda p: (p, 0)),
            pl.BlockSpec((2 * PAIR, width), lambda p: (p, 0)),
            pl.BlockSpec((1, 8, PAIR), lambda p: (p, 0, 0)),
        ],
        out_shape=[
            made((tokens, 3 * feats), bf16),
            made((2 * feats, width), bf16),
            made((2 * feats, width), bf16),
            made((pairs, 8, PAIR), f32),
        ],
        scratch_shapes=[
            half,
            half,
            half,
            half,
            pltpu.VMEM((2, PAIR, tokens), bf16),
            pltpu.VMEM((8, tokens), f32),
            acc,
            acc,
            acc,
            pltpu.VMEM((4 * PAIR, width), f32),
        ],
        compiler_params=ROOM,
        cost_estimate=SMALL,
        name="attend_backward",
    )(info, q, k, v, grad_branch, x, wo, mixture, inverse, raw, cosine, sine, scale, qa, ka)


def up_gate_kernel(h_ref, w_ref, scale_ref, ug_ref, product_ref):
    group = product_ref.shape[1] // 4
    for k in range(4):
        pair = slice(2 * k * group, 2 * (k + 1) * group)
        both = dot(h_ref[...], w_ref[pair, :], NT)
        ug_ref[:, pair] = both.astype(bf16)
        scaled = both * scale_ref[:, pair]
        gated = scaled[:, group:]
        product = scaled[:, :group] * gated / (1.0 + jnp.exp(-gated))
        product_ref[:, k * group : (k + 1) * group] = product.astype(bf16)


def tile_of(tokens):
    return 512 if tokens % 512 == 0 else 256


def up_gate(hidden, w, scale):
    tokens, width = hidden.shape
    units = w.shape[0] // 2
    tile = tile_of(tokens)
    return pl.pallas_call(
        up_gate_kernel,
        grid=(tokens // tile,),
        in_specs=[
            pl.BlockSpec((tile, width), lambda t: (t, 0)),
            whole((2 * units, width)),
            whole((1, 2 * units)),
        ],
        out_specs=[
            pl.BlockSpec((tile, 2 * units), lambda t: (t, 0)),
            pl.BlockSpec((tile, units), lambda t: (t, 0)),
        ],
        out_shape=[
            made((tokens, 2 * units), bf16),
            made((tokens, units), bf16),
        ],
        compiler_params=ROOM,
        cost_estimate=SMALL,
        name="up_gate",
    )(hidden, w, scale)


def feed_back_kernel(
    grad_ref, h_ref, w_ref, ug_ref, product_ref, scale_ref, gug_ref, dw_ref, gscale_ref, ug_acc, d_acc
):
    group = w_ref.shape[0] // 4
    step = pl.program_id(0)

    @pl.when(step == 0)
    def _():
        gscale_ref[...] = jnp.zeros_like(gscale_ref)
        ug_acc[...] = jnp.zeros_like(ug_acc)
        d_acc[...] = jnp.zeros_like(d_acc)

    rows = grad_ref.shape[0] // 8
    d_acc[...] += dot(product_ref[...], grad_ref[...], TN)
    for k in range(4):
        ups = slice(2 * k * group, (2 * k + 1) * group)
        gates = slice((2 * k + 1) * group, (2 * k + 2) * group)
        grad = dot(grad_ref[...], w_ref[k * group : (k + 1) * group, :], NT)
        up = ug_ref[:, ups].astype(f32)
        gate = ug_ref[:, gates].astype(f32)
        up_scale, gate_scale = scale_ref[:, ups], scale_ref[:, gates]
        gated = gate * gate_scale
        sig = 1.0 / (1.0 + jnp.exp(-gated))
        silu = gated * sig
        through = grad * silu
        grad_gated = grad * (up * up_scale) * (sig + silu * (1.0 - sig))
        gug_ref[:, ups] = (through * up_scale).astype(bf16)
        gug_ref[:, gates] = (grad_gated * gate_scale).astype(bf16)
        gscale_ref[:, ups] += jnp.sum((through * up).reshape(rows, 8, group), axis=0)
        gscale_ref[:, gates] += jnp.sum((grad_gated * gate).reshape(rows, 8, group), axis=0)
    ug_acc[...] += dot(gug_ref[...], h_ref[...], TN)

    @pl.when(step == pl.num_programs(0) - 1)
    def _():
        for k in range(4):
            at = 3 * k * group
            dw_ref[at : at + 2 * group, :] = ug_acc[2 * k * group : 2 * (k + 1) * group, :].astype(bf16)
            dw_ref[at + 2 * group : at + 3 * group, :] = d_acc[k * group : (k + 1) * group, :].astype(bf16)


def feed_back(grad, hidden, w, ug, product, scale):
    tokens, width = grad.shape
    units = w.shape[0]
    tile = tile_of(tokens)
    row = pl.BlockSpec((tile, width), lambda t: (t, 0))
    wide = pl.BlockSpec((tile, 2 * units), lambda t: (t, 0))
    return pl.pallas_call(
        feed_back_kernel,
        grid=(tokens // tile,),
        in_specs=[
            row,
            row,
            whole((units, width)),
            wide,
            pl.BlockSpec((tile, units), lambda t: (t, 0)),
            whole((1, 2 * units)),
        ],
        out_specs=[wide, whole((3 * units, width)), whole((8, 2 * units))],
        out_shape=[
            made((tokens, 2 * units), bf16),
            made((3 * units, width), bf16),
            made((8, 2 * units), f32),
        ],
        scratch_shapes=[pltpu.VMEM((2 * units, width), f32), pltpu.VMEM((units, width), f32)],
        compiler_params=ROOM,
        cost_estimate=SMALL,
        name="feed_back",
    )(grad, hidden, w, ug, product, scale)


def sum_dots_kernel(count, *refs):
    total = dot(refs[0][...], refs[count][...])
    for c in range(1, count):
        total = total + dot(refs[c][...], refs[count + c][...])
    if len(refs) > 2 * count + 1:
        total = total + refs[2 * count][...].astype(f32)
    refs[-1][...] = total.astype(refs[-1].dtype)


def sum_dots(lefts, rights, start, rows, dtype, addend=None):
    tile = 256
    depth, width = rights[0].shape
    count = len(lefts)
    more = [] if addend is None else [addend]
    return pl.pallas_call(
        functools.partial(sum_dots_kernel, count),
        grid=(rows // tile,),
        in_specs=[pl.BlockSpec((tile, depth), lambda t: (t + start // tile, 0))] * count
        + [whole((depth, width))] * count
        + [pl.BlockSpec((tile, width), lambda t: (t, 0))] * len(more),
        out_specs=pl.BlockSpec((tile, width), lambda t: (t, 0)),
        out_shape=made((rows, width), dtype),
        compiler_params=ROOM,
        cost_estimate=SMALL,
        name="sum_dots",
    )(*lefts, *rights, *more)


def rms_scale(values):
    return lax.rsqrt(jnp.mean(values * values, axis=-1, keepdims=True) + norm_eps)


def blend_parts(residual, branch, mixing):
    branch_scale = rms_scale(branch)
    unit = branch * branch_scale
    step = unit - residual
    mixed = residual + mixing * step
    mixed_scale = rms_scale(mixed)
    return branch_scale, unit, step, mixed * mixed_scale, mixed_scale


def blend_grads(parts, mixing, grad):
    branch_scale, unit, step, result, mixed_scale = parts
    grad_mixed = mixed_scale * (grad - result * jnp.mean(grad * result, axis=-1, keepdims=True))
    grad_unit = mixing * grad_mixed
    grad_branch = branch_scale * (grad_unit - unit * jnp.mean(unit * grad_unit, axis=-1, keepdims=True))
    return grad_mixed - grad_unit, grad_branch, grad_mixed * step


def add_rows(ref, values):
    @pl.when(pl.program_id(0) == 0)
    def _():
        ref[...] = jnp.zeros_like(ref)

    ref[...] += jnp.sum(values.reshape(values.shape[0] // 8, 8, values.shape[1]), axis=0)


def hidden_kernel(x_ref, own_ref, other_ref, mix_ref, hidden_ref, round_ref):
    branch = own_ref[...] + other_ref[...].astype(f32)
    hidden = blend_parts(x_ref[...].astype(f32), branch, mix_ref[...])[3]
    hidden_ref[...] = hidden
    round_ref[...] = hidden.astype(bf16)


def output_kernel(
    hidden_ref, own_ref, other_ref, mix_ref, cot_ref, out_ref, res_ref, down_ref, gmix_ref
):
    mixing = mix_ref[...]
    parts = blend_parts(hidden_ref[...], own_ref[...] + other_ref[...].astype(f32), mixing)
    out_ref[...] = parts[3]
    grad_res, grad_down, grad_mix = blend_grads(parts, mixing, cot_ref[...].astype(f32))
    res_ref[...] = grad_res
    down_ref[...] = grad_down.astype(bf16)
    add_rows(gmix_ref, grad_mix)


def hidden_back_kernel(
    x_ref, own_ref, other_ref, mix_ref, res_ref, back_ref, from_ref, in_ref, branch_ref, gmix_ref
):
    mixing = mix_ref[...]
    parts = blend_parts(x_ref[...].astype(f32), own_ref[...] + other_ref[...].astype(f32), mixing)
    grad = res_ref[...] + back_ref[...] + from_ref[...].astype(f32)
    grad_res, grad_branch, grad_mix = blend_grads(parts, mixing, grad)
    in_ref[...] = grad_res
    branch_ref[...] = grad_branch.astype(bf16)
    add_rows(gmix_ref, grad_mix)


def rowwise(kernel, name, arrays, outs, reduced=False):
    tokens, width = arrays[0].shape
    tile = 128
    row = pl.BlockSpec((tile, width), lambda t: (t, 0))
    out_shape = [made((tokens * (2 if dtype == bf16 else 1), width), dtype) for dtype in outs]
    out_specs = [row] * len(outs)
    if reduced:
        out_shape.append(made((8, width), f32))
        out_specs.append(whole((8, width)))
    return pl.pallas_call(
        kernel,
        grid=(tokens // tile,),
        in_specs=[row if a.shape[0] == tokens else whole((1, width)) for a in arrays],
        out_specs=out_specs,
        out_shape=out_shape,
        compiler_params=ROOM,
        cost_estimate=SMALL,
        name=name,
    )(*arrays)


def adam_change(weight, gradient, moment_one, moment_two, renormalize):
    moment_one_new = beta_one * moment_one + (1.0 - beta_one) * gradient
    moment_two_new = beta_two * moment_two + (1.0 - beta_two) * gradient * gradient
    stepped = weight - learn_rate * (moment_one_new / corr_one) / (
        jnp.sqrt(moment_two_new / corr_two) + adam_eps
    )
    if renormalize:
        stepped = stepped * lax.rsqrt(jnp.sum(stepped * stepped, axis=-1, keepdims=True) + norm_eps)
    return stepped - weight


def adam_kernel(w_ref, g_ref, one_ref, two_ref, out_ref):
    out_ref[...] = adam_change(w_ref[...], g_ref[...], one_ref[...], two_ref[...], True)


def adam_rows(weight, gradient, moment_one, moment_two):
    shape = weight.shape
    rows, width = shape[0] * shape[1], shape[2]
    tile = next(t for t in (128, 64, 32, 16, 8) if rows % t == 0)
    block = pl.BlockSpec((tile, width), lambda t: (t, 0))
    return pl.pallas_call(
        adam_kernel,
        grid=(rows // tile,),
        in_specs=[block] * 4,
        out_specs=block,
        out_shape=made((rows, width), f32),
        compiler_params=ROOM,
        cost_estimate=SMALL,
        name="adam",
    )(*(a.reshape(rows, width) for a in (weight, gradient, moment_one, moment_two))).reshape(shape)


def own_half(x, rank, axis):
    size = x.shape[axis] // 2
    return lax.dynamic_slice_in_dim(x, rank * size, size, axis)


def pick(rank, zero, one):
    return jnp.where(rank == 0, zero, one)


def document_tables(segment_ids, rank, count):
    segments = segment_ids.reshape(-1)
    docs = jnp.arange(8, dtype=jnp.int32)
    begins = jnp.sum((segments[None, :] < docs[:, None]).astype(jnp.int32), axis=1)
    is_doc = segments[:, None] == docs[None, :]
    starts = jnp.sum(jnp.where(is_doc, begins[None, :], 0), axis=1)
    info = jnp.concatenate([starts[::BLOCK] // BLOCK, rank[None].astype(jnp.int32)])
    place = jnp.arange(2 * count, dtype=jnp.int32)

    def arranged(values):
        own = lax.dynamic_slice_in_dim(values, rank * count, count, 0)
        other = lax.dynamic_slice_in_dim(values, (1 - rank) * count, count, 0)
        return jnp.concatenate([own, other], 0)

    positions = arranged(place - starts).astype(f32)
    frequency = jnp.exp(
        jnp.arange(HEAD_DIM // 2, dtype=f32) * (-2.0 * math.log(rope_base) / HEAD_DIM)
    )
    angles = positions[:, None] * jnp.tile(frequency, 4)[None, :]
    cosine = jnp.cos(angles)
    sign = jnp.where(jnp.arange(PAIR) < HEAD_DIM, -1.0, 1.0).astype(f32)
    sine = jnp.sin(angles) * sign[None, :]
    lanes = jnp.arange(PAIR, dtype=jnp.int32)
    lanes = jnp.where(lanes < HEAD_DIM, lanes & 31, 8)
    own_doc = arranged(segments)[:, None] == lanes[None, :]
    query_mark = own_doc.astype(bf16)
    key_mark = jnp.where(own_doc | (lanes >= 8)[None, :], 0.0, -apart).astype(bf16)
    return info, cosine, sine, query_mark, key_mark


def pair_lanes(values):
    pairs = values.shape[0]
    return jnp.swapaxes(values.reshape(pairs, 2, 2, HEAD_DIM // 2), 1, 2).reshape(pairs, 1, PAIR)


def head_order(values):
    pairs = values.shape[0]
    return jnp.swapaxes(values.reshape(pairs, 2, 2, HEAD_DIM // 2), 1, 2).reshape(2 * pairs, HEAD_DIM)


class Group:
    def __init__(self, tables, x_all, mine, other, scale):
        self.tables, self.scale = tables, scale
        info, cosine, sine, query_mark, key_mark = tables
        (self.w, self.wo, self.raw, self.q, self.k, self.v, self.mixture, self.inverse) = attend_forward(
            info, x_all, mine, other, cosine, sine, scale, query_mark, key_mark
        )

    def back(self, grad_branch, x_all):
        info, cosine, sine, query_mark, key_mark = self.tables
        grad_qkv, keep, send, grad_scale = attend_backward(
            info, self.q, self.k, self.v, grad_branch, x_all, self.wo, self.mixture, self.inverse, self.raw,
            cosine, sine, self.scale, query_mark, key_mark,
        )
        return grad_qkv, keep, send, head_order(jnp.sum(grad_scale, axis=1))


def local_sixteen(
    tokens,
    segment_ids,
    cotangent,
    attention_weights,
    feed_weights,
    attention_scales,
    feed_scales,
    attention_first,
    attention_second,
    feed_first,
    feed_second,
    attention_scale_first,
    attention_scale_second,
    feed_scale_first,
    feed_scale_second,
):
    count, width = tokens.shape[0] * tokens.shape[1], tokens.shape[-1]
    rank, place = lax.axis_index("seq"), lax.axis_index("dp")
    slots = jnp.arange(HEADS, dtype=jnp.int32)
    x = tokens.reshape(count, width)

    part = own_half(attention_weights, rank, 1).astype(bf16)
    rows = part.shape[1]
    body = 4 * rows
    extra = jnp.concatenate(
        [attention_scales.reshape(-1), own_half(feed_scales, rank, 1).reshape(-1)]
    ).astype(bf16)
    used = extra.shape[0]
    extra = jnp.pad(extra[None], ((0, 7), (0, width - used)))
    block_a = jnp.concatenate([part.reshape(body, width), extra], axis=0)
    feed_part = own_half(feed_weights, rank, 1).astype(bf16)
    units = feed_part.shape[1]
    block_u = feed_part[:2].reshape(2 * units, width)
    block_d = feed_part[2]

    z_a = by_z(block_a)
    x_other = swap(x)
    tables = document_tables(segment_ids, rank, count)
    x_all = jnp.concatenate([x, x_other], 0)
    block_a, z_a, block_u, block_d, x_all, tables = tie(block_a, z_a, block_u, block_d, x_all, tables)

    own_a = join(block_a, *z_a)
    x_a, y_a = via(own_a, 1), via(own_a, 2)
    z_u = [via(block_u, 4), via(block_u, 8)]
    own_a, x_a, y_a, z_u, block_u = tie(own_a, x_a, y_a, z_u, block_u)

    def bare(chunk):
        return chunk.reshape(4, -1, width)[:, :body].reshape(4 * body, width)

    def extras(chunk):
        return chunk.reshape(4, -1, width)[:, body, :used].astype(f32)

    def qk_scale(extras_of):
        return pair_lanes(extras_of[:, :HEAD_DIM].reshape(2, 2, HEAD_DIM))

    d_a = diagonal_in(x_a, y_a)
    z_u = z_u + [via(block_u, 12)]
    other_0 = swap(pick(rank, bare(y_a), bare(own_a)))
    mine_0 = pick(rank, bare(own_a), bare(y_a))
    scale_0 = qk_scale(pick(rank, extras(own_a), extras(y_a)))
    group_0 = Group(tables, x_all, mine_0, other_0, scale_0)
    d_a, z_u, block_u, block_d, group_0.mixture, x_all = tie(
        d_a, z_u, block_u, block_d, group_0.mixture, x_all
    )

    own_u = join(block_u, *z_u)
    x_u, y_u = via(own_u, 1), via(own_u, 2)
    z_d = by_z(block_d)
    d_a = join(*d_a)
    other_1 = swap(pick(rank, bare(d_a), bare(x_a)))
    mine_1 = pick(rank, bare(x_a), bare(d_a))
    scale_1 = qk_scale(pick(rank, extras(x_a), extras(d_a)))
    group_1 = Group(tables, x_all, mine_1, other_1, scale_1)
    groups = (group_0, group_1)
    mixtures, wos = [g.mixture for g in groups], [g.wo for g in groups]
    branch_other = sum_dots(mixtures, wos, count, count, bf16)
    branch_own = sum_dots(mixtures, wos, 0, count, f32)
    branch_other, branch_own, x_u, y_u, z_d, d_a = tie(branch_other, branch_own, x_u, y_u, z_d, d_a)

    d_u = diagonal_in(x_u, y_u)
    own_d = join(block_d, *z_d)
    d_u, own_d = tie(d_u, own_d)
    x_d, y_d = via(own_d, 1), via(own_d, 2)
    all_extras = jnp.concatenate([extras(c) for c in (own_a, x_a, y_a, d_a)], 0)
    alpha = jnp.take(all_extras[:, HEAD_DIM : 3 * HEAD_DIM], slot_of(slots ^ place), axis=0)
    alpha = jnp.swapaxes(alpha.reshape(HEADS, 2, HEAD_DIM), 0, 1).reshape(2, width)
    feed_scale = all_extras[:, 3 * HEAD_DIM :].reshape(4, 1, -1)

    branch_from = swap(branch_other)
    hidden, hidden_round = rowwise(
        hidden_kernel, "hidden", [x, branch_own, branch_from, alpha[:1]], [f32, bf16]
    )
    hidden_all = fill(hidden_round, swap(hidden_round[:count]))
    ug_own, product_own = up_gate(hidden_all, own_u, feed_scale[0])
    ug_x, product_x = up_gate(hidden_all, x_u, feed_scale[1])
    ug_y, product_y = up_gate(hidden_all, y_u, feed_scale[2])
    product_own, product_x, product_y, hidden_all, d_u, x_d, y_d = tie(
        product_own, product_x, product_y, hidden_all, d_u, x_d, y_d
    )

    d_d = diagonal_in(x_d, y_d)
    d_u = join(*d_u)
    ug_d, product_d = up_gate(hidden_all, d_u, feed_scale[3])
    products = [product_own, product_x, product_y]
    w_ds = [own_d, x_d, y_d]
    down_other = sum_dots(products, w_ds, count, count, f32)
    down_own = sum_dots(products, w_ds, 0, count, f32)
    down_other, down_own, d_d, product_d = tie(down_other, down_own, d_d, product_d)

    d_d = join(*d_d)
    down_other = sum_dots([product_d], [d_d], count, count, bf16, down_other)
    down_own = sum_dots([product_d], [d_d], 0, count, f32, down_own)
    output, grad_hidden_res, grad_down_round, grad_alpha_feed = rowwise(
        output_kernel,
        "output",
        [hidden, down_own, swap(down_other), alpha[1:], cotangent.reshape(count, width)],
        [f32, f32, bf16],
        True,
    )

    grad_down = fill(grad_down_round, swap(grad_down_round[:count]))

    gug_d, r_d, gs_d = feed_back(grad_down, hidden_all, d_d, ug_d, product_d, feed_scale[3])
    r_d, grad_down, product_x, product_y, product_own = tie(r_d, grad_down, product_x, product_y, product_own)
    t_d = diagonal_out(r_d)
    gug_x, r_x, gs_x = feed_back(grad_down, hidden_all, x_d, ug_x, product_x, feed_scale[1])
    gug_y, r_y, gs_y = feed_back(grad_down, hidden_all, y_d, ug_y, product_y, feed_scale[2])
    gug_own, r_own, gs_own = feed_back(grad_down, hidden_all, own_d, ug_own, product_own, feed_scale[0])
    gugs, w_ugs = [gug_own, gug_x, gug_y, gug_d], [own_u, x_u, y_u, d_u]
    t_d, r_x, r_y, r_own, gugs = tie(t_d, r_x, r_y, r_own, gugs)

    r_x, r_y = with_diagonal(r_x, r_y, t_d)
    r_x, r_y, gugs = tie(r_x, r_y, gugs)
    v_x, v_y = via(r_x, 1), via(r_y, 2)
    back_other = sum_dots(gugs, w_ugs, count, count, bf16)
    back_from = swap(back_other)
    back_own = sum_dots(gugs, w_ugs, 0, count, f32)
    grad_input_res, grad_branch_round, grad_alpha_attend = rowwise(
        hidden_back_kernel,
        "hidden_back",
        [x, branch_own, branch_from, alpha[:1], grad_hidden_res, back_own, back_from],
        [f32, bf16],
        True,
    )
    grad_branch_all = fill(grad_branch_round, swap(grad_branch_round[:count]))
    grad_qkv_1, keep_1, send_1, gscale_1 = group_1.back(grad_branch_all, x_all)
    v_x, v_y, grad_qkv_1, keep_1, send_1, gscale_1, grad_branch_all = tie(
        v_x, v_y, grad_qkv_1, keep_1, send_1, gscale_1, grad_branch_all
    )

    other_1 = swap(send_1)
    feed_mine, feed_parts = column_sum(r_own, v_x, v_y)
    other_1, feed_mine, feed_parts, keep_1, gscale_1 = tie(other_1, feed_mine, feed_parts, keep_1, gscale_1)
    z_feed = [via(feed_parts[0], 4), via(feed_parts[1], 8)]

    alpha_terms = jnp.stack([jnp.sum(grad_alpha_attend, 0), jnp.sum(grad_alpha_feed, 0)])
    alpha_terms = jnp.swapaxes(alpha_terms.reshape(2, HEADS, HEAD_DIM), 0, 1).reshape(HEADS, 2 * HEAD_DIM)
    alpha_terms = jnp.take(alpha_terms, place ^ offset_of(slots), axis=0)

    def sent(body_rows, grad_scale, c, grad_feed):
        terms = jnp.concatenate(
            [grad_scale, alpha_terms[4 * c : 4 * c + 4], jnp.sum(grad_feed, 0).reshape(4, -1)], 1
        ).astype(bf16)
        terms = jnp.pad(terms[:, None], ((0, 0), (0, 7), (0, width - used)))
        return jnp.concatenate([body_rows.reshape(4, body, width), terms], 1).reshape(-1, width)

    zero_scale = jnp.zeros((4, HEAD_DIM), f32)
    a_x = sent(pick(rank, keep_1, other_1), pick(rank, gscale_1, zero_scale), 1, gs_x)
    a_d = sent(pick(rank, other_1, keep_1), pick(rank, zero_scale, gscale_1), 3, gs_d)
    a_x, a_d, grad_branch_all = tie(a_x, a_d, grad_branch_all)
    t_a = diagonal_out(a_d)
    grad_qkv_0, keep_0, send_0, gscale_0 = group_0.back(grad_branch_all, x_all)
    t_a, z_feed, grad_qkv_0, keep_0, send_0, gscale_0 = tie(t_a, z_feed, grad_qkv_0, keep_0, send_0, gscale_0)

    z_feed = z_feed + [via(feed_parts[2], 12)]
    other_0 = swap(send_0)
    a_own = sent(pick(rank, keep_0, other_0), pick(rank, gscale_0, zero_scale), 0, gs_own)
    a_y = sent(pick(rank, other_0, keep_0), pick(rank, zero_scale, gscale_0), 2, gs_y)
    a_x, a_y = with_diagonal(a_x, a_y, t_a)
    a_x, a_y, grad_qkv_0 = tie(a_x, a_y, grad_qkv_0)
    b_x, b_y = via(a_x, 1), via(a_y, 2)
    grad_qkvs = [grad_qkv_0, grad_qkv_1]
    w_flats = [g.w.reshape(-1, width) for g in groups]
    input_other = sum_dots(grad_qkvs, w_flats, count, count, bf16)
    input_own = sum_dots(grad_qkvs, w_flats, 0, count, f32, grad_input_res)
    input_other, input_own, b_x, b_y, z_feed = tie(input_other, input_own, b_x, b_y, z_feed)

    attend_mine, attend_parts = column_sum(a_own, b_x, b_y)
    attend_parts = z_out(attend_parts)
    input_grad = input_own + swap(input_other).astype(f32)
    total = z_sum(feed_mine, z_feed).reshape(3, units, width)
    other = swap(total)
    feed_grad = jnp.concatenate([pick(rank, total, other), pick(rank, other, total)], 1)
    feed_change = adam_rows(feed_weights, feed_grad, feed_first, feed_second)
    attend_parts, input_grad, feed_grad, feed_change = tie(attend_parts, input_grad, feed_grad, feed_change)

    total = z_sum(attend_mine, attend_parts)
    other = swap(total)
    low, high = pick(rank, total, other), pick(rank, other, total)
    attend_grad = jnp.concatenate(
        [low[:body].reshape(4, rows, width), high[:body].reshape(4, rows, width)], 1
    )
    at = 3 * HEAD_DIM
    attend_grad_s = (low[body, :at] + high[body, :at]).reshape(3, HEAD_DIM)
    feed_grad_s = jnp.concatenate(
        [low[body, at:used].reshape(2, -1), high[body, at:used].reshape(2, -1)], 1
    )
    return (
        output.reshape(tokens.shape),
        input_grad.reshape(tokens.shape),
        attend_grad,
        feed_grad,
        attend_grad_s,
        feed_grad_s,
        adam_rows(attention_weights, attend_grad, attention_first, attention_second),
        feed_change,
        adam_change(attention_scales, attend_grad_s, attention_scale_first, attention_scale_second, False),
        adam_change(feed_scales, feed_grad_s, feed_scale_first, feed_scale_second, False),
    )


def local_any(
    tokens,
    segment_ids,
    cotangent,
    attention_weights,
    feed_weights,
    attention_scales,
    feed_scales,
    attention_first,
    attention_second,
    feed_first,
    feed_second,
    attention_scale_first,
    attention_scale_second,
    feed_scale_first,
    feed_scale_second,
):
    count, width = tokens.shape[0] * tokens.shape[1], tokens.shape[-1]
    rank = lax.axis_index("seq")
    x = tokens.reshape(count, width)
    x_all = jnp.concatenate([x, swap(x)], axis=0)
    tables = document_tables(segment_ids, rank, count)

    full = lax.all_gather(attention_weights.astype(bf16), "dp", axis=1, tiled=True)
    scales = lax.all_gather(attention_scales.astype(bf16), "dp", axis=1, tiled=True).astype(f32)
    half = width // 2
    alpha = scales[1:]
    mine = lax.dynamic_slice_in_dim(full, rank * half, half, 1)
    mine = jnp.swapaxes(mine.reshape(4, HEADS // 2, 2, HEAD_DIM // 2, width), 0, 1)
    own_scale = lax.dynamic_slice_in_dim(scales[0], rank * half, half, 0).reshape(2, 2, 2, HEAD_DIM)
    groups = []
    for g in range(2):
        heads = mine[4 * g : 4 * g + 4]
        low = heads[:, :, 0].reshape(-1, width)
        high = heads[:, :, 1].reshape(-1, width)
        groups.append(Group(tables, x_all, pick(rank, low, high), pick(rank, high, low), pair_lanes(own_scale[g])))

    feed = lax.all_gather(own_half(feed_weights, rank, 1).astype(bf16), "dp", axis=1, tiled=True)
    feed_s = lax.all_gather(own_half(feed_scales, rank, 1).astype(bf16), "dp", axis=1, tiled=True).astype(f32)
    units = feed.shape[1] // 4
    w_ugs, w_ds, feed_scale = [], [], []
    for c in range(4):
        piece = feed[:2, c * units : (c + 1) * units].reshape(2, 4, units // 4, width)
        w_ugs.append(jnp.swapaxes(piece, 0, 1).reshape(2 * units, width))
        w_ds.append(feed[2, c * units : (c + 1) * units])
        piece = feed_s[:, c * units : (c + 1) * units].reshape(2, 4, units // 4)
        feed_scale.append(jnp.swapaxes(piece, 0, 1).reshape(1, 2 * units))

    mixtures, wos = [g.mixture for g in groups], [g.wo for g in groups]
    branch_other = sum_dots(mixtures, wos, count, count, bf16)
    branch_own, branch_from = sum_dots(mixtures, wos, 0, count, f32), swap(branch_other)
    hidden, hidden_round = rowwise(
        hidden_kernel, "hidden", [x, branch_own, branch_from, alpha[:1]], [f32, bf16]
    )
    hidden_all = fill(hidden_round, swap(hidden_round[:count]))
    ugs, products = zip(*[up_gate(hidden_all, w, s) for w, s in zip(w_ugs, feed_scale)])
    down_other = sum_dots(products, w_ds, count, count, bf16)
    down_own = sum_dots(products, w_ds, 0, count, f32)
    output, grad_hidden_res, grad_down_round, grad_alpha_feed = rowwise(
        output_kernel,
        "output",
        [hidden, down_own, swap(down_other), alpha[1:], cotangent.reshape(count, width)],
        [f32, f32, bf16],
        True,
    )
    grad_down = fill(grad_down_round, swap(grad_down_round[:count]))
    gugs, rows, gscales = zip(
        *[
            feed_back(grad_down, hidden_all, w, ug, product, s)
            for w, ug, product, s in zip(w_ds, ugs, products, feed_scale)
        ]
    )
    back_other = sum_dots(gugs, w_ugs, count, count, bf16)
    back_own = sum_dots(gugs, w_ugs, 0, count, f32)
    grad_input_res, grad_branch_round, grad_alpha_attend = rowwise(
        hidden_back_kernel,
        "hidden_back",
        [x, branch_own, branch_from, alpha[:1], grad_hidden_res, back_own, swap(back_other)],
        [f32, bf16],
        True,
    )
    grad_branch_all = fill(grad_branch_round, swap(grad_branch_round[:count]))

    terms, term_scales = [], []
    for chunk, gscale in zip(rows, gscales):
        terms.append(jnp.swapaxes(chunk.reshape(4, 3, units // 4, width), 0, 1).reshape(3, units, width))
        piece = jnp.sum(gscale, 0).reshape(4, 2, units // 4)
        term_scales.append(jnp.swapaxes(piece, 0, 1).reshape(2, units))

    def scattered(values):
        return lax.psum_scatter(values, "dp", scatter_dimension=1, tiled=True)

    def both_halves(total):
        other = swap(total)
        return jnp.concatenate([pick(rank, total, other), pick(rank, other, total)], 1)

    feed_grad = both_halves(scattered(jnp.concatenate(terms, 1)).astype(f32))
    feed_grad_s = both_halves(scattered(jnp.concatenate(term_scales, 1)))

    grad_qkvs, gscales, pieces = [], [], []
    for group in groups:
        grad_qkv, keep, send, grad_scale = group.back(grad_branch_all, x_all)
        halves = jnp.stack([pick(rank, keep, send), pick(rank, send, keep)])
        halves = halves.reshape(2, 4, 4, HEAD_DIM // 2, width)
        pieces.append(jnp.transpose(halves, (2, 1, 0, 3, 4)).reshape(4, 4 * HEAD_DIM, width))
        grad_qkvs.append(grad_qkv)
        gscales.append(grad_scale.reshape(1, -1))
    w_flats = [g.w.reshape(-1, width) for g in groups]
    input_other = sum_dots(grad_qkvs, w_flats, count, count, bf16)
    input_own = sum_dots(grad_qkvs, w_flats, 0, count, f32)
    input_grad = grad_input_res + input_own + swap(input_other).astype(f32)

    total = jnp.zeros((4, width, width), bf16)
    total = scattered(lax.dynamic_update_slice(total, jnp.concatenate(pieces, 1), (0, rank * half, 0)))
    attend_grad = total.astype(f32) + swap(total.astype(f32))
    qk = jnp.zeros((1, width), f32)
    qk = lax.dynamic_update_slice(qk, jnp.concatenate(gscales, 1), (0, rank * half))
    total = jnp.concatenate(
        [qk, jnp.sum(grad_alpha_attend, 0)[None], jnp.sum(grad_alpha_feed, 0)[None]], 0
    )
    total = scattered(total)
    attend_grad_s = total + swap(total)
    return (
        output.reshape(tokens.shape),
        input_grad.reshape(tokens.shape),
        attend_grad,
        feed_grad,
        attend_grad_s,
        feed_grad_s,
        adam_rows(attention_weights, attend_grad, attention_first, attention_second),
        adam_rows(feed_weights, feed_grad, feed_first, feed_second),
        adam_change(attention_scales, attend_grad_s, attention_scale_first, attention_scale_second, False),
        adam_change(feed_scales, feed_grad_s, feed_scale_first, feed_scale_second, False),
    )


def solution(mesh):
    rows = P("dp", "seq", None)
    matrix = P(None, "dp", None)
    scale = P(None, "dp")
    return jax.shard_map(
        local_sixteen if mesh.shape["dp"] == HEADS else local_any,
        mesh=mesh,
        in_specs=(rows, P("dp", None), rows, matrix, matrix, scale, scale)
        + (matrix,) * 4
        + (scale,) * 4,
        out_specs=(rows, rows, matrix, matrix, scale, scale, matrix, matrix, scale, scale),
        check_vma=False,
    )
```

```python
import functools
import math

import jax
import jax.numpy as jnp
from jax import lax
from jax.experimental import pallas as pl
from jax.experimental.pallas import tpu as pltpu
from jax.sharding import PartitionSpec as P

HEADS = 16
HEAD_DIM = 64
PAIR = 2 * HEAD_DIM
BLOCK = 256
ROWS = 4 * (HEAD_DIM // 2) + 16

norm_eps = 1e-06
rope_base = 10000.0
learn_rate = 0.003
beta_one = 0.9
beta_two = 0.95
adam_eps = 1e-08
corr_one = 1.0 - 0.9**10
corr_two = 1.0 - 0.95**10
apart = 1024.0

bf16 = jnp.bfloat16
f32 = jnp.float32
NT = (((1,), (1,)), ((), ()))
NN = (((1,), (0,)), ((), ()))
TN = (((0,), (0,)), ((), ()))
MIB = 1024 * 1024
SMALL = pl.CostEstimate(flops=1, bytes_accessed=1, transcendentals=0)
ROOM = pltpu.CompilerParams(vmem_limit_bytes=40 * MIB)


def made(shape, dtype):
    return pltpu.HBM(shape, dtype)


def far(*arrays):
    return [pltpu.with_memory_space_constraint(a, pltpu.HBM) for a in arrays]


def dot(a, b, dims=NN, precision=None):
    return lax.dot_general(a, b, dims, precision=precision, preferred_element_type=f32)


def tie(*values):
    return lax.optimization_barrier(values)


def swap(x):
    return lax.ppermute(x, "seq", [(0, 1), (1, 0)])


def via(x, bits):
    count = lax.axis_size("dp")
    return lax.ppermute(x, "dp", [(i, i ^ bits) for i in range(count)])


def upper_half(x):
    return x[: x.shape[0] // 2]


def lower_half(x):
    return x[x.shape[0] // 2 :]


def join_kernel(steps, *refs):
    for k in range(len(refs) - 1):

        @pl.when(pl.program_id(0) // steps == k)
        def _():
            refs[-1][...] = refs[k][...]


def join(*parts):
    rows, width = parts[0].shape
    steps = max(1, rows // 256)
    tile = rows // steps

    def spec(k):
        return pl.BlockSpec((tile, width), lambda t: (jnp.clip(t - k * steps, 0, steps - 1), 0))

    return pl.pallas_call(
        functools.partial(join_kernel, steps),
        grid=(len(parts) * steps,),
        in_specs=[spec(k) for k in range(len(parts))],
        out_specs=pl.BlockSpec((tile, width), lambda t: (t, 0)),
        out_shape=made((len(parts) * rows, width), parts[0].dtype),
        compiler_params=ROOM,
        cost_estimate=SMALL,
        name="join",
    )(*parts)


def fill_kernel(whole_ref, part_ref, out_ref):
    out_ref[...] = part_ref[...]


def fill(target, part):
    rows, width = part.shape
    tile = rows // 2
    return pl.pallas_call(
        fill_kernel,
        grid=(2,),
        in_specs=[pl.BlockSpec(memory_space=pl.ANY), pl.BlockSpec((tile, width), lambda t: (t, 0))],
        out_specs=pl.BlockSpec((tile, width), lambda t: (t + 2, 0)),
        out_shape=made(target.shape, target.dtype),
        input_output_aliases={0: 0},
        compiler_params=ROOM,
        cost_estimate=SMALL,
        name="fill",
    )(target, part)


def half_kernel(x_ref, out_ref):
    out_ref[...] = x_ref[...]


def half_of(x, lower):
    rows, width = x.shape[0] // 4, x.shape[1]
    at = 2 if lower else 0
    return pl.pallas_call(
        half_kernel,
        grid=(2,),
        in_specs=[pl.BlockSpec((rows, width), lambda t: (t + at, 0))],
        out_specs=pl.BlockSpec((rows, width), lambda t: (t, 0)),
        out_shape=made((2 * rows, width), x.dtype),
        compiler_params=ROOM,
        cost_estimate=SMALL,
        name="half",
    )(x)


def diagonal_in(by_x, by_y):
    return via(half_of(by_y, False), 1), via(half_of(by_x, True), 2)


def plus(a, b):
    return (a.astype(f32) + b.astype(f32)).astype(bf16)


def add_half_kernel(a_ref, b_ref, o_ref):
    o_ref[...] = plus(a_ref[...], b_ref[...])


def add_half(x, part, lower):
    rows, width = part.shape
    tile = rows // 2
    at = 2 if lower else 0
    return pl.pallas_call(
        add_half_kernel,
        grid=(2,),
        in_specs=[
            pl.BlockSpec((tile, width), lambda t: (t + at, 0)),
            pl.BlockSpec((tile, width), lambda t: (t, 0)),
        ],
        out_specs=pl.BlockSpec((tile, width), lambda t: (t + at, 0)),
        out_shape=made(x.shape, x.dtype),
        input_output_aliases={0: 0},
        compiler_params=ROOM,
        cost_estimate=SMALL,
        name="add_half",
    )(x, part)


def column_kernel(own_ref, x_ref, y_ref, *outs):
    total = own_ref[...].astype(f32) + x_ref[...].astype(f32) + y_ref[...].astype(f32)
    for k in range(4):

        @pl.when(pl.program_id(0) == k)
        def _():
            outs[k][...] = total.astype(outs[k].dtype)


def column_sum(own, from_x, from_y):
    rows, width = own.shape[0] // 4, own.shape[1]
    block = pl.BlockSpec((rows, width), lambda t: (t, 0))
    mine, *parts = pl.pallas_call(
        column_kernel,
        grid=(4,),
        in_specs=[block] * 3,
        out_specs=[whole((rows, width))] * 4,
        out_shape=[made((rows, width), f32)] + [made((rows, width), bf16)] * 3,
        compiler_params=ROOM,
        cost_estimate=SMALL,
        name="column_sum",
    )(own, from_x, from_y)
    return mine, parts


def z_sum(mine, parts):
    for part in parts:
        mine = mine + part.astype(f32)
    return mine


def slot_of(offset):
    return (offset & 3) * 4 + (offset >> 2)


def of_first(shape, dim):
    return (lax.broadcasted_iota(jnp.int32, shape, dim) & 32) == 0


def head_sums(x, same):
    high = x.astype(bf16)
    low = (x - high.astype(f32)).astype(bf16)
    return dot(high, same) + dot(low, same)


def same_head():
    same = of_first((PAIR, PAIR), 0) == of_first((PAIR, PAIR), 1)
    return jnp.where(same, 1.0, 0.0).astype(bf16)


def turned_unit(raw, cosine, sine, same):
    turned = raw * cosine + pltpu.roll(raw, HEAD_DIM, 1) * sine
    scale = lax.rsqrt(head_sums(turned * turned, same) + norm_eps)
    return turned * scale, scale


def local_rows(block, half_blocks, rank):
    count = 2 * half_blocks
    return pl.multiple_of(lax.rem(block + half_blocks * rank, count) * BLOCK, BLOCK)


def attend_kernel(
    info, x_ref, a_ref, b_ref, a_other, b_other, cos_ref, sin_ref, qa_ref, ka_ref,
    w_ref, wo_ref, scale_ref, raw_ref, q_ref, k_ref, v_ref, mix_ref, inv_ref,
    q_aug, k_aug,
):
    blocks = x_ref.shape[0] // BLOCK
    rank = info[blocks]
    part = HEAD_DIM // 2

    def assemble(halves):
        for t, ref in enumerate(halves):
            for head in range(2):
                for m in range(4):
                    source = slice(head * ROWS + m * part, head * ROWS + (m + 1) * part)
                    at = t * HEAD_DIM + head * part
                    if m < 3:
                        w_ref[0, m * PAIR + at : m * PAIR + at + part, :] = ref[source, :]
                    else:
                        wo_ref[at : at + part, :] = ref[source, :]
        rows = [
            halves[0][head * ROWS + 4 * part : (head + 1) * ROWS, :PAIR].astype(f32)[:8] for head in range(2)
        ]
        scales = jnp.where(of_first((8, PAIR), 1), rows[0], pltpu.roll(rows[1], 32, 1))
        scale_ref[0] = scales[:1]

    pl.when(rank == 0)(functools.partial(assemble, (a_ref, a_other)))
    pl.when(rank != 0)(functools.partial(assemble, (b_other, b_ref)))

    first = of_first((BLOCK, PAIR), 1)
    tall = 2 * BLOCK if blocks % 2 == 0 else BLOCK
    first_tall = of_first((tall, PAIR), 1)
    same = same_head()

    def project(t, carry):
        rows = pl.ds(pl.multiple_of(t * tall, tall), tall)
        raw = dot(x_ref[rows, :], w_ref[0], NT)
        raw_ref[rows, :] = raw[:, : 2 * PAIR]
        v_ref[rows, :] = raw[:, 2 * PAIR :].astype(bf16)
        cosine, sine = cos_ref[rows, :], sin_ref[rows, :]
        scale = scale_ref[0]
        q = (turned_unit(raw[:, :PAIR], cosine, sine, same)[0] * scale).astype(bf16)
        k = (turned_unit(raw[:, PAIR : 2 * PAIR], cosine, sine, same)[0] * scale).astype(bf16)
        q_ref[rows, :] = q
        k_ref[rows, :] = k
        q8 = q * jnp.asarray(8.0, bf16)
        qa, ka = qa_ref[rows, :], ka_ref[rows, :]
        q_aug[0, rows, :] = jnp.where(first_tall, q8, qa)
        q_aug[1, rows, :] = jnp.where(first_tall, qa, q8)
        k_aug[0, rows, :] = jnp.where(first_tall, k, ka)
        k_aug[1, rows, :] = jnp.where(first_tall, ka, k)
        return carry

    lax.fori_loop(0, blocks * BLOCK // tall, project, 0)

    row = lax.broadcasted_iota(jnp.int32, (BLOCK, BLOCK), 0)
    col = lax.broadcasted_iota(jnp.int32, (BLOCK, BLOCK), 1)
    causal = col <= row

    def query_block(g, carry):
        q_rows = pl.ds(local_rows(g, blocks // 2, rank), BLOCK)
        count = g - info[g] + 1

        def variant(nk):
            mixed = []
            k_rows = [pl.ds(local_rows(g - (nk - 1) + j, blocks // 2, rank), BLOCK) for j in range(nk)]
            for h in range(2):
                q = q_aug[h, q_rows, :]
                lacc = acc = None
                for j in range(nk):
                    p = jnp.exp(dot(q, k_aug[h, k_rows[j], :], NT))
                    if j == nk - 1:
                        p = jnp.where(causal, p, 0.0)
                    part = p[:, :PAIR] + p[:, PAIR:]
                    lacc = part if lacc is None else lacc + part
                    part = dot(p.astype(bf16), v_ref[k_rows[j], :])
                    acc = part if acc is None else acc + part
                inverse = 1.0 / jnp.sum(lacc, axis=1, keepdims=True)
                inv_ref[0, h : h + 1, q_rows] = 1.0 / jnp.sum(lacc.T, axis=0, keepdims=True)
                mixed.append(acc * inverse)
            mix_ref[q_rows, :] = jnp.where(first, mixed[0], mixed[1]).astype(bf16)

        for nk in range(1, 5):
            pl.when(count == nk if nk < 4 else count >= 4)(functools.partial(variant, nk))
        return carry

    lax.fori_loop(0, blocks, query_block, 0)


def whole(shape):
    return pl.BlockSpec(shape, lambda p: (0,) * len(shape))


def attend_forward(info, x_all, parts, cosine, sine, qa, ka):
    tokens, width = x_all.shape
    pairs = 2
    feats = pairs * PAIR
    by_pair = pl.BlockSpec((tokens, PAIR), lambda p: (0, p))
    return pl.pallas_call(
        attend_kernel,
        grid=(pairs,),
        in_specs=[
            pl.BlockSpec(memory_space=pltpu.SMEM),
            whole((tokens, width)),
        ]
        + [pl.BlockSpec((2 * ROWS, width), lambda p: (p, 0))] * 4
        + [
            whole((tokens, PAIR)),
            whole((tokens, PAIR)),
            whole((tokens, PAIR)),
            whole((tokens, PAIR)),
        ],
        out_specs=[
            pl.BlockSpec((1, 3 * PAIR, width), lambda p: (p, 0, 0)),
            pl.BlockSpec((PAIR, width), lambda p: (p, 0)),
            pl.BlockSpec((1, 1, PAIR), lambda p: (p, 0, 0)),
            pl.BlockSpec((tokens, 2 * PAIR), lambda p: (0, p)),
            by_pair,
            by_pair,
            by_pair,
            by_pair,
            pl.BlockSpec((1, 8, tokens), lambda p: (p, 0, 0)),
        ],
        out_shape=[
            made((pairs, 3 * PAIR, width), bf16),
            made((feats, width), bf16),
            made((pairs, 1, PAIR), f32),
            made((tokens, 2 * feats), f32),
            made((tokens, feats), bf16),
            made((tokens, feats), bf16),
            made((tokens, feats), bf16),
            made((tokens, feats), bf16),
            made((pairs, 8, tokens), f32),
        ],
        scratch_shapes=[
            pltpu.VMEM((2, tokens, PAIR), bf16),
            pltpu.VMEM((2, tokens, PAIR), bf16),
        ],
        compiler_params=ROOM,
        cost_estimate=SMALL,
        name="attend_forward",
    )(info, *far(x_all), *parts, *far(cosine, sine, qa, ka))


def attend_back_kernel(
    info, q_ref, k_ref, v_ref, gb_ref, x_ref, wo_ref, mix_ref, inv_ref, raw_ref, cos_ref, sin_ref, scale_ref,
    qa_ref, ka_ref,
    grad_ref, keep_0, keep_1, send_0, send_1,
    q_aug, k_aug, do_h, q_h, kt_h, delta, dq_acc, dk_acc, dv_acc, dw_acc,
):
    blocks = q_ref.shape[0] // BLOCK
    rank = info[blocks]
    first = of_first((BLOCK, PAIR), 1)
    first_rows = of_first((PAIR, BLOCK), 0)
    zero = jnp.zeros((BLOCK, PAIR), bf16)
    eight = jnp.asarray(8.0, bf16)
    same = same_head()

    def prepare(t, carry):
        start = pl.multiple_of(t * BLOCK, BLOCK)
        rows = pl.ds(start, BLOCK)
        q8 = q_ref[rows, :] * eight
        k = k_ref[rows, :]
        qa, ka = qa_ref[rows, :], ka_ref[rows, :]
        q_aug[0, rows, :] = jnp.where(first, q8, qa)
        q_aug[1, rows, :] = jnp.where(first, qa, q8)
        k_aug[0, rows, :] = jnp.where(first, k, ka)
        k_aug[1, rows, :] = jnp.where(first, ka, k)
        q_h[0, rows, :] = jnp.where(first, q8, zero)
        q_h[1, rows, :] = jnp.where(first, zero, q8)
        k_t = (k * eight).astype(f32).T
        kt_h[0, :, rows] = jnp.where(first_rows, k_t, 0.0).astype(bf16)
        kt_h[1, :, rows] = jnp.where(first_rows, 0.0, k_t).astype(bf16)
        grad = dot(gb_ref[rows, :], wo_ref[...], NT).astype(bf16)
        do_h[0, rows, :] = jnp.where(first, grad, zero)
        do_h[1, rows, :] = jnp.where(first, zero, grad)
        inner = (grad.astype(f32) * mix_ref[rows, :].astype(f32)).T
        inner = inner[:HEAD_DIM] + inner[HEAD_DIM:]
        delta[0:1, rows] = jnp.sum(inner[: HEAD_DIM // 2], axis=0, keepdims=True)
        delta[1:2, rows] = jnp.sum(inner[HEAD_DIM // 2 :], axis=0, keepdims=True)
        dk_acc[rows, :] = jnp.zeros((BLOCK, PAIR), f32)
        dv_acc[rows, :] = jnp.zeros((BLOCK, PAIR), f32)
        return carry

    lax.fori_loop(0, blocks, prepare, 0)

    row = lax.broadcasted_iota(jnp.int32, (BLOCK, BLOCK), 0)
    col = lax.broadcasted_iota(jnp.int32, (BLOCK, BLOCK), 1)
    causal = row <= col

    def query_block(g, carry):
        q_rows = pl.ds(local_rows(g, blocks // 2, rank), BLOCK)
        count = g - info[g] + 1

        def variant(nk):
            dq_t = None
            for j in range(nk):
                k_rows = pl.ds(local_rows(g - (nk - 1) + j, blocks // 2, rank), BLOCK)
                dk = dv = None
                for h in range(2):
                    scores = dot(k_aug[h, k_rows, :], q_aug[h, q_rows, :], NT)
                    p = jnp.exp(scores) * inv_ref[0, h : h + 1, q_rows]
                    if j == nk - 1:
                        p = jnp.where(causal, p, 0.0)
                    dp = dot(v_ref[k_rows, :], do_h[h, q_rows, :], NT)
                    ds = (p * (dp - delta[h : h + 1, q_rows])).astype(bf16)
                    dv_part = dot(p.astype(bf16), do_h[h, q_rows, :])
                    dk_part = dot(ds, q_h[h, q_rows, :])
                    dq_part = dot(kt_h[h, :, k_rows], ds)
                    dv = dv_part if dv is None else dv + dv_part
                    dk = dk_part if dk is None else dk + dk_part
                    dq_t = dq_part if dq_t is None else dq_t + dq_part
                dv_acc[k_rows, :] += dv
                dk_acc[k_rows, :] += dk
            dq_acc[q_rows, :] = dq_t.T

        for nk in range(1, 5):
            pl.when(count == nk if nk < 4 else count >= 4)(functools.partial(variant, nk))
        return carry

    lax.fori_loop(0, blocks, query_block, 0)

    tall = 2 * BLOCK if blocks % 2 == 0 else BLOCK

    def unturn(t, total):
        rows = pl.ds(pl.multiple_of(t * tall, tall), tall)
        cosine, sine = cos_ref[rows, :], sin_ref[rows, :]
        scale = scale_ref[0]
        for which, acc in ((0, dq_acc), (1, dk_acc)):
            raw = raw_ref[rows, which * PAIR : (which + 1) * PAIR]
            unit, size = turned_unit(raw, cosine, sine, same)
            grad = acc[rows, :]
            total = total + jnp.sum((grad * unit).reshape(tall // 8, 8, PAIR), axis=0)
            grad_unit = grad * scale
            grad_turned = size * (grad_unit - unit * head_sums(unit * grad_unit, same))
            grad_raw = grad_turned * cosine - pltpu.roll(grad_turned, HEAD_DIM, 1) * sine
            grad_ref[rows, which * PAIR : (which + 1) * PAIR] = grad_raw.astype(bf16)
        grad_ref[rows, 2 * PAIR :] = dv_acc[rows, :].astype(bf16)
        return total

    total = lax.fori_loop(0, blocks * BLOCK // tall, unturn, jnp.zeros((8, PAIR), f32))
    scale_row = jnp.sum(total, axis=0, keepdims=True)

    dw_acc[...] = jnp.zeros_like(dw_acc)

    def row_grads(t, carry):
        rows = pl.ds(pl.multiple_of(t * tall, tall), tall)
        dw_acc[: 3 * PAIR, :] += dot(grad_ref[rows, :], x_ref[rows, :], TN)
        dw_acc[3 * PAIR :, :] += dot(mix_ref[rows, :], gb_ref[rows, :], TN)
        return carry

    lax.fori_loop(0, blocks * BLOCK // tall, row_grads, 0)
    part = HEAD_DIM // 2

    pair = pl.program_id(0)

    def deal(keep, send):
        for half, out in enumerate((keep, send)):
            for head in range(2):
                base = head * ROWS
                for m in range(4):
                    for t in range(2):

                        @pl.when((rank == t) == (half == 0))
                        def _():
                            at = m * PAIR + t * HEAD_DIM + head * part
                            out[base + m * part : base + (m + 1) * part, :] = dw_acc[at : at + part, :].astype(bf16)

                tail = slice(base + 4 * part, base + ROWS)
                out[tail, :] = jnp.zeros((ROWS - 4 * part, out.shape[1]), bf16)
                if half == 0:
                    row = scale_row if head == 0 else pltpu.roll(jnp.broadcast_to(scale_row, (8, PAIR)), 96, 1)[:1]
                    rows = ROWS - 4 * part
                    top = lax.broadcasted_iota(jnp.int32, (rows, PAIR), 0) == 0
                    out[tail, :PAIR] = jnp.where(top, jnp.broadcast_to(row, (rows, PAIR)), 0.0).astype(bf16)

    pl.when(pair == 0)(functools.partial(deal, keep_0, send_0))
    pl.when(pair == 1)(functools.partial(deal, keep_1, send_1))


def attend_backward(info, q, k, v, grad_branch, x, wo, mixture, inverse, raw, cosine, sine, scale, qa, ka):
    tokens, feats = q.shape
    width = x.shape[1]
    pairs = feats // PAIR
    by_pair = pl.BlockSpec((tokens, PAIR), lambda p: (0, p))
    half = pltpu.VMEM((2, tokens, PAIR), bf16)
    acc = pltpu.VMEM((tokens, PAIR), f32)
    return pl.pallas_call(
        attend_back_kernel,
        grid=(pairs,),
        in_specs=[
            pl.BlockSpec(memory_space=pltpu.SMEM),
            by_pair,
            by_pair,
            by_pair,
            whole((tokens, width)),
            whole((tokens, width)),
            pl.BlockSpec((PAIR, width), lambda p: (p, 0)),
            by_pair,
            pl.BlockSpec((1, 8, tokens), lambda p: (p, 0, 0)),
            pl.BlockSpec((tokens, 2 * PAIR), lambda p: (0, p)),
            whole((tokens, PAIR)),
            whole((tokens, PAIR)),
            pl.BlockSpec((1, 1, PAIR), lambda p: (p, 0, 0)),
            whole((tokens, PAIR)),
            whole((tokens, PAIR)),
        ],
        out_specs=[
            pl.BlockSpec((tokens, 3 * PAIR), lambda p: (0, p)),
        ]
        + [whole((2 * ROWS, width))] * 4,
        out_shape=[made((tokens, 3 * feats), bf16)] + [made((2 * ROWS, width), bf16)] * 4,
        scratch_shapes=[
            half,
            half,
            half,
            half,
            pltpu.VMEM((2, PAIR, tokens), bf16),
            pltpu.VMEM((8, tokens), f32),
            acc,
            acc,
            acc,
            pltpu.VMEM((4 * PAIR, width), f32),
        ],
        compiler_params=ROOM,
        cost_estimate=SMALL,
        name="attend_backward",
    )(info, *far(q, k, v, grad_branch, x, wo, mixture, inverse, raw, cosine, sine), scale, *far(qa, ka))


def slot_scale(ref, group):
    return ref[:, 2 * PAIR : 2 * PAIR + 2 * group].astype(f32)[:1]


def scale_specs(width):
    return [pl.BlockSpec((16, width), lambda t, n=n: ((n * ROWS + 2 * HEAD_DIM) // 16, 0)) for n in range(4)]


def up_gate_kernel(h_ref, *refs):
    *w_refs, s_0, s_1, s_2, s_3, ug_ref, product_ref = refs
    group = product_ref.shape[1] // 4
    per = 4 // len(w_refs)
    for k in range(4):
        pair = slice(2 * k * group, 2 * (k + 1) * group)
        at = 2 * (k % per) * group
        both = dot(h_ref[...], w_refs[k // per][at : at + 2 * group, :], NT)
        ug_ref[:, pair] = both.astype(bf16)
        scaled = both * slot_scale((s_0, s_1, s_2, s_3)[k], group)
        gated = scaled[:, group:]
        product = scaled[:, :group] * gated / (1.0 + jnp.exp(-gated))
        product_ref[:, k * group : (k + 1) * group] = product.astype(bf16)


def tile_of(tokens):
    return 512 if tokens % 512 == 0 else 256


def up_gate(hidden, w, scale):
    tokens, width = hidden.shape
    w = w if isinstance(w, tuple) else (w,)
    units = w[0].shape[0] * len(w) // 2
    tile = tile_of(tokens)
    return pl.pallas_call(
        up_gate_kernel,
        grid=(tokens // tile,),
        in_specs=[
            pl.BlockSpec((tile, width), lambda t: (t, 0)),
        ]
        + [whole(part.shape) for part in w]
        + scale_specs(width),
        out_specs=[
            pl.BlockSpec((tile, 2 * units), lambda t: (t, 0)),
            pl.BlockSpec((tile, units), lambda t: (t, 0)),
        ],
        out_shape=[made((tokens, 2 * units), bf16), made((tokens, units), bf16)],
        compiler_params=ROOM,
        cost_estimate=SMALL,
        name="up_gate",
    )(*far(hidden), *w, *[scale] * 4)


def feed_back_kernel(
    count, grad_ref, h_ref, *rest
):
    w_refs, rest = rest[:count], rest[count:]
    ug_ref, product_ref, s_0, s_1, s_2, s_3, gug_ref, *dws, ug_acc, d_acc, gscale = rest
    group = product_ref.shape[1] // 4
    per_w, per = 4 // count, 4 // len(dws)
    step = pl.program_id(0)

    @pl.when(step == 0)
    def _():
        gscale[...] = jnp.zeros_like(gscale)
        ug_acc[...] = jnp.zeros_like(ug_acc)
        d_acc[...] = jnp.zeros_like(d_acc)

    rows = grad_ref.shape[0] // 8
    d_acc[...] += dot(product_ref[...], grad_ref[...], TN)
    for k in range(4):
        ups = slice(2 * k * group, (2 * k + 1) * group)
        gates = slice((2 * k + 1) * group, (2 * k + 2) * group)
        at = (k % per_w) * group
        grad = dot(grad_ref[...], w_refs[k // per_w][at : at + group, :], NT)
        up = ug_ref[:, ups].astype(f32)
        gate = ug_ref[:, gates].astype(f32)
        scales = slot_scale((s_0, s_1, s_2, s_3)[k], group)
        up_scale, gate_scale = scales[:, :group], scales[:, group:]
        gated = gate * gate_scale
        sig = 1.0 / (1.0 + jnp.exp(-gated))
        silu = gated * sig
        through = grad * silu
        grad_gated = grad * (up * up_scale) * (sig + silu * (1.0 - sig))
        gug_ref[:, ups] = (through * up_scale).astype(bf16)
        gug_ref[:, gates] = (grad_gated * gate_scale).astype(bf16)
        gscale[:, ups] += jnp.sum((through * up).reshape(rows, 8, group), axis=0)
        gscale[:, gates] += jnp.sum((grad_gated * gate).reshape(rows, 8, group), axis=0)
    ug_acc[...] += dot(gug_ref[...], h_ref[...], TN)

    @pl.when(step == pl.num_programs(0) - 1)
    def _():
        top = lax.broadcasted_iota(jnp.int32, (16, 2 * group), 0) == 0
        for k in range(4):
            out, at = dws[k // per], (k % per) * (3 * group + 16)
            out[at : at + 2 * group, :] = ug_acc[2 * k * group : 2 * (k + 1) * group, :].astype(bf16)
            out[at + 2 * group : at + 3 * group, :] = d_acc[k * group : (k + 1) * group, :].astype(bf16)
            sums = jnp.sum(gscale[:, 2 * k * group : 2 * (k + 1) * group], axis=0, keepdims=True)
            tail = slice(at + 3 * group, at + 3 * group + 16)
            out[tail, :] = jnp.zeros((16, out.shape[1]), bf16)
            out[tail, : 2 * group] = jnp.where(top, jnp.broadcast_to(sums, top.shape), 0.0).astype(bf16)


def feed_back(grad, hidden, w, ug, product, scale, pieces=1):
    tokens, width = grad.shape
    w = w if isinstance(w, tuple) else (w,)
    units = product.shape[1]
    tile = tile_of(tokens)
    row = pl.BlockSpec((tile, width), lambda t: (t, 0))
    wide = pl.BlockSpec((tile, 2 * units), lambda t: (t, 0))
    rows = (units * 3 + 64) // pieces
    return pl.pallas_call(
        functools.partial(feed_back_kernel, len(w)),
        grid=(tokens // tile,),
        in_specs=[
            row,
            row,
            *[whole(part.shape) for part in w],
            wide,
            pl.BlockSpec((tile, units), lambda t: (t, 0)),
        ]
        + scale_specs(width),
        out_specs=[wide] + [whole((rows, width))] * pieces,
        out_shape=[made((tokens, 2 * units), bf16)] + [made((rows, width), bf16)] * pieces,
        scratch_shapes=[
            pltpu.VMEM((2 * units, width), f32),
            pltpu.VMEM((units, width), f32),
            pltpu.VMEM((8, 2 * units), f32),
        ],
        compiler_params=ROOM,
        cost_estimate=SMALL,
        name="feed_back",
    )(*far(grad, hidden), *w, *far(ug, product), *[scale] * 4)


def sum_dots_kernel(plan, start, tile, *refs):
    rights = plan[-1][2] + 1
    has = len(refs) - rights - 3 - 2 * len(plan)
    addend = refs[rights] if has else None
    out, acc, *bufs, sems = refs[rights + has :]
    rows = out.shape[0]
    copies = []
    for n, (left, at, right) in enumerate(plan):
        depth = refs[right].shape[0]
        copies.append((
            pltpu.make_async_copy(refs[left].at[pl.ds(start, rows), pl.ds(at, depth)], bufs[2 * n], sems.at[2 * n]),
            pltpu.make_async_copy(refs[right], bufs[2 * n + 1], sems.at[2 * n + 1]),
        ))
    for pair in copies:
        for copy in pair:
            copy.start()
    last = len(plan) - 1
    for n, pair in enumerate(copies):
        for copy in pair:
            copy.wait()
        for r in range(0, rows, tile):
            here = slice(r, r + tile)
            part = dot(bufs[2 * n][here, :], bufs[2 * n + 1][...])
            if n > 0:
                part = part + acc[here, :]
            elif addend is not None:
                part = part + addend[here, :].astype(f32)
            if n < last:
                acc[here, :] = part
            else:
                out[here, :] = part.astype(out.dtype)


def sum_dots(lefts, rights, start, rows, dtype, addend=None):
    plan, parts = [], []
    for c, right in enumerate(rights):
        at = 0
        for part in right if isinstance(right, tuple) else (right,):
            plan.append((c, at, len(lefts) + len(parts)))
            parts.append(part)
            at += part.shape[0]
    width = parts[0].shape[1]
    bufs = [pltpu.VMEM(shape, bf16) for part in parts for shape in ((rows, part.shape[0]), part.shape)]
    more = [] if addend is None else [addend]
    far_ref = pl.BlockSpec(memory_space=pltpu.HBM)
    near = pl.BlockSpec(memory_space=pltpu.VMEM)
    return pl.pallas_call(
        functools.partial(sum_dots_kernel, plan, start, 256),
        in_specs=[far_ref] * (len(lefts) + len(parts)) + [near] * len(more),
        out_specs=near,
        out_shape=made((rows, width), dtype),
        scratch_shapes=[pltpu.VMEM((rows, width), f32), *bufs, pltpu.SemaphoreType.DMA((2 * len(plan),))],
        compiler_params=ROOM,
        cost_estimate=SMALL,
        name="sum_dots",
    )(*lefts, *parts, *more)


def alpha_kernel(place, *refs):
    slots, one, two, rows = refs[:HEADS], refs[HEADS], refs[HEADS + 1], refs[HEADS + 2]
    for j in range(HEADS):
        rows[j : j + 1, :] = slots[j][:, PAIR : 2 * PAIR].astype(f32)[:1]
    low = lax.broadcasted_iota(jnp.int32, (1, PAIR), 1) < HEAD_DIM
    for k in range(HEADS // 2):
        pair = []
        for owner in (2 * k, 2 * k + 1):
            slot = slot_of(jnp.bitwise_xor(place[0], owner))
            pair.append(jnp.broadcast_to(rows[pl.ds(slot, 1), :], (8, PAIR)))
        turned = [pltpu.roll(p, HEAD_DIM, 1)[:1] for p in pair]
        lanes = slice(k * PAIR, (k + 1) * PAIR)
        one[:, lanes] = jnp.where(low, pair[0][:1], turned[1])
        two[:, lanes] = jnp.where(low, turned[0], pair[1][:1])


def alpha_rows(place, chunks):
    width = chunks[0].shape[1]
    specs = scale_specs(width)
    return pl.pallas_call(
        alpha_kernel,
        grid=(1,),
        in_specs=[pl.BlockSpec(memory_space=pltpu.SMEM)] + specs * 4,
        out_specs=[whole((1, width))] * 2,
        out_shape=[made((1, width), f32)] * 2,
        scratch_shapes=[pltpu.VMEM((HEADS, PAIR), f32)],
        compiler_params=ROOM,
        cost_estimate=SMALL,
        name="alpha",
    )(place[None].astype(jnp.int32), *(chunk for chunk in chunks for _ in range(4)))


def rms_scale(values):
    return lax.rsqrt(jnp.mean(values * values, axis=-1, keepdims=True) + norm_eps)


def blend_parts(residual, branch, mixing):
    branch_scale = rms_scale(branch)
    unit = branch * branch_scale
    step = unit - residual
    mixed = residual + mixing * step
    mixed_scale = rms_scale(mixed)
    return branch_scale, unit, step, mixed * mixed_scale, mixed_scale


def blend_grads(parts, mixing, grad):
    branch_scale, unit, step, result, mixed_scale = parts
    grad_mixed = mixed_scale * (grad - result * jnp.mean(grad * result, axis=-1, keepdims=True))
    grad_unit = mixing * grad_mixed
    grad_branch = branch_scale * (grad_unit - unit * jnp.mean(unit * grad_unit, axis=-1, keepdims=True))
    return grad_mixed - grad_unit, grad_branch, grad_mixed * step


def add_rows(ref, values):
    @pl.when(pl.program_id(0) == 0)
    def _():
        ref[...] = jnp.zeros_like(ref)

    ref[...] += jnp.sum(values.reshape(values.shape[0] // 8, 8, values.shape[1]), axis=0)


def hidden_kernel(x_ref, own_ref, other_ref, mix_ref, hidden_ref, round_ref, wide_ref):
    branch = own_ref[...] + other_ref[...].astype(f32)
    hidden = blend_parts(x_ref[...].astype(f32), branch, mix_ref[...])[3]
    hidden_ref[...] = hidden
    round_ref[...] = wide_ref[...] = hidden.astype(bf16)


def output_kernel(
    hidden_ref, own_ref, other_ref, mix_ref, cot_ref, out_ref, res_ref, down_ref, wide_ref, gmix_ref
):
    mixing = mix_ref[...]
    parts = blend_parts(hidden_ref[...], own_ref[...] + other_ref[...].astype(f32), mixing)
    out_ref[...] = parts[3]
    grad_res, grad_down, grad_mix = blend_grads(parts, mixing, cot_ref[...].astype(f32))
    res_ref[...] = grad_res
    down_ref[...] = wide_ref[...] = grad_down.astype(bf16)
    add_rows(gmix_ref, grad_mix)


def hidden_back_kernel(
    x_ref, own_ref, other_ref, mix_ref, res_ref, back_ref, from_ref, in_ref, branch_ref, wide_ref, gmix_ref
):
    mixing = mix_ref[...]
    parts = blend_parts(x_ref[...].astype(f32), own_ref[...] + other_ref[...].astype(f32), mixing)
    grad = res_ref[...] + back_ref[...] + from_ref[...].astype(f32)
    grad_res, grad_branch, grad_mix = blend_grads(parts, mixing, grad)
    in_ref[...] = grad_res
    branch_ref[...] = wide_ref[...] = grad_branch.astype(bf16)
    add_rows(gmix_ref, grad_mix)


def rowwise(kernel, name, arrays, floats, reduced=False):
    tokens, width = arrays[0].shape
    tile = 128
    row = pl.BlockSpec((tile, width), lambda t: (t, 0))
    out_shape = [made((tokens, width), f32)] * floats
    out_shape += [made((tokens, width), bf16), made((2 * tokens, width), bf16)]
    out_specs = [row] * (floats + 2)
    if reduced:
        out_shape.append(made((8, width), f32))
        out_specs.append(whole((8, width)))
    return pl.pallas_call(
        kernel,
        grid=(tokens // tile,),
        in_specs=[row if a.shape[0] == tokens else whole((1, width)) for a in arrays],
        out_specs=out_specs,
        out_shape=out_shape,
        compiler_params=ROOM,
        cost_estimate=SMALL,
        name=name,
    )(*(far(a)[0] if a.dtype == f32 and a.shape[0] == tokens else a for a in arrays))


def adam_change(weight, gradient, moment_one, moment_two, renormalize):
    moment_one_new = beta_one * moment_one + (1.0 - beta_one) * gradient
    moment_two_new = beta_two * moment_two + (1.0 - beta_two) * gradient * gradient
    stepped = weight - learn_rate * (moment_one_new / corr_one) / (
        jnp.sqrt(moment_two_new / corr_two) + adam_eps
    )
    if renormalize:
        stepped = stepped * lax.rsqrt(jnp.sum(stepped * stepped, axis=-1, keepdims=True) + norm_eps)
    return stepped - weight


def adam_kernel(w_ref, g_ref, one_ref, two_ref, out_ref):
    out_ref[...] = adam_change(w_ref[...], g_ref[...], one_ref[...], two_ref[...], True)


def adam_rows(weight, gradient, moment_one, moment_two):
    shape = weight.shape
    rows, width = shape[0] * shape[1], shape[2]
    tile = next(t for t in (128, 64, 32, 16, 8) if rows % t == 0)
    block = pl.BlockSpec((tile, width), lambda t: (t, 0))
    return pl.pallas_call(
        adam_kernel,
        grid=(rows // tile,),
        in_specs=[block] * 4,
        out_specs=block,
        out_shape=made((rows, width), f32),
        compiler_params=ROOM,
        cost_estimate=SMALL,
        name="adam",
    )(*far(*(a.reshape(rows, width) for a in (weight, gradient, moment_one, moment_two)))).reshape(shape)


def own_half(x, rank, axis):
    size = x.shape[axis] // 2
    return lax.dynamic_slice_in_dim(x, rank * size, size, axis)


def pick(rank, zero, one):
    return jnp.where(rank == 0, zero, one)


def document_tables(segment_ids, rank, count):
    segments = segment_ids.reshape(-1)
    docs = jnp.arange(8, dtype=jnp.int32)
    begins = jnp.sum((segments[None, :] < docs[:, None]).astype(jnp.int32), axis=1)
    is_doc = segments[:, None] == docs[None, :]
    starts = jnp.sum(jnp.where(is_doc, begins[None, :], 0), axis=1)
    info = jnp.concatenate([starts[::BLOCK] // BLOCK, rank[None].astype(jnp.int32)])
    place = jnp.arange(2 * count, dtype=jnp.int32)

    def arranged(values):
        own = lax.dynamic_slice_in_dim(values, rank * count, count, 0)
        other = lax.dynamic_slice_in_dim(values, (1 - rank) * count, count, 0)
        return jnp.concatenate([own, other], 0)

    positions = arranged(place - starts).astype(f32)
    frequency = jnp.exp(
        jnp.arange(HEAD_DIM // 2, dtype=f32) * (-2.0 * math.log(rope_base) / HEAD_DIM)
    )
    angles = positions[:, None] * jnp.tile(frequency, 4)[None, :]
    cosine = jnp.cos(angles)
    sign = jnp.where(jnp.arange(PAIR) < HEAD_DIM, -1.0, 1.0).astype(f32)
    sine = jnp.sin(angles) * sign[None, :]
    lanes = jnp.arange(PAIR, dtype=jnp.int32)
    lanes = jnp.where(lanes < HEAD_DIM, lanes & 31, 8)
    own_doc = arranged(segments)[:, None] == lanes[None, :]
    query_mark = own_doc.astype(bf16)
    key_mark = jnp.where(own_doc | (lanes >= 8)[None, :], 0.0, -apart).astype(bf16)
    return info, cosine, sine, query_mark, key_mark


def scale_row(qk, alpha, feed, width):
    count = qk.shape[0]
    gap = jnp.zeros((count, HEAD_DIM // 2), f32)
    row = [qk[:, : HEAD_DIM // 2], gap, qk[:, HEAD_DIM // 2 :], gap]
    row += [jnp.broadcast_to(alpha.reshape(1, -1), (count, PAIR)), feed.reshape(count, -1)]
    row = jnp.concatenate(row, 1).astype(bf16)
    return jnp.pad(row[:, None], ((0, 0), (0, 15), (0, width - row.shape[1])))


class Group:
    def __init__(self, tables, x_all, parts):
        self.tables = tables
        info, cosine, sine, query_mark, key_mark = tables
        (self.w, self.wo, self.scale, self.raw, self.q, self.k, self.v, self.mixture, self.inverse) = attend_forward(
            info, x_all, parts, cosine, sine, query_mark, key_mark
        )

    def back(self, grad_branch, x_all):
        info, cosine, sine, query_mark, key_mark = self.tables
        grad_qkv, *rows = attend_backward(
            info, self.q, self.k, self.v, grad_branch, x_all, self.wo, self.mixture, self.inverse, self.raw,
            cosine, sine, self.scale, query_mark, key_mark,
        )
        return grad_qkv, tuple(rows[:2]), tuple(rows[2:])


def local_sixteen(
    tokens,
    segment_ids,
    cotangent,
    attention_weights,
    feed_weights,
    attention_scales,
    feed_scales,
    attention_first,
    attention_second,
    feed_first,
    feed_second,
    attention_scale_first,
    attention_scale_second,
    feed_scale_first,
    feed_scale_second,
):
    count, width = tokens.shape[0] * tokens.shape[1], tokens.shape[-1]
    rank, place = lax.axis_index("seq"), lax.axis_index("dp")
    x = tokens.reshape(count, width)

    part = own_half(attention_weights, rank, 1).astype(bf16)
    rows = part.shape[1]
    body = 4 * rows
    extra = scale_row(attention_scales[0:1], attention_scales[1:], own_half(feed_scales, rank, 1)[None], width)
    block_a = jnp.concatenate([part.reshape(body, width), extra[0]], axis=0)
    feed_part = own_half(feed_weights, rank, 1).astype(bf16)
    units = feed_part.shape[1]
    block_u = feed_part[:2].reshape(2 * units, width)
    block_d = feed_part[2]

    z_a = [via(block_a, 4 * k) for k in (1, 2, 3)]
    x_all = jnp.concatenate([x, swap(x)], 0)
    tables = document_tables(segment_ids, rank, count)
    block_a, z_a, block_u, block_d, x_all, tables = tie(block_a, z_a, block_u, block_d, x_all, tables)

    own_a = join(block_a, *z_a)
    x_a, y_a = via(own_a, 1), via(own_a, 2)
    z_u = [via(block_u, 4), via(block_u, 8)]
    own_a, x_a, y_a, z_u, block_u, x_all = tie(own_a, x_a, y_a, z_u, block_u, x_all)

    d_a = diagonal_in(x_a, y_a)
    z_u = z_u + [via(block_u, 12)]
    group_0 = Group(tables, x_all, (own_a, y_a, swap(own_a), swap(y_a)))
    d_a, z_u, block_u, block_d, group_0.mixture, x_all = tie(d_a, z_u, block_u, block_d, group_0.mixture, x_all)

    own_u = join(block_u, *z_u)
    x_u, y_u = via(own_u, 1), via(own_u, 2)
    z_d = [via(block_d, 4), via(block_d, 8)]
    d_a = join(*d_a)
    group_1 = Group(tables, x_all, (x_a, d_a, swap(x_a), swap(d_a)))
    groups = (group_0, group_1)
    mixtures, wos = [g.mixture for g in groups], [g.wo for g in groups]
    branch_other = sum_dots(mixtures, wos, count, count, bf16)
    branch_own = sum_dots(mixtures, wos, 0, count, f32)
    branch_other, branch_own, x_u, y_u, z_d, d_a = tie(branch_other, branch_own, x_u, y_u, z_d, d_a)

    d_u = diagonal_in(x_u, y_u)
    z_d = z_d + [via(block_d, 12)]
    alpha = alpha_rows(place, (own_a, x_a, y_a, d_a))
    branch_from = swap(branch_other)
    hidden, hidden_round, hidden_all = rowwise(
        hidden_kernel, "hidden", [x, branch_own, branch_from, alpha[0]], 1
    )
    d_u, z_d, hidden_round = tie(d_u, z_d, hidden_round)
    own_d = join(block_d, *z_d)
    x_d, y_d = via(own_d, 1), via(own_d, 2)
    hidden_all = fill(hidden_all, swap(hidden_round))
    ug_own, product_own = up_gate(hidden_all, own_u, own_a)
    ug_x, product_x = up_gate(hidden_all, x_u, x_a)
    ug_y, product_y = up_gate(hidden_all, y_u, y_a)
    product_own, product_x, product_y, hidden_all, d_u, x_d, y_d = tie(
        product_own, product_x, product_y, hidden_all, d_u, x_d, y_d
    )

    d_d = diagonal_in(x_d, y_d)
    ug_d, product_d = up_gate(hidden_all, d_u, d_a)
    products = [product_own, product_x, product_y]
    w_ds = [own_d, x_d, y_d]
    down_other = sum_dots(products, w_ds, count, count, f32)
    down_own = sum_dots(products, w_ds, 0, count, f32)
    down_other, down_own, d_d, product_d = tie(down_other, down_own, d_d, product_d)

    down_other = sum_dots([product_d], [d_d], count, count, bf16, down_other)
    down_own = sum_dots([product_d], [d_d], 0, count, f32, down_own)
    output, grad_hidden_res, grad_down_round, grad_down, grad_alpha_feed = rowwise(
        output_kernel,
        "output",
        [hidden, down_own, swap(down_other), alpha[1], cotangent.reshape(count, width)],
        2,
        True,
    )

    grad_down = fill(grad_down, swap(grad_down_round))
    gug_d, *r_d = feed_back(grad_down, hidden_all, d_d, ug_d, product_d, d_a, 2)
    r_d, grad_down, product_x, product_y, product_own = tie(r_d, grad_down, product_x, product_y, product_own)
    t_d = via(r_d[0], 1), via(r_d[1], 2)
    gug_x, r_x = feed_back(grad_down, hidden_all, x_d, ug_x, product_x, x_a)
    gug_y, r_y = feed_back(grad_down, hidden_all, y_d, ug_y, product_y, y_a)
    gug_own, r_own = feed_back(grad_down, hidden_all, own_d, ug_own, product_own, own_a)
    gugs, w_ugs = [gug_own, gug_x, gug_y, gug_d], [own_u, x_u, y_u, d_u]
    t_d, r_x, r_y, r_own, gugs = tie(t_d, r_x, r_y, r_own, gugs)

    r_x, r_y = add_half(r_x, t_d[1], True), add_half(r_y, t_d[0], False)
    r_x, r_y, gugs = tie(r_x, r_y, gugs)
    v_x, v_y = via(r_x, 1), via(r_y, 2)
    back_other = sum_dots(gugs, w_ugs, count, count, bf16)
    back_from = swap(back_other)
    back_own = sum_dots(gugs, w_ugs, 0, count, f32)
    grad_input_res, grad_branch_round, grad_branch_all, grad_alpha_attend = rowwise(
        hidden_back_kernel,
        "hidden_back",
        [x, branch_own, branch_from, alpha[0], grad_hidden_res, back_own, back_from],
        1,
        True,
    )
    grad_branch_all = fill(grad_branch_all, swap(grad_branch_round))
    grad_qkv_1, keep_1, send_1 = group_1.back(grad_branch_all, x_all)
    v_x, v_y, grad_qkv_1, keep_1, send_1, grad_branch_all = tie(
        v_x, v_y, grad_qkv_1, keep_1, send_1, grad_branch_all
    )

    grad_alpha = jnp.stack([jnp.sum(grad_alpha_attend, 0), jnp.sum(grad_alpha_feed, 0)])
    alpha_from = via(grad_alpha, 1)
    feed_mine, feed_parts = column_sum(r_own, v_x, v_y)
    feed_mine, feed_parts, send_1, grad_alpha, alpha_from = tie(feed_mine, feed_parts, send_1, grad_alpha, alpha_from)
    grad_alpha = grad_alpha + alpha_from
    z_feed = [via(feed_parts[0], 4), via(feed_parts[1], 8)]
    other_1 = swap(send_1[0]), swap(send_1[1])
    a_x = jnp.concatenate([pick(rank, k, o) for k, o in zip(keep_1, other_1)], 0)
    a_d = tuple(pick(rank, o, k) for k, o in zip(keep_1, other_1))
    a_x, a_d, grad_branch_all = tie(a_x, a_d, grad_branch_all)

    t_a = via(a_d[0], 1), via(a_d[1], 2)
    alpha_from = via(grad_alpha, 2)
    grad_qkv_0, keep_0, send_0 = group_0.back(grad_branch_all, x_all)
    t_a, z_feed, alpha_from, grad_qkv_0, keep_0, send_0 = tie(t_a, z_feed, alpha_from, grad_qkv_0, keep_0, send_0)

    z_feed = z_feed + [via(feed_parts[2], 12)]
    grad_alpha = grad_alpha + alpha_from
    other_0 = swap(send_0[0]), swap(send_0[1])
    a_own = jnp.concatenate([pick(rank, k, o) for k, o in zip(keep_0, other_0)], 0)
    a_y = [pick(rank, o, k) for k, o in zip(keep_0, other_0)]
    a_y = jnp.concatenate([plus(a_y[0], t_a[0]), a_y[1]], 0)
    a_x = add_half(a_x, t_a[1], True)
    a_x, a_y, grad_qkv_0, grad_alpha = tie(a_x, a_y, grad_qkv_0, grad_alpha)
    b_x, b_y = via(a_x, 1), via(a_y, 2)
    alpha_from = via(grad_alpha, 4)
    grad_qkvs = [grad_qkv_0, grad_qkv_1]
    w_flats = [g.w.reshape(-1, width) for g in groups]
    input_other = sum_dots(grad_qkvs, w_flats, count, count, bf16)
    input_own = sum_dots(grad_qkvs, w_flats, 0, count, f32, grad_input_res)
    input_other, input_own, b_x, b_y, z_feed, alpha_from = tie(input_other, input_own, b_x, b_y, z_feed, alpha_from)
    grad_alpha = grad_alpha + alpha_from
    alpha_from = via(grad_alpha, 8)

    attend_mine, attend_parts = column_sum(a_own, b_x, b_y)
    attend_parts = [via(part, 4 * k) for part, k in zip(attend_parts, (1, 2, 3))]
    input_grad = input_own + swap(input_other).astype(f32)
    total = z_sum(feed_mine, z_feed)
    other = swap(total)
    low, high = pick(rank, total, other), pick(rank, other, total)
    feed_grad = jnp.concatenate([t[: 3 * units].reshape(3, units, width) for t in (low, high)], 1)
    feed_grad_s = jnp.concatenate([t[3 * units, : 2 * units].reshape(2, units) for t in (low, high)], 1)
    feed_change = adam_rows(feed_weights, feed_grad, feed_first, feed_second)
    attend_parts, alpha_from, input_grad, feed_grad, feed_change = tie(
        attend_parts, alpha_from, input_grad, feed_grad, feed_change
    )
    grad_alpha = grad_alpha + alpha_from
    grad_alpha = grad_alpha + swap(grad_alpha)
    own_alpha = lax.dynamic_slice_in_dim(grad_alpha, place * HEAD_DIM, HEAD_DIM, 1)

    total = z_sum(attend_mine, attend_parts)
    other = swap(total)
    low, high = pick(rank, total, other), pick(rank, other, total)
    attend_grad = jnp.concatenate([t[:body].reshape(4, rows, width) for t in (low, high)], 1)
    grad_qk = low[body] + high[body]
    grad_qk = jnp.concatenate([grad_qk[: HEAD_DIM // 2], grad_qk[HEAD_DIM : 3 * HEAD_DIM // 2]], 0)
    attend_grad_s = jnp.concatenate([grad_qk[None], own_alpha], 0)
    return (
        output.reshape(tokens.shape),
        input_grad.reshape(tokens.shape),
        attend_grad,
        feed_grad,
        attend_grad_s,
        feed_grad_s,
        adam_rows(attention_weights, attend_grad, attention_first, attention_second),
        feed_change,
        adam_change(attention_scales, attend_grad_s, attention_scale_first, attention_scale_second, False),
        adam_change(feed_scales, feed_grad_s, feed_scale_first, feed_scale_second, False),
    )


def local_any(
    tokens,
    segment_ids,
    cotangent,
    attention_weights,
    feed_weights,
    attention_scales,
    feed_scales,
    attention_first,
    attention_second,
    feed_first,
    feed_second,
    attention_scale_first,
    attention_scale_second,
    feed_scale_first,
    feed_scale_second,
):
    count, width = tokens.shape[0] * tokens.shape[1], tokens.shape[-1]
    rank = lax.axis_index("seq")
    x = tokens.reshape(count, width)
    x_all = jnp.concatenate([x, swap(x)], axis=0)
    tables = document_tables(segment_ids, rank, count)

    full = lax.all_gather(attention_weights.astype(bf16), "dp", axis=1, tiled=True)
    scales = lax.all_gather(attention_scales.astype(bf16), "dp", axis=1, tiled=True).astype(f32)
    half = width // 2
    alpha = scales[1:]
    mine = lax.dynamic_slice_in_dim(full, rank * half, half, 1)
    mine = jnp.swapaxes(mine.reshape(4, HEADS // 2, 2, HEAD_DIM // 2, width), 0, 1)
    own_scale = lax.dynamic_slice_in_dim(scales[0], rank * half, half, 0).reshape(HEADS // 2, HEAD_DIM)

    groups = []
    for g in range(2):
        heads = slice(4 * g, 4 * g + 4)
        tail = scale_row(own_scale[heads], jnp.zeros((2, HEAD_DIM)), jnp.zeros((4, 2 * PAIR)), width)
        low = jnp.concatenate([mine[heads, :, 0].reshape(4, -1, width), tail], 1).reshape(-1, width)
        high = jnp.concatenate([mine[heads, :, 1].reshape(4, -1, width), tail], 1).reshape(-1, width)
        groups.append(Group(tables, x_all, (low, high, high, low)))

    feed = lax.all_gather(own_half(feed_weights, rank, 1).astype(bf16), "dp", axis=1, tiled=True)
    feed_s = lax.all_gather(own_half(feed_scales, rank, 1).astype(bf16), "dp", axis=1, tiled=True).astype(f32)
    units = feed.shape[1] // 4
    w_ugs, w_ds, feed_scale = [], [], []
    for c in range(4):
        piece = feed[:2, c * units : (c + 1) * units].reshape(2, 4, units // 4, width)
        piece = jnp.swapaxes(piece, 0, 1).reshape(2 * units, width)
        w_ugs.append(piece)
        w_ds.append(feed[2, c * units : (c + 1) * units])
        piece = feed_s[:, c * units : (c + 1) * units].reshape(2, 4, units // 4)
        piece = jnp.swapaxes(piece, 0, 1).reshape(4, units // 2)
        tail = scale_row(jnp.zeros((4, HEAD_DIM)), jnp.zeros((2, HEAD_DIM)), piece, width)
        tail = jnp.concatenate([jnp.zeros((4, 2 * HEAD_DIM, width), bf16), tail], 1)
        feed_scale.append(tail.reshape(-1, width))

    mixtures, wos = [g.mixture for g in groups], [g.wo for g in groups]
    branch_other = sum_dots(mixtures, wos, count, count, bf16)
    branch_own, branch_from = sum_dots(mixtures, wos, 0, count, f32), swap(branch_other)
    hidden, hidden_round, hidden_all = rowwise(
        hidden_kernel, "hidden", [x, branch_own, branch_from, alpha[:1]], 1
    )
    hidden_all = fill(hidden_all, swap(hidden_round))
    ugs, products = zip(*[up_gate(hidden_all, w, s) for w, s in zip(w_ugs, feed_scale)])
    down_other = sum_dots(products, w_ds, count, count, bf16)
    down_own = sum_dots(products, w_ds, 0, count, f32)
    output, grad_hidden_res, grad_down_round, grad_down, grad_alpha_feed = rowwise(
        output_kernel,
        "output",
        [hidden, down_own, swap(down_other), alpha[1:], cotangent.reshape(count, width)],
        2,
        True,
    )
    grad_down = fill(grad_down, swap(grad_down_round))
    gugs, chunks = zip(
        *[
            feed_back(grad_down, hidden_all, w, ug, product, s)
            for w, ug, product, s in zip(w_ds, ugs, products, feed_scale)
        ]
    )
    back_other = sum_dots(gugs, w_ugs, count, count, bf16)
    back_own = sum_dots(gugs, w_ugs, 0, count, f32)
    grad_input_res, grad_branch_round, grad_branch_all, grad_alpha_attend = rowwise(
        hidden_back_kernel,
        "hidden_back",
        [x, branch_own, branch_from, alpha[:1], grad_hidden_res, back_own, swap(back_other)],
        1,
        True,
    )
    grad_branch_all = fill(grad_branch_all, swap(grad_branch_round))

    terms, term_scales = [], []
    for chunk in chunks:
        chunk = chunk.reshape(4, -1, width)
        body = chunk[:, : 3 * units // 4].reshape(4, 3, units // 4, width)
        terms.append(jnp.swapaxes(body, 0, 1).reshape(3, units, width))
        piece = chunk[:, 3 * units // 4, : units // 2].astype(f32).reshape(4, 2, units // 4)
        term_scales.append(jnp.swapaxes(piece, 0, 1).reshape(2, units))

    def scattered(values):
        return lax.psum_scatter(values, "dp", scatter_dimension=1, tiled=True)

    def both_halves(total):
        other = swap(total)
        return jnp.concatenate([pick(rank, total, other), pick(rank, other, total)], 1)

    feed_grad = both_halves(scattered(jnp.concatenate(terms, 1)).astype(f32))
    feed_grad_s = both_halves(scattered(jnp.concatenate(term_scales, 1)))

    grad_qkvs, gscales, pieces = [], [], []
    for group in groups:
        grad_qkv, keep, send = group.back(grad_branch_all, x_all)
        keep, send = jnp.concatenate(keep, 0), jnp.concatenate(send, 0)
        halves = jnp.stack([pick(rank, keep, send), pick(rank, send, keep)]).reshape(2, 4, ROWS, width)
        scale = jnp.sum(halves[:, :, 2 * HEAD_DIM].astype(f32), 0)
        scale = jnp.concatenate([scale[:, : HEAD_DIM // 2], scale[:, HEAD_DIM : 3 * HEAD_DIM // 2]], 1)
        halves = halves[:, :, : 2 * HEAD_DIM].reshape(2, 4, 4, HEAD_DIM // 2, width)
        pieces.append(jnp.transpose(halves, (2, 1, 0, 3, 4)).reshape(4, 4 * HEAD_DIM, width))
        grad_qkvs.append(grad_qkv)
        gscales.append(scale.reshape(1, -1))
    w_flats = [g.w.reshape(-1, width) for g in groups]
    input_other = sum_dots(grad_qkvs, w_flats, count, count, bf16)
    input_own = sum_dots(grad_qkvs, w_flats, 0, count, f32)
    input_grad = grad_input_res + input_own + swap(input_other).astype(f32)

    total = jnp.zeros((4, width, width), bf16)
    total = scattered(lax.dynamic_update_slice(total, jnp.concatenate(pieces, 1), (0, rank * half, 0)))
    attend_grad = total.astype(f32) + swap(total.astype(f32))
    qk = jnp.zeros((1, width), f32)
    qk = lax.dynamic_update_slice(qk, jnp.concatenate(gscales, 1), (0, rank * half))
    total = jnp.concatenate(
        [qk, jnp.sum(grad_alpha_attend, 0)[None], jnp.sum(grad_alpha_feed, 0)[None]], 0
    )
    total = scattered(total)
    attend_grad_s = total + swap(total)
    return (
        output.reshape(tokens.shape),
        input_grad.reshape(tokens.shape),
        attend_grad,
        feed_grad,
        attend_grad_s,
        feed_grad_s,
        adam_rows(attention_weights, attend_grad, attention_first, attention_second),
        adam_rows(feed_weights, feed_grad, feed_first, feed_second),
        adam_change(attention_scales, attend_grad_s, attention_scale_first, attention_scale_second, False),
        adam_change(feed_scales, feed_grad_s, feed_scale_first, feed_scale_second, False),
    )


def solution(mesh):
    rows = P("dp", "seq", None)
    matrix = P(None, "dp", None)
    scale = P(None, "dp")
    return jax.shard_map(
        local_sixteen if mesh.shape["dp"] == HEADS else local_any,
        mesh=mesh,
        in_specs=(rows, P("dp", None), rows, matrix, matrix, scale, scale)
        + (matrix,) * 4
        + (scale,) * 4,
        out_specs=(rows, rows, matrix, matrix, scale, scale, matrix, matrix, scale, scale),
        check_vma=False,
    )
```

```python
import functools
import math

import jax
import jax.numpy as jnp
from jax import lax
from jax.experimental import pallas as pl
from jax.experimental.pallas import tpu as pltpu
from jax.sharding import PartitionSpec as P

HEADS = 16
HEAD_DIM = 64
PAIR = 2 * HEAD_DIM
BLOCK = 256
ROWS = 4 * (HEAD_DIM // 2) + 16

norm_eps = 1e-06
rope_base = 10000.0
learn_rate = 0.003
beta_one = 0.9
beta_two = 0.95
adam_eps = 1e-08
corr_one = 1.0 - 0.9**10
corr_two = 1.0 - 0.95**10
apart = 1024.0

bf16 = jnp.bfloat16
f32 = jnp.float32
NT = (((1,), (1,)), ((), ()))
NN = (((1,), (0,)), ((), ()))
TN = (((0,), (0,)), ((), ()))
MIB = 1024 * 1024
SMALL = pl.CostEstimate(flops=1, bytes_accessed=1, transcendentals=0)
ROOM = pltpu.CompilerParams(vmem_limit_bytes=40 * MIB)


def made(shape, dtype):
    return pltpu.HBM(shape, dtype)


def far(*arrays):
    return [pltpu.with_memory_space_constraint(a, pltpu.HBM) for a in arrays]


def dot(a, b, dims=NN, precision=None):
    return lax.dot_general(a, b, dims, precision=precision, preferred_element_type=f32)


def tie(*values):
    return lax.optimization_barrier(values)


def swap(x):
    return lax.ppermute(x, "seq", [(0, 1), (1, 0)])


def via(x, bits):
    count = lax.axis_size("dp")
    return lax.ppermute(x, "dp", [(i, i ^ bits) for i in range(count)])


def upper_half(x):
    return x[: x.shape[0] // 2]


def lower_half(x):
    return x[x.shape[0] // 2 :]


def join_kernel(steps, *refs):
    for k in range(len(refs) - 1):

        @pl.when(pl.program_id(0) // steps == k)
        def _():
            refs[-1][...] = refs[k][...]


def join(*parts):
    rows, width = parts[0].shape
    steps = max(1, rows // 256)
    tile = rows // steps

    def spec(k):
        return pl.BlockSpec((tile, width), lambda t: (jnp.clip(t - k * steps, 0, steps - 1), 0))

    return pl.pallas_call(
        functools.partial(join_kernel, steps),
        grid=(len(parts) * steps,),
        in_specs=[spec(k) for k in range(len(parts))],
        out_specs=pl.BlockSpec((tile, width), lambda t: (t, 0)),
        out_shape=made((len(parts) * rows, width), parts[0].dtype),
        compiler_params=ROOM,
        cost_estimate=SMALL,
        name="join",
    )(*parts)


def fill_kernel(whole_ref, part_ref, out_ref):
    out_ref[...] = part_ref[...]


def fill(target, part):
    rows, width = part.shape
    tile = rows // 2
    return pl.pallas_call(
        fill_kernel,
        grid=(2,),
        in_specs=[pl.BlockSpec(memory_space=pl.ANY), pl.BlockSpec((tile, width), lambda t: (t, 0))],
        out_specs=pl.BlockSpec((tile, width), lambda t: (t + 2, 0)),
        out_shape=made(target.shape, target.dtype),
        input_output_aliases={0: 0},
        compiler_params=ROOM,
        cost_estimate=SMALL,
        name="fill",
    )(target, part)


def half_kernel(x_ref, out_ref):
    out_ref[...] = x_ref[...]


def half_of(x, lower):
    rows, width = x.shape[0] // 4, x.shape[1]
    at = 2 if lower else 0
    return pl.pallas_call(
        half_kernel,
        grid=(2,),
        in_specs=[pl.BlockSpec((rows, width), lambda t: (t + at, 0))],
        out_specs=pl.BlockSpec((rows, width), lambda t: (t, 0)),
        out_shape=made((2 * rows, width), x.dtype),
        compiler_params=ROOM,
        cost_estimate=SMALL,
        name="half",
    )(x)


def diagonal_in(by_x, by_y):
    return via(half_of(by_y, False), 1), via(half_of(by_x, True), 2)


def plus(a, b):
    return (a.astype(f32) + b.astype(f32)).astype(bf16)


def add_half_kernel(a_ref, b_ref, o_ref):
    o_ref[...] = plus(a_ref[...], b_ref[...])


def add_half(x, part, lower):
    rows, width = part.shape
    tile = rows // 2
    at = 2 if lower else 0
    return pl.pallas_call(
        add_half_kernel,
        grid=(2,),
        in_specs=[
            pl.BlockSpec((tile, width), lambda t: (t + at, 0)),
            pl.BlockSpec((tile, width), lambda t: (t, 0)),
        ],
        out_specs=pl.BlockSpec((tile, width), lambda t: (t + at, 0)),
        out_shape=made(x.shape, x.dtype),
        input_output_aliases={0: 0},
        compiler_params=ROOM,
        cost_estimate=SMALL,
        name="add_half",
    )(x, part)


def column_kernel(own_ref, x_ref, y_ref, *outs):
    total = own_ref[...].astype(f32) + x_ref[...].astype(f32) + y_ref[...].astype(f32)
    for k in range(4):

        @pl.when(pl.program_id(0) == k)
        def _():
            if k < 3 or len(outs) == 4:
                outs[k][...] = total.astype(outs[k].dtype)
            else:
                cut = outs[3].shape[0]
                outs[3][...] = total[:cut].astype(bf16)
                outs[4][...] = total[cut:].astype(bf16)


def column_sum(own, from_x, from_y, cut=0):
    rows, width = own.shape[0] // 4, own.shape[1]
    sizes = [rows] * 4 if cut == 0 else [rows] * 3 + [cut, rows - cut]
    block = pl.BlockSpec((rows, width), lambda t: (t, 0))
    mine, *parts = pl.pallas_call(
        column_kernel,
        grid=(4,),
        in_specs=[block] * 3,
        out_specs=[whole((size, width)) for size in sizes],
        out_shape=[made((rows, width), f32)] + [made((size, width), bf16) for size in sizes[1:]],
        compiler_params=ROOM,
        cost_estimate=SMALL,
        name="column_sum",
    )(own, from_x, from_y)
    return mine, parts


def z_sum(mine, parts):
    for part in parts:
        mine = mine + part.astype(f32)
    return mine


def slot_of(offset):
    return (offset & 3) * 4 + (offset >> 2)


def of_first(shape, dim):
    return (lax.broadcasted_iota(jnp.int32, shape, dim) & 32) == 0


def head_sums(x, same):
    high = x.astype(bf16)
    low = (x - high.astype(f32)).astype(bf16)
    return dot(high, same) + dot(low, same)


def same_head():
    same = of_first((PAIR, PAIR), 0) == of_first((PAIR, PAIR), 1)
    return jnp.where(same, 1.0, 0.0).astype(bf16)


def turned_unit(raw, cosine, sine, same):
    turned = raw * cosine + pltpu.roll(raw, HEAD_DIM, 1) * sine
    scale = lax.rsqrt(head_sums(turned * turned, same) + norm_eps)
    return turned * scale, scale


def local_rows(block, half_blocks, rank):
    count = 2 * half_blocks
    return pl.multiple_of(lax.rem(block + half_blocks * rank, count) * BLOCK, BLOCK)


def attend_kernel(
    info, x_ref, a_ref, b_ref, a_other, b_other, cos_ref, sin_ref, qa_ref, ka_ref,
    w_ref, wo_ref, scale_ref, raw_ref, q_ref, k_ref, v_ref, mix_ref, inv_ref,
    q_aug, k_aug,
):
    blocks = x_ref.shape[0] // BLOCK
    rank = info[blocks]
    part = HEAD_DIM // 2

    def assemble(halves):
        for t, ref in enumerate(halves):
            for head in range(2):
                for m in range(4):
                    source = slice(head * ROWS + m * part, head * ROWS + (m + 1) * part)
                    at = t * HEAD_DIM + head * part
                    if m < 3:
                        w_ref[0, m * PAIR + at : m * PAIR + at + part, :] = ref[source, :]
                    else:
                        wo_ref[at : at + part, :] = ref[source, :]
        rows = [
            halves[0][head * ROWS + 4 * part : (head + 1) * ROWS, :PAIR].astype(f32)[:8] for head in range(2)
        ]
        scales = jnp.where(of_first((8, PAIR), 1), rows[0], pltpu.roll(rows[1], 32, 1))
        scale_ref[0] = scales[:1]

    pl.when(rank == 0)(functools.partial(assemble, (a_ref, a_other)))
    pl.when(rank != 0)(functools.partial(assemble, (b_other, b_ref)))

    first = of_first((BLOCK, PAIR), 1)
    tall = 2 * BLOCK if blocks % 2 == 0 else BLOCK
    first_tall = of_first((tall, PAIR), 1)
    same = same_head()

    def project(t, carry):
        rows = pl.ds(pl.multiple_of(t * tall, tall), tall)
        raw = dot(x_ref[rows, :], w_ref[0], NT)
        raw_ref[rows, :] = raw[:, : 2 * PAIR]
        v_ref[rows, :] = raw[:, 2 * PAIR :].astype(bf16)
        cosine, sine = cos_ref[rows, :], sin_ref[rows, :]
        scale = scale_ref[0]
        q = (turned_unit(raw[:, :PAIR], cosine, sine, same)[0] * scale).astype(bf16)
        k = (turned_unit(raw[:, PAIR : 2 * PAIR], cosine, sine, same)[0] * scale).astype(bf16)
        q_ref[rows, :] = q
        k_ref[rows, :] = k
        q8 = q * jnp.asarray(8.0, bf16)
        qa, ka = qa_ref[rows, :], ka_ref[rows, :]
        q_aug[0, rows, :] = jnp.where(first_tall, q8, qa)
        q_aug[1, rows, :] = jnp.where(first_tall, qa, q8)
        k_aug[0, rows, :] = jnp.where(first_tall, k, ka)
        k_aug[1, rows, :] = jnp.where(first_tall, ka, k)
        return carry

    lax.fori_loop(0, blocks * BLOCK // tall, project, 0)

    row = lax.broadcasted_iota(jnp.int32, (BLOCK, BLOCK), 0)
    col = lax.broadcasted_iota(jnp.int32, (BLOCK, BLOCK), 1)
    causal = col <= row

    def query_block(g, carry):
        q_rows = pl.ds(local_rows(g, blocks // 2, rank), BLOCK)
        count = g - info[g] + 1

        def variant(nk):
            mixed = []
            k_rows = [pl.ds(local_rows(g - (nk - 1) + j, blocks // 2, rank), BLOCK) for j in range(nk)]
            for h in range(2):
                q = q_aug[h, q_rows, :]
                lacc = acc = None
                for j in range(nk):
                    p = jnp.exp(dot(q, k_aug[h, k_rows[j], :], NT))
                    if j == nk - 1:
                        p = jnp.where(causal, p, 0.0)
                    part = p[:, :PAIR] + p[:, PAIR:]
                    lacc = part if lacc is None else lacc + part
                    part = dot(p.astype(bf16), v_ref[k_rows[j], :])
                    acc = part if acc is None else acc + part
                inverse = 1.0 / jnp.sum(lacc, axis=1, keepdims=True)
                inv_ref[0, h : h + 1, q_rows] = 1.0 / jnp.sum(lacc.T, axis=0, keepdims=True)
                mixed.append(acc * inverse)
            mix_ref[q_rows, :] = jnp.where(first, mixed[0], mixed[1]).astype(bf16)

        for nk in range(1, 5):
            pl.when(count == nk if nk < 4 else count >= 4)(functools.partial(variant, nk))
        return carry

    lax.fori_loop(0, blocks, query_block, 0)


def whole(shape):
    return pl.BlockSpec(shape, lambda p: (0,) * len(shape))


def attend_forward(info, x_all, parts, cosine, sine, qa, ka):
    tokens, width = x_all.shape
    pairs = 2
    feats = pairs * PAIR
    by_pair = pl.BlockSpec((tokens, PAIR), lambda p: (0, p))
    return pl.pallas_call(
        attend_kernel,
        grid=(pairs,),
        in_specs=[
            pl.BlockSpec(memory_space=pltpu.SMEM),
            whole((tokens, width)),
        ]
        + [pl.BlockSpec((2 * ROWS, width), lambda p: (p, 0))] * 4
        + [
            whole((tokens, PAIR)),
            whole((tokens, PAIR)),
            whole((tokens, PAIR)),
            whole((tokens, PAIR)),
        ],
        out_specs=[
            pl.BlockSpec((1, 3 * PAIR, width), lambda p: (p, 0, 0)),
            pl.BlockSpec((PAIR, width), lambda p: (p, 0)),
            pl.BlockSpec((1, 1, PAIR), lambda p: (p, 0, 0)),
            pl.BlockSpec((tokens, 2 * PAIR), lambda p: (0, p)),
            by_pair,
            by_pair,
            by_pair,
            by_pair,
            pl.BlockSpec((1, 8, tokens), lambda p: (p, 0, 0)),
        ],
        out_shape=[
            made((pairs, 3 * PAIR, width), bf16),
            made((feats, width), bf16),
            made((pairs, 1, PAIR), f32),
            made((tokens, 2 * feats), f32),
            made((tokens, feats), bf16),
            made((tokens, feats), bf16),
            made((tokens, feats), bf16),
            made((tokens, feats), bf16),
            made((pairs, 8, tokens), f32),
        ],
        scratch_shapes=[
            pltpu.VMEM((2, tokens, PAIR), bf16),
            pltpu.VMEM((2, tokens, PAIR), bf16),
        ],
        compiler_params=ROOM,
        cost_estimate=SMALL,
        name="attend_forward",
    )(info, *far(x_all), *parts, *far(cosine, sine, qa, ka))


def attend_back_kernel(
    info, q_ref, k_ref, v_ref, gb_ref, x_ref, wo_ref, mix_ref, inv_ref, raw_ref, cos_ref, sin_ref, scale_ref,
    qa_ref, ka_ref,
    grad_ref, keep_0, keep_1, send_0, send_1,
    q_aug, k_aug, do_h, q_h, kt_h, delta, dq_acc, dk_acc, dv_acc, dw_acc,
):
    blocks = q_ref.shape[0] // BLOCK
    rank = info[blocks]
    first = of_first((BLOCK, PAIR), 1)
    first_rows = of_first((PAIR, BLOCK), 0)
    zero = jnp.zeros((BLOCK, PAIR), bf16)
    eight = jnp.asarray(8.0, bf16)
    same = same_head()

    def prepare(t, carry):
        start = pl.multiple_of(t * BLOCK, BLOCK)
        rows = pl.ds(start, BLOCK)
        q8 = q_ref[rows, :] * eight
        k = k_ref[rows, :]
        qa, ka = qa_ref[rows, :], ka_ref[rows, :]
        q_aug[0, rows, :] = jnp.where(first, q8, qa)
        q_aug[1, rows, :] = jnp.where(first, qa, q8)
        k_aug[0, rows, :] = jnp.where(first, k, ka)
        k_aug[1, rows, :] = jnp.where(first, ka, k)
        q_h[0, rows, :] = jnp.where(first, q8, zero)
        q_h[1, rows, :] = jnp.where(first, zero, q8)
        k_t = (k * eight).astype(f32).T
        kt_h[0, :, rows] = jnp.where(first_rows, k_t, 0.0).astype(bf16)
        kt_h[1, :, rows] = jnp.where(first_rows, 0.0, k_t).astype(bf16)
        grad = dot(gb_ref[rows, :], wo_ref[...], NT).astype(bf16)
        do_h[0, rows, :] = jnp.where(first, grad, zero)
        do_h[1, rows, :] = jnp.where(first, zero, grad)
        inner = (grad.astype(f32) * mix_ref[rows, :].astype(f32)).T
        inner = inner[:HEAD_DIM] + inner[HEAD_DIM:]
        delta[0:1, rows] = jnp.sum(inner[: HEAD_DIM // 2], axis=0, keepdims=True)
        delta[1:2, rows] = jnp.sum(inner[HEAD_DIM // 2 :], axis=0, keepdims=True)
        dk_acc[rows, :] = jnp.zeros((BLOCK, PAIR), f32)
        dv_acc[rows, :] = jnp.zeros((BLOCK, PAIR), f32)
        return carry

    lax.fori_loop(0, blocks, prepare, 0)

    row = lax.broadcasted_iota(jnp.int32, (BLOCK, BLOCK), 0)
    col = lax.broadcasted_iota(jnp.int32, (BLOCK, BLOCK), 1)
    causal = row <= col

    def query_block(g, carry):
        q_rows = pl.ds(local_rows(g, blocks // 2, rank), BLOCK)
        count = g - info[g] + 1

        def variant(nk):
            dq_t = None
            for j in range(nk):
                k_rows = pl.ds(local_rows(g - (nk - 1) + j, blocks // 2, rank), BLOCK)
                dk = dv = None
                for h in range(2):
                    scores = dot(k_aug[h, k_rows, :], q_aug[h, q_rows, :], NT)
                    p = jnp.exp(scores) * inv_ref[0, h : h + 1, q_rows]
                    if j == nk - 1:
                        p = jnp.where(causal, p, 0.0)
                    dp = dot(v_ref[k_rows, :], do_h[h, q_rows, :], NT)
                    ds = (p * (dp - delta[h : h + 1, q_rows])).astype(bf16)
                    dv_part = dot(p.astype(bf16), do_h[h, q_rows, :])
                    dk_part = dot(ds, q_h[h, q_rows, :])
                    dq_part = dot(kt_h[h, :, k_rows], ds)
                    dv = dv_part if dv is None else dv + dv_part
                    dk = dk_part if dk is None else dk + dk_part
                    dq_t = dq_part if dq_t is None else dq_t + dq_part
                dv_acc[k_rows, :] += dv
                dk_acc[k_rows, :] += dk
            dq_acc[q_rows, :] = dq_t.T

        for nk in range(1, 5):
            pl.when(count == nk if nk < 4 else count >= 4)(functools.partial(variant, nk))
        return carry

    lax.fori_loop(0, blocks, query_block, 0)

    tall = 2 * BLOCK if blocks % 2 == 0 else BLOCK

    def unturn(t, total):
        rows = pl.ds(pl.multiple_of(t * tall, tall), tall)
        cosine, sine = cos_ref[rows, :], sin_ref[rows, :]
        scale = scale_ref[0]
        for which, acc in ((0, dq_acc), (1, dk_acc)):
            raw = raw_ref[rows, which * PAIR : (which + 1) * PAIR]
            unit, size = turned_unit(raw, cosine, sine, same)
            grad = acc[rows, :]
            total = total + jnp.sum((grad * unit).reshape(tall // 8, 8, PAIR), axis=0)
            grad_unit = grad * scale
            grad_turned = size * (grad_unit - unit * head_sums(unit * grad_unit, same))
            grad_raw = grad_turned * cosine - pltpu.roll(grad_turned, HEAD_DIM, 1) * sine
            grad_ref[rows, which * PAIR : (which + 1) * PAIR] = grad_raw.astype(bf16)
        grad_ref[rows, 2 * PAIR :] = dv_acc[rows, :].astype(bf16)
        return total

    total = lax.fori_loop(0, blocks * BLOCK // tall, unturn, jnp.zeros((8, PAIR), f32))
    scale_row = jnp.sum(total, axis=0, keepdims=True)

    dw_acc[...] = jnp.zeros_like(dw_acc)

    def row_grads(t, carry):
        rows = pl.ds(pl.multiple_of(t * tall, tall), tall)
        dw_acc[: 3 * PAIR, :] += dot(grad_ref[rows, :], x_ref[rows, :], TN)
        dw_acc[3 * PAIR :, :] += dot(mix_ref[rows, :], gb_ref[rows, :], TN)
        return carry

    lax.fori_loop(0, blocks * BLOCK // tall, row_grads, 0)
    part = HEAD_DIM // 2

    pair = pl.program_id(0)

    def deal(keep, send):
        for half, out in enumerate((keep, send)):
            for head in range(2):
                base = head * ROWS
                for m in range(4):
                    for t in range(2):

                        @pl.when((rank == t) == (half == 0))
                        def _():
                            at = m * PAIR + t * HEAD_DIM + head * part
                            out[base + m * part : base + (m + 1) * part, :] = dw_acc[at : at + part, :].astype(bf16)

                tail = slice(base + 4 * part, base + ROWS)
                out[tail, :] = jnp.zeros((ROWS - 4 * part, out.shape[1]), bf16)
                if half == 0:
                    row = scale_row if head == 0 else pltpu.roll(jnp.broadcast_to(scale_row, (8, PAIR)), 96, 1)[:1]
                    rows = ROWS - 4 * part
                    top = lax.broadcasted_iota(jnp.int32, (rows, PAIR), 0) == 0
                    out[tail, :PAIR] = jnp.where(top, jnp.broadcast_to(row, (rows, PAIR)), 0.0).astype(bf16)

    pl.when(pair == 0)(functools.partial(deal, keep_0, send_0))
    pl.when(pair == 1)(functools.partial(deal, keep_1, send_1))


def attend_backward(info, q, k, v, grad_branch, x, wo, mixture, inverse, raw, cosine, sine, scale, qa, ka):
    tokens, feats = q.shape
    width = x.shape[1]
    pairs = feats // PAIR
    by_pair = pl.BlockSpec((tokens, PAIR), lambda p: (0, p))
    half = pltpu.VMEM((2, tokens, PAIR), bf16)
    acc = pltpu.VMEM((tokens, PAIR), f32)
    return pl.pallas_call(
        attend_back_kernel,
        grid=(pairs,),
        in_specs=[
            pl.BlockSpec(memory_space=pltpu.SMEM),
            by_pair,
            by_pair,
            by_pair,
            whole((tokens, width)),
            whole((tokens, width)),
            pl.BlockSpec((PAIR, width), lambda p: (p, 0)),
            by_pair,
            pl.BlockSpec((1, 8, tokens), lambda p: (p, 0, 0)),
            pl.BlockSpec((tokens, 2 * PAIR), lambda p: (0, p)),
            whole((tokens, PAIR)),
            whole((tokens, PAIR)),
            pl.BlockSpec((1, 1, PAIR), lambda p: (p, 0, 0)),
            whole((tokens, PAIR)),
            whole((tokens, PAIR)),
        ],
        out_specs=[
            pl.BlockSpec((tokens, 3 * PAIR), lambda p: (0, p)),
        ]
        + [whole((2 * ROWS, width))] * 4,
        out_shape=[made((tokens, 3 * feats), bf16)] + [made((2 * ROWS, width), bf16)] * 4,
        scratch_shapes=[
            half,
            half,
            half,
            half,
            pltpu.VMEM((2, PAIR, tokens), bf16),
            pltpu.VMEM((8, tokens), f32),
            acc,
            acc,
            acc,
            pltpu.VMEM((4 * PAIR, width), f32),
        ],
        compiler_params=ROOM,
        cost_estimate=SMALL,
        name="attend_backward",
    )(info, *far(q, k, v, grad_branch, x, wo, mixture, inverse, raw, cosine, sine), scale, *far(qa, ka))


def slot_scale(ref, group):
    return ref[:, 2 * PAIR : 2 * PAIR + 2 * group].astype(f32)[:1]


def scale_specs(width):
    return [pl.BlockSpec((16, width), lambda t, n=n: ((n * ROWS + 2 * HEAD_DIM) // 16, 0)) for n in range(4)]


def up_gate_kernel(h_ref, *refs):
    *w_refs, s_0, s_1, s_2, s_3, ug_ref, product_ref = refs
    group = product_ref.shape[1] // 4
    per = 4 // len(w_refs)
    for k in range(4):
        pair = slice(2 * k * group, 2 * (k + 1) * group)
        at = 2 * (k % per) * group
        both = dot(h_ref[...], w_refs[k // per][at : at + 2 * group, :], NT)
        ug_ref[:, pair] = both.astype(bf16)
        scaled = both * slot_scale((s_0, s_1, s_2, s_3)[k], group)
        gated = scaled[:, group:]
        product = scaled[:, :group] * gated / (1.0 + jnp.exp(-gated))
        product_ref[:, k * group : (k + 1) * group] = product.astype(bf16)


def tile_of(tokens):
    return 512 if tokens % 512 == 0 else 256


def up_gate(hidden, w, scale, before=None):
    tokens, width = hidden.shape
    w = w if isinstance(w, tuple) else (w,)
    units = w[0].shape[0] * len(w) // 2
    tile = tokens // 2
    at = 0 if before is None else 2
    more = [] if before is None else list(before)
    inputs = 5 + len(w)

    def kernel(*refs):
        up_gate_kernel(*refs[:inputs], *refs[inputs + len(more) :])

    return pl.pallas_call(
        kernel,
        grid=(2,),
        in_specs=[
            pl.BlockSpec((tile, width), lambda t: (t, 0)),
        ]
        + [whole(part.shape) for part in w]
        + scale_specs(width)
        + [pl.BlockSpec(memory_space=pl.ANY)] * len(more),
        out_specs=[
            pl.BlockSpec((tile, 2 * units), lambda t: (t + at, 0)),
            pl.BlockSpec((tile, units), lambda t: (t + at, 0)),
        ],
        out_shape=[made((2 * tokens, 2 * units), bf16), made((2 * tokens, units), bf16)],
        input_output_aliases={inputs + n: n for n in range(len(more))},
        compiler_params=ROOM,
        cost_estimate=SMALL,
        name="up_gate",
    )(hidden, *w, *[scale] * 4, *more)


def feed_back_kernel(
    count, grad_ref, h_ref, *rest
):
    w_refs, rest = rest[:count], rest[count:]
    ug_ref, product_ref, s_0, s_1, s_2, s_3, gug_ref, *dws, ug_acc, d_acc, gscale = rest
    group = product_ref.shape[1] // 4
    per_w, per = 4 // count, 4 // len(dws)
    step = pl.program_id(0)

    @pl.when(step == 0)
    def _():
        gscale[...] = jnp.zeros_like(gscale)
        ug_acc[...] = jnp.zeros_like(ug_acc)
        d_acc[...] = jnp.zeros_like(d_acc)

    rows = grad_ref.shape[0] // 8
    d_acc[...] += dot(product_ref[...], grad_ref[...], TN)
    for k in range(4):
        ups = slice(2 * k * group, (2 * k + 1) * group)
        gates = slice((2 * k + 1) * group, (2 * k + 2) * group)
        at = (k % per_w) * group
        grad = dot(grad_ref[...], w_refs[k // per_w][at : at + group, :], NT)
        up = ug_ref[:, ups].astype(f32)
        gate = ug_ref[:, gates].astype(f32)
        scales = slot_scale((s_0, s_1, s_2, s_3)[k], group)
        up_scale, gate_scale = scales[:, :group], scales[:, group:]
        gated = gate * gate_scale
        sig = 1.0 / (1.0 + jnp.exp(-gated))
        silu = gated * sig
        through = grad * silu
        grad_gated = grad * (up * up_scale) * (sig + silu * (1.0 - sig))
        gug_ref[:, ups] = (through * up_scale).astype(bf16)
        gug_ref[:, gates] = (grad_gated * gate_scale).astype(bf16)
        gscale[:, ups] += jnp.sum((through * up).reshape(rows, 8, group), axis=0)
        gscale[:, gates] += jnp.sum((grad_gated * gate).reshape(rows, 8, group), axis=0)
    ug_acc[...] += dot(gug_ref[...], h_ref[...], TN)

    @pl.when(step == pl.num_programs(0) - 1)
    def _():
        top = lax.broadcasted_iota(jnp.int32, (16, 2 * group), 0) == 0
        for k in range(4):
            out, at = dws[k // per], (k % per) * (3 * group + 16)
            out[at : at + 2 * group, :] = ug_acc[2 * k * group : 2 * (k + 1) * group, :].astype(bf16)
            out[at + 2 * group : at + 3 * group, :] = d_acc[k * group : (k + 1) * group, :].astype(bf16)
            sums = jnp.sum(gscale[:, 2 * k * group : 2 * (k + 1) * group], axis=0, keepdims=True)
            tail = slice(at + 3 * group, at + 3 * group + 16)
            out[tail, :] = jnp.zeros((16, out.shape[1]), bf16)
            out[tail, : 2 * group] = jnp.where(top, jnp.broadcast_to(sums, top.shape), 0.0).astype(bf16)


def feed_back(grad, hidden, w, ug, product, scale, pieces=1):
    tokens, width = grad.shape
    w = w if isinstance(w, tuple) else (w,)
    units = product.shape[1]
    tile = tile_of(tokens)
    row = pl.BlockSpec((tile, width), lambda t: (t, 0))
    wide = pl.BlockSpec((tile, 2 * units), lambda t: (t, 0))
    rows = (units * 3 + 64) // pieces
    return pl.pallas_call(
        functools.partial(feed_back_kernel, len(w)),
        grid=(tokens // tile,),
        in_specs=[
            row,
            row,
            *[whole(part.shape) for part in w],
            wide,
            pl.BlockSpec((tile, units), lambda t: (t, 0)),
        ]
        + scale_specs(width),
        out_specs=[wide] + [whole((rows, width))] * pieces,
        out_shape=[made((tokens, 2 * units), bf16)] + [made((rows, width), bf16)] * pieces,
        scratch_shapes=[
            pltpu.VMEM((2 * units, width), f32),
            pltpu.VMEM((units, width), f32),
            pltpu.VMEM((8, 2 * units), f32),
        ],
        compiler_params=ROOM,
        cost_estimate=SMALL,
        name="feed_back",
    )(*far(grad, hidden), *w, *far(ug, product), *[scale] * 4)


def sum_dots_kernel(plan, start, tile, *refs):
    rights = plan[-1][2] + 1
    has = len(refs) - rights - 3 - 2 * len(plan)
    addend = refs[rights] if has else None
    out, acc, *bufs, sems = refs[rights + has :]
    rows = out.shape[0]
    copies = []
    for n, (left, at, right) in enumerate(plan):
        depth = refs[right].shape[0]
        copies.append((
            pltpu.make_async_copy(refs[left].at[pl.ds(start, rows), pl.ds(at, depth)], bufs[2 * n], sems.at[2 * n]),
            pltpu.make_async_copy(refs[right], bufs[2 * n + 1], sems.at[2 * n + 1]),
        ))
    for pair in copies:
        for copy in pair:
            copy.start()
    last = len(plan) - 1
    for n, pair in enumerate(copies):
        for copy in pair:
            copy.wait()
        for r in range(0, rows, tile):
            here = slice(r, r + tile)
            part = dot(bufs[2 * n][here, :], bufs[2 * n + 1][...])
            if n > 0:
                part = part + acc[here, :]
            elif addend is not None:
                part = part + addend[here, :].astype(f32)
            if n < last:
                acc[here, :] = part
            else:
                out[here, :] = part.astype(out.dtype)


def sum_dots(lefts, rights, start, rows, dtype, addend=None):
    plan, parts = [], []
    for c, right in enumerate(rights):
        at = 0
        for part in right if isinstance(right, tuple) else (right,):
            plan.append((c, at, len(lefts) + len(parts)))
            parts.append(part)
            at += part.shape[0]
    width = parts[0].shape[1]
    bufs = [pltpu.VMEM(shape, bf16) for part in parts for shape in ((rows, part.shape[0]), part.shape)]
    more = [] if addend is None else [addend]
    far_ref = pl.BlockSpec(memory_space=pltpu.HBM)
    near = pl.BlockSpec(memory_space=pltpu.VMEM)
    return pl.pallas_call(
        functools.partial(sum_dots_kernel, plan, start, 256),
        in_specs=[far_ref] * (len(lefts) + len(parts)) + [near] * len(more),
        out_specs=near,
        out_shape=made((rows, width), dtype),
        scratch_shapes=[pltpu.VMEM((rows, width), f32), *bufs, pltpu.SemaphoreType.DMA((2 * len(plan),))],
        compiler_params=ROOM,
        cost_estimate=SMALL,
        name="sum_dots",
    )(*lefts, *parts, *more)


def alpha_kernel(place, *refs):
    slots, one, two, rows = refs[:HEADS], refs[HEADS], refs[HEADS + 1], refs[HEADS + 2]
    for j in range(HEADS):
        rows[j : j + 1, :] = slots[j][:, PAIR : 2 * PAIR].astype(f32)[:1]
    low = lax.broadcasted_iota(jnp.int32, (1, PAIR), 1) < HEAD_DIM
    for k in range(HEADS // 2):
        pair = []
        for owner in (2 * k, 2 * k + 1):
            slot = slot_of(jnp.bitwise_xor(place[0], owner))
            pair.append(jnp.broadcast_to(rows[pl.ds(slot, 1), :], (8, PAIR)))
        turned = [pltpu.roll(p, HEAD_DIM, 1)[:1] for p in pair]
        lanes = slice(k * PAIR, (k + 1) * PAIR)
        one[:, lanes] = jnp.where(low, pair[0][:1], turned[1])
        two[:, lanes] = jnp.where(low, turned[0], pair[1][:1])


def alpha_rows(place, chunks):
    width = chunks[0].shape[1]
    specs = scale_specs(width)
    return pl.pallas_call(
        alpha_kernel,
        grid=(1,),
        in_specs=[pl.BlockSpec(memory_space=pltpu.SMEM)] + specs * 4,
        out_specs=[whole((1, width))] * 2,
        out_shape=[made((1, width), f32)] * 2,
        scratch_shapes=[pltpu.VMEM((HEADS, PAIR), f32)],
        compiler_params=ROOM,
        cost_estimate=SMALL,
        name="alpha",
    )(place[None].astype(jnp.int32), *(chunk for chunk in chunks for _ in range(4)))


def rms_scale(values):
    return lax.rsqrt(jnp.mean(values * values, axis=-1, keepdims=True) + norm_eps)


def blend_parts(residual, branch, mixing):
    branch_scale = rms_scale(branch)
    unit = branch * branch_scale
    step = unit - residual
    mixed = residual + mixing * step
    mixed_scale = rms_scale(mixed)
    return branch_scale, unit, step, mixed * mixed_scale, mixed_scale


def blend_grads(parts, mixing, grad):
    branch_scale, unit, step, result, mixed_scale = parts
    grad_mixed = mixed_scale * (grad - result * jnp.mean(grad * result, axis=-1, keepdims=True))
    grad_unit = mixing * grad_mixed
    grad_branch = branch_scale * (grad_unit - unit * jnp.mean(unit * grad_unit, axis=-1, keepdims=True))
    return grad_mixed - grad_unit, grad_branch, grad_mixed * step


def add_rows(ref, values):
    @pl.when(pl.program_id(0) == 0)
    def _():
        ref[...] = jnp.zeros_like(ref)

    ref[...] += jnp.sum(values.reshape(values.shape[0] // 8, 8, values.shape[1]), axis=0)


def hidden_kernel(x_ref, own_ref, other_ref, mix_ref, hidden_ref, round_ref, wide_ref):
    branch = own_ref[...] + other_ref[...].astype(f32)
    hidden = blend_parts(x_ref[...].astype(f32), branch, mix_ref[...])[3]
    hidden_ref[...] = hidden
    round_ref[...] = wide_ref[...] = hidden.astype(bf16)


def output_kernel(
    hidden_ref, own_ref, other_ref, mix_ref, cot_ref, out_ref, res_ref, down_ref, wide_ref, gmix_ref
):
    mixing = mix_ref[...]
    parts = blend_parts(hidden_ref[...], own_ref[...] + other_ref[...].astype(f32), mixing)
    out_ref[...] = parts[3]
    grad_res, grad_down, grad_mix = blend_grads(parts, mixing, cot_ref[...].astype(f32))
    res_ref[...] = grad_res
    down_ref[...] = wide_ref[...] = grad_down.astype(bf16)
    add_rows(gmix_ref, grad_mix)


def hidden_back_kernel(
    x_ref, own_ref, other_ref, mix_ref, res_ref, back_ref, from_ref, in_ref, branch_ref, wide_ref, gmix_ref
):
    mixing = mix_ref[...]
    parts = blend_parts(x_ref[...].astype(f32), own_ref[...] + other_ref[...].astype(f32), mixing)
    grad = res_ref[...] + back_ref[...] + from_ref[...].astype(f32)
    grad_res, grad_branch, grad_mix = blend_grads(parts, mixing, grad)
    in_ref[...] = grad_res
    branch_ref[...] = wide_ref[...] = grad_branch.astype(bf16)
    add_rows(gmix_ref, grad_mix)


def rowwise(kernel, name, arrays, floats, reduced=False):
    tokens, width = arrays[0].shape
    tile = 128
    row = pl.BlockSpec((tile, width), lambda t: (t, 0))
    out_shape = [made((tokens, width), f32)] * floats
    out_shape += [made((tokens, width), bf16), made((2 * tokens, width), bf16)]
    out_specs = [row] * (floats + 2)
    if reduced:
        out_shape.append(made((8, width), f32))
        out_specs.append(whole((8, width)))
    return pl.pallas_call(
        kernel,
        grid=(tokens // tile,),
        in_specs=[row if a.shape[0] == tokens else whole((1, width)) for a in arrays],
        out_specs=out_specs,
        out_shape=out_shape,
        compiler_params=ROOM,
        cost_estimate=SMALL,
        name=name,
    )(*(far(a)[0] if a.dtype == f32 and a.shape[0] == tokens else a for a in arrays))


def adam_change(weight, gradient, moment_one, moment_two, renormalize):
    moment_one_new = beta_one * moment_one + (1.0 - beta_one) * gradient
    moment_two_new = beta_two * moment_two + (1.0 - beta_two) * gradient * gradient
    stepped = weight - learn_rate * (moment_one_new / corr_one) / (
        jnp.sqrt(moment_two_new / corr_two) + adam_eps
    )
    if renormalize:
        stepped = stepped * lax.rsqrt(jnp.sum(stepped * stepped, axis=-1, keepdims=True) + norm_eps)
    return stepped - weight


def adam_kernel(w_ref, g_ref, one_ref, two_ref, out_ref):
    out_ref[...] = adam_change(w_ref[...], g_ref[...], one_ref[...], two_ref[...], True)


def adam_rows(weight, gradient, moment_one, moment_two):
    shape = weight.shape
    rows, width = shape[0] * shape[1], shape[2]
    tile = next(t for t in (128, 64, 32, 16, 8) if rows % t == 0)
    block = pl.BlockSpec((tile, width), lambda t: (t, 0))
    return pl.pallas_call(
        adam_kernel,
        grid=(rows // tile,),
        in_specs=[block] * 4,
        out_specs=block,
        out_shape=made((rows, width), f32),
        compiler_params=ROOM,
        cost_estimate=SMALL,
        name="adam",
    )(*far(*(a.reshape(rows, width) for a in (weight, gradient, moment_one, moment_two)))).reshape(shape)


def own_half(x, rank, axis):
    size = x.shape[axis] // 2
    return lax.dynamic_slice_in_dim(x, rank * size, size, axis)


def pick(rank, zero, one):
    return jnp.where(rank == 0, zero, one)


def document_tables(segment_ids, rank, count):
    segments = segment_ids.reshape(-1)
    docs = jnp.arange(8, dtype=jnp.int32)
    begins = jnp.sum((segments[None, :] < docs[:, None]).astype(jnp.int32), axis=1)
    is_doc = segments[:, None] == docs[None, :]
    starts = jnp.sum(jnp.where(is_doc, begins[None, :], 0), axis=1)
    info = jnp.concatenate([starts[::BLOCK] // BLOCK, rank[None].astype(jnp.int32)])
    place = jnp.arange(2 * count, dtype=jnp.int32)

    def arranged(values):
        own = lax.dynamic_slice_in_dim(values, rank * count, count, 0)
        other = lax.dynamic_slice_in_dim(values, (1 - rank) * count, count, 0)
        return jnp.concatenate([own, other], 0)

    positions = arranged(place - starts).astype(f32)
    frequency = jnp.exp(
        jnp.arange(HEAD_DIM // 2, dtype=f32) * (-2.0 * math.log(rope_base) / HEAD_DIM)
    )
    angles = positions[:, None] * jnp.tile(frequency, 4)[None, :]
    cosine = jnp.cos(angles)
    sign = jnp.where(jnp.arange(PAIR) < HEAD_DIM, -1.0, 1.0).astype(f32)
    sine = jnp.sin(angles) * sign[None, :]
    lanes = jnp.arange(PAIR, dtype=jnp.int32)
    lanes = jnp.where(lanes < HEAD_DIM, lanes & 31, 8)
    own_doc = arranged(segments)[:, None] == lanes[None, :]
    query_mark = own_doc.astype(bf16)
    key_mark = jnp.where(own_doc | (lanes >= 8)[None, :], 0.0, -apart).astype(bf16)
    return info, cosine, sine, query_mark, key_mark


def scale_row(qk, alpha, feed, width):
    count = qk.shape[0]
    gap = jnp.zeros((count, HEAD_DIM // 2), f32)
    row = [qk[:, : HEAD_DIM // 2], gap, qk[:, HEAD_DIM // 2 :], gap]
    row += [jnp.broadcast_to(alpha.reshape(1, -1), (count, PAIR)), feed.reshape(count, -1)]
    row = jnp.concatenate(row, 1).astype(bf16)
    return jnp.pad(row[:, None], ((0, 0), (0, 15), (0, width - row.shape[1])))


class Group:
    def __init__(self, tables, x_all, parts):
        self.tables = tables
        info, cosine, sine, query_mark, key_mark = tables
        (self.w, self.wo, self.scale, self.raw, self.q, self.k, self.v, self.mixture, self.inverse) = attend_forward(
            info, x_all, parts, cosine, sine, query_mark, key_mark
        )

    def back(self, grad_branch, x_all):
        info, cosine, sine, query_mark, key_mark = self.tables
        grad_qkv, *rows = attend_backward(
            info, self.q, self.k, self.v, grad_branch, x_all, self.wo, self.mixture, self.inverse, self.raw,
            cosine, sine, self.scale, query_mark, key_mark,
        )
        return grad_qkv, tuple(rows[:2]), tuple(rows[2:])


def local_sixteen(
    tokens,
    segment_ids,
    cotangent,
    attention_weights,
    feed_weights,
    attention_scales,
    feed_scales,
    attention_first,
    attention_second,
    feed_first,
    feed_second,
    attention_scale_first,
    attention_scale_second,
    feed_scale_first,
    feed_scale_second,
):
    count, width = tokens.shape[0] * tokens.shape[1], tokens.shape[-1]
    rank, place = lax.axis_index("seq"), lax.axis_index("dp")
    x = tokens.reshape(count, width)

    part = own_half(attention_weights, rank, 1).astype(bf16)
    rows = part.shape[1]
    body = 4 * rows
    extra = scale_row(attention_scales[0:1], attention_scales[1:], own_half(feed_scales, rank, 1)[None], width)
    block_a = jnp.concatenate([part.reshape(body, width), extra[0]], axis=0)
    feed_part = own_half(feed_weights, rank, 1).astype(bf16)
    units = feed_part.shape[1]
    block_u = feed_part[:2].reshape(2 * units, width)
    block_d = feed_part[2]

    z_a = [via(block_a, 4 * k) for k in (1, 2, 3)]
    x_all = jnp.concatenate([x, swap(x)], 0)
    tables = document_tables(segment_ids, rank, count)
    block_a, z_a, block_u, block_d, x_all, tables = tie(block_a, z_a, block_u, block_d, x_all, tables)

    own_a = join(block_a, *z_a)
    x_a, y_a = via(own_a, 1), via(own_a, 2)
    z_u = [via(block_u, 4), via(block_u, 8)]
    own_a, x_a, y_a, z_u, block_u, x_all = tie(own_a, x_a, y_a, z_u, block_u, x_all)

    d_a = diagonal_in(x_a, y_a)
    z_u = z_u + [via(block_u, 12)]
    group_0 = Group(tables, x_all, (own_a, y_a, swap(own_a), swap(y_a)))
    d_a, z_u, block_u, block_d, group_0.mixture, x_all = tie(d_a, z_u, block_u, block_d, group_0.mixture, x_all)

    own_u = join(block_u, *z_u)
    x_u, y_u = via(own_u, 1), via(own_u, 2)
    z_d = [via(block_d, 4), via(block_d, 8)]
    d_a = join(*d_a)
    group_1 = Group(tables, x_all, (x_a, d_a, swap(x_a), swap(d_a)))
    groups = (group_0, group_1)
    mixtures, wos = [g.mixture for g in groups], [g.wo for g in groups]
    branch_other = sum_dots(mixtures, wos, count, count, bf16)
    branch_own = sum_dots(mixtures, wos, 0, count, f32)
    branch_other, branch_own, x_u, y_u, z_d, d_a = tie(branch_other, branch_own, x_u, y_u, z_d, d_a)

    d_u = diagonal_in(x_u, y_u)
    z_d = z_d + [via(block_d, 12)]
    alpha = alpha_rows(place, (own_a, x_a, y_a, d_a))
    branch_from = swap(branch_other)
    hidden, hidden_round, hidden_all = rowwise(
        hidden_kernel, "hidden", [x, branch_own, branch_from, alpha[0]], 1
    )
    first_own = up_gate(hidden_round, own_u, own_a)
    first_x = up_gate(hidden_round, x_u, x_a)
    first_y = up_gate(hidden_round, y_u, y_a)
    d_u, z_d, hidden_round, first_own, first_x, first_y = tie(d_u, z_d, hidden_round, first_own, first_x, first_y)
    own_d = join(block_d, *z_d)
    x_d, y_d = via(own_d, 1), via(own_d, 2)
    hidden_other = swap(hidden_round)
    hidden_all = fill(hidden_all, hidden_other)
    ug_own, product_own = up_gate(hidden_other, own_u, own_a, first_own)
    ug_x, product_x = up_gate(hidden_other, x_u, x_a, first_x)
    ug_y, product_y = up_gate(hidden_other, y_u, y_a, first_y)
    ug_d, product_d = up_gate(hidden_other, d_u, d_a, up_gate(hidden_round, d_u, d_a))
    product_own, product_x, product_y, product_d, hidden_all, x_d, y_d = tie(
        product_own, product_x, product_y, product_d, hidden_all, x_d, y_d
    )

    d_d = diagonal_in(x_d, y_d)
    products = [product_own, product_x, product_y]
    w_ds = [own_d, x_d, y_d]
    down_other = sum_dots(products, w_ds, count, count, f32)
    down_own = sum_dots(products, w_ds, 0, count, f32)
    down_other, down_own, d_d = tie(down_other, down_own, d_d)

    down_other = sum_dots([product_d], [d_d], count, count, bf16, down_other)
    down_own = sum_dots([product_d], [d_d], 0, count, f32, down_own)
    output, grad_hidden_res, grad_down_round, grad_down, grad_alpha_feed = rowwise(
        output_kernel,
        "output",
        [hidden, down_own, swap(down_other), alpha[1], cotangent.reshape(count, width)],
        2,
        True,
    )

    grad_down = fill(grad_down, swap(grad_down_round))
    gug_d, *r_d = feed_back(grad_down, hidden_all, d_d, ug_d, product_d, d_a, 2)
    r_d, grad_down, product_x, product_y, product_own = tie(r_d, grad_down, product_x, product_y, product_own)
    t_d = via(r_d[0], 1), via(r_d[1], 2)
    gug_x, r_x = feed_back(grad_down, hidden_all, x_d, ug_x, product_x, x_a)
    gug_y, r_y = feed_back(grad_down, hidden_all, y_d, ug_y, product_y, y_a)
    gug_own, r_own = feed_back(grad_down, hidden_all, own_d, ug_own, product_own, own_a)
    gugs, w_ugs = [gug_own, gug_x, gug_y, gug_d], [own_u, x_u, y_u, d_u]
    t_d, r_x, r_y, r_own, gugs = tie(t_d, r_x, r_y, r_own, gugs)

    r_x, r_y = add_half(r_x, t_d[1], True), add_half(r_y, t_d[0], False)
    r_x, r_y, gugs = tie(r_x, r_y, gugs)
    v_x, v_y = via(r_x, 1), via(r_y, 2)
    back_other = sum_dots(gugs, w_ugs, count, count, bf16)
    back_from = swap(back_other)
    back_own = sum_dots(gugs, w_ugs, 0, count, f32)
    grad_input_res, grad_branch_round, grad_branch_all, grad_alpha_attend = rowwise(
        hidden_back_kernel,
        "hidden_back",
        [x, branch_own, branch_from, alpha[0], grad_hidden_res, back_own, back_from],
        1,
        True,
    )
    grad_branch_all = fill(grad_branch_all, swap(grad_branch_round))
    grad_alpha = jnp.stack([jnp.sum(grad_alpha_attend, 0), jnp.sum(grad_alpha_feed, 0)])
    alpha_from = via(grad_alpha, 4)
    grad_qkv_1, keep_1, send_1 = group_1.back(grad_branch_all, x_all)
    v_x, v_y, grad_qkv_1, keep_1, send_1, grad_branch_all, alpha_from = tie(
        v_x, v_y, grad_qkv_1, keep_1, send_1, grad_branch_all, alpha_from
    )

    grad_alpha = grad_alpha + alpha_from
    alpha_from = via(grad_alpha, 1)
    feed_mine, feed_parts = column_sum(r_own, v_x, v_y, 112)
    feed_mine, feed_parts, send_1, grad_alpha, alpha_from = tie(feed_mine, feed_parts, send_1, grad_alpha, alpha_from)
    grad_alpha = grad_alpha + alpha_from
    z_feed = [via(feed_parts[0], 4), via(feed_parts[1], 8), via(feed_parts[2], 12)]
    other_1 = swap(send_1[0]), swap(send_1[1])
    a_x = jnp.concatenate([pick(rank, k, o) for k, o in zip(keep_1, other_1)], 0)
    a_d = tuple(pick(rank, o, k) for k, o in zip(keep_1, other_1))
    a_x, a_d, grad_branch_all = tie(a_x, a_d, grad_branch_all)

    t_a = via(a_d[0], 1), via(a_d[1], 2)
    grad_qkv_0, keep_0, send_0 = group_0.back(grad_branch_all, x_all)
    t_a, z_feed, grad_qkv_0, keep_0, send_0 = tie(t_a, z_feed, grad_qkv_0, keep_0, send_0)

    z_rest = via(feed_parts[3], 12)
    other_0 = swap(send_0[0]), swap(send_0[1])
    a_own = jnp.concatenate([pick(rank, k, o) for k, o in zip(keep_0, other_0)], 0)
    a_y = [pick(rank, o, k) for k, o in zip(keep_0, other_0)]
    a_y = jnp.concatenate([plus(a_y[0], t_a[0]), a_y[1]], 0)
    a_x = add_half(a_x, t_a[1], True)
    a_x, a_y, grad_qkv_0, grad_alpha = tie(a_x, a_y, grad_qkv_0, grad_alpha)
    b_x, b_y = via(a_x, 1), via(a_y, 2)
    alpha_from = via(grad_alpha, 2)
    grad_qkvs = [grad_qkv_0, grad_qkv_1]
    w_flats = [g.w.reshape(-1, width) for g in groups]
    input_other = sum_dots(grad_qkvs, w_flats, count, count, bf16)
    input_own = sum_dots(grad_qkvs, w_flats, 0, count, f32, grad_input_res)
    input_other, input_own, b_x, b_y, z_rest, alpha_from = tie(input_other, input_own, b_x, b_y, z_rest, alpha_from)
    z_feed = [z_feed[0], z_feed[1], jnp.concatenate([z_feed[2], z_rest], 0)]
    grad_alpha = grad_alpha + alpha_from
    alpha_from = via(grad_alpha, 8)

    attend_mine, attend_parts = column_sum(a_own, b_x, b_y)
    attend_parts = [via(part, 4 * k) for part, k in zip(attend_parts, (1, 2, 3))]
    input_grad = input_own + swap(input_other).astype(f32)
    total = z_sum(feed_mine, z_feed)
    other = swap(total)
    low, high = pick(rank, total, other), pick(rank, other, total)
    feed_grad = jnp.concatenate([t[: 3 * units].reshape(3, units, width) for t in (low, high)], 1)
    feed_grad_s = jnp.concatenate([t[3 * units, : 2 * units].reshape(2, units) for t in (low, high)], 1)
    feed_change = adam_rows(feed_weights, feed_grad, feed_first, feed_second)
    attend_parts, alpha_from, input_grad, feed_grad, feed_change = tie(
        attend_parts, alpha_from, input_grad, feed_grad, feed_change
    )
    grad_alpha = grad_alpha + alpha_from
    grad_alpha = grad_alpha + swap(grad_alpha)
    own_alpha = lax.dynamic_slice_in_dim(grad_alpha, place * HEAD_DIM, HEAD_DIM, 1)

    total = z_sum(attend_mine, attend_parts)
    other = swap(total)
    low, high = pick(rank, total, other), pick(rank, other, total)
    attend_grad = jnp.concatenate([t[:body].reshape(4, rows, width) for t in (low, high)], 1)
    grad_qk = low[body] + high[body]
    grad_qk = jnp.concatenate([grad_qk[: HEAD_DIM // 2], grad_qk[HEAD_DIM : 3 * HEAD_DIM // 2]], 0)
    attend_grad_s = jnp.concatenate([grad_qk[None], own_alpha], 0)
    return (
        output.reshape(tokens.shape),
        input_grad.reshape(tokens.shape),
        attend_grad,
        feed_grad,
        attend_grad_s,
        feed_grad_s,
        adam_rows(attention_weights, attend_grad, attention_first, attention_second),
        feed_change,
        adam_change(attention_scales, attend_grad_s, attention_scale_first, attention_scale_second, False),
        adam_change(feed_scales, feed_grad_s, feed_scale_first, feed_scale_second, False),
    )


def local_any(
    tokens,
    segment_ids,
    cotangent,
    attention_weights,
    feed_weights,
    attention_scales,
    feed_scales,
    attention_first,
    attention_second,
    feed_first,
    feed_second,
    attention_scale_first,
    attention_scale_second,
    feed_scale_first,
    feed_scale_second,
):
    count, width = tokens.shape[0] * tokens.shape[1], tokens.shape[-1]
    rank = lax.axis_index("seq")
    x = tokens.reshape(count, width)
    x_all = jnp.concatenate([x, swap(x)], axis=0)
    tables = document_tables(segment_ids, rank, count)

    full = lax.all_gather(attention_weights.astype(bf16), "dp", axis=1, tiled=True)
    scales = lax.all_gather(attention_scales.astype(bf16), "dp", axis=1, tiled=True).astype(f32)
    half = width // 2
    alpha = scales[1:]
    mine = lax.dynamic_slice_in_dim(full, rank * half, half, 1)
    mine = jnp.swapaxes(mine.reshape(4, HEADS // 2, 2, HEAD_DIM // 2, width), 0, 1)
    own_scale = lax.dynamic_slice_in_dim(scales[0], rank * half, half, 0).reshape(HEADS // 2, HEAD_DIM)

    groups = []
    for g in range(2):
        heads = slice(4 * g, 4 * g + 4)
        tail = scale_row(own_scale[heads], jnp.zeros((2, HEAD_DIM)), jnp.zeros((4, 2 * PAIR)), width)
        low = jnp.concatenate([mine[heads, :, 0].reshape(4, -1, width), tail], 1).reshape(-1, width)
        high = jnp.concatenate([mine[heads, :, 1].reshape(4, -1, width), tail], 1).reshape(-1, width)
        groups.append(Group(tables, x_all, (low, high, high, low)))

    feed = lax.all_gather(own_half(feed_weights, rank, 1).astype(bf16), "dp", axis=1, tiled=True)
    feed_s = lax.all_gather(own_half(feed_scales, rank, 1).astype(bf16), "dp", axis=1, tiled=True).astype(f32)
    units = feed.shape[1] // 4
    w_ugs, w_ds, feed_scale = [], [], []
    for c in range(4):
        piece = feed[:2, c * units : (c + 1) * units].reshape(2, 4, units // 4, width)
        piece = jnp.swapaxes(piece, 0, 1).reshape(2 * units, width)
        w_ugs.append(piece)
        w_ds.append(feed[2, c * units : (c + 1) * units])
        piece = feed_s[:, c * units : (c + 1) * units].reshape(2, 4, units // 4)
        piece = jnp.swapaxes(piece, 0, 1).reshape(4, units // 2)
        tail = scale_row(jnp.zeros((4, HEAD_DIM)), jnp.zeros((2, HEAD_DIM)), piece, width)
        tail = jnp.concatenate([jnp.zeros((4, 2 * HEAD_DIM, width), bf16), tail], 1)
        feed_scale.append(tail.reshape(-1, width))

    mixtures, wos = [g.mixture for g in groups], [g.wo for g in groups]
    branch_other = sum_dots(mixtures, wos, count, count, bf16)
    branch_own, branch_from = sum_dots(mixtures, wos, 0, count, f32), swap(branch_other)
    hidden, hidden_round, hidden_all = rowwise(
        hidden_kernel, "hidden", [x, branch_own, branch_from, alpha[:1]], 1
    )
    hidden_all = fill(hidden_all, swap(hidden_round))
    hidden_other = hidden_all[count:]
    ugs, products = zip(
        *[up_gate(hidden_other, w, s, up_gate(hidden_round, w, s)) for w, s in zip(w_ugs, feed_scale)]
    )
    down_other = sum_dots(products, w_ds, count, count, bf16)
    down_own = sum_dots(products, w_ds, 0, count, f32)
    output, grad_hidden_res, grad_down_round, grad_down, grad_alpha_feed = rowwise(
        output_kernel,
        "output",
        [hidden, down_own, swap(down_other), alpha[1:], cotangent.reshape(count, width)],
        2,
        True,
    )
    grad_down = fill(grad_down, swap(grad_down_round))
    gugs, chunks = zip(
        *[
            feed_back(grad_down, hidden_all, w, ug, product, s)
            for w, ug, product, s in zip(w_ds, ugs, products, feed_scale)
        ]
    )
    back_other = sum_dots(gugs, w_ugs, count, count, bf16)
    back_own = sum_dots(gugs, w_ugs, 0, count, f32)
    grad_input_res, grad_branch_round, grad_branch_all, grad_alpha_attend = rowwise(
        hidden_back_kernel,
        "hidden_back",
        [x, branch_own, branch_from, alpha[:1], grad_hidden_res, back_own, swap(back_other)],
        1,
        True,
    )
    grad_branch_all = fill(grad_branch_all, swap(grad_branch_round))

    terms, term_scales = [], []
    for chunk in chunks:
        chunk = chunk.reshape(4, -1, width)
        body = chunk[:, : 3 * units // 4].reshape(4, 3, units // 4, width)
        terms.append(jnp.swapaxes(body, 0, 1).reshape(3, units, width))
        piece = chunk[:, 3 * units // 4, : units // 2].astype(f32).reshape(4, 2, units // 4)
        term_scales.append(jnp.swapaxes(piece, 0, 1).reshape(2, units))

    def scattered(values):
        return lax.psum_scatter(values, "dp", scatter_dimension=1, tiled=True)

    def both_halves(total):
        other = swap(total)
        return jnp.concatenate([pick(rank, total, other), pick(rank, other, total)], 1)

    feed_grad = both_halves(scattered(jnp.concatenate(terms, 1)).astype(f32))
    feed_grad_s = both_halves(scattered(jnp.concatenate(term_scales, 1)))

    grad_qkvs, gscales, pieces = [], [], []
    for group in groups:
        grad_qkv, keep, send = group.back(grad_branch_all, x_all)
        keep, send = jnp.concatenate(keep, 0), jnp.concatenate(send, 0)
        halves = jnp.stack([pick(rank, keep, send), pick(rank, send, keep)]).reshape(2, 4, ROWS, width)
        scale = jnp.sum(halves[:, :, 2 * HEAD_DIM].astype(f32), 0)
        scale = jnp.concatenate([scale[:, : HEAD_DIM // 2], scale[:, HEAD_DIM : 3 * HEAD_DIM // 2]], 1)
        halves = halves[:, :, : 2 * HEAD_DIM].reshape(2, 4, 4, HEAD_DIM // 2, width)
        pieces.append(jnp.transpose(halves, (2, 1, 0, 3, 4)).reshape(4, 4 * HEAD_DIM, width))
        grad_qkvs.append(grad_qkv)
        gscales.append(scale.reshape(1, -1))
    w_flats = [g.w.reshape(-1, width) for g in groups]
    input_other = sum_dots(grad_qkvs, w_flats, count, count, bf16)
    input_own = sum_dots(grad_qkvs, w_flats, 0, count, f32)
    input_grad = grad_input_res + input_own + swap(input_other).astype(f32)

    total = jnp.zeros((4, width, width), bf16)
    total = scattered(lax.dynamic_update_slice(total, jnp.concatenate(pieces, 1), (0, rank * half, 0)))
    attend_grad = total.astype(f32) + swap(total.astype(f32))
    qk = jnp.zeros((1, width), f32)
    qk = lax.dynamic_update_slice(qk, jnp.concatenate(gscales, 1), (0, rank * half))
    total = jnp.concatenate(
        [qk, jnp.sum(grad_alpha_attend, 0)[None], jnp.sum(grad_alpha_feed, 0)[None]], 0
    )
    total = scattered(total)
    attend_grad_s = total + swap(total)
    return (
        output.reshape(tokens.shape),
        input_grad.reshape(tokens.shape),
        attend_grad,
        feed_grad,
        attend_grad_s,
        feed_grad_s,
        adam_rows(attention_weights, attend_grad, attention_first, attention_second),
        adam_rows(feed_weights, feed_grad, feed_first, feed_second),
        adam_change(attention_scales, attend_grad_s, attention_scale_first, attention_scale_second, False),
        adam_change(feed_scales, feed_grad_s, feed_scale_first, feed_scale_second, False),
    )


def solution(mesh):
    rows = P("dp", "seq", None)
    matrix = P(None, "dp", None)
    scale = P(None, "dp")
    return jax.shard_map(
        local_sixteen if mesh.shape["dp"] == HEADS else local_any,
        mesh=mesh,
        in_specs=(rows, P("dp", None), rows, matrix, matrix, scale, scale)
        + (matrix,) * 4
        + (scale,) * 4,
        out_specs=(rows, rows, matrix, matrix, scale, scale, matrix, matrix, scale, scale),
        check_vma=False,
    )
```

```python
import functools
import math

import jax
import jax.numpy as jnp
from jax import lax
from jax.experimental import pallas as pl
from jax.experimental.pallas import tpu as pltpu
from jax.sharding import PartitionSpec as P

HEADS = 16
HEAD_DIM = 64
PAIR = 2 * HEAD_DIM
BLOCK = 256
ROWS = 4 * (HEAD_DIM // 2) + 16

norm_eps = 1e-06
rope_base = 10000.0
learn_rate = 0.003
beta_one = 0.9
beta_two = 0.95
adam_eps = 1e-08
corr_one = 1.0 - 0.9**10
corr_two = 1.0 - 0.95**10
apart = 1024.0

bf16 = jnp.bfloat16
f32 = jnp.float32
NT = (((1,), (1,)), ((), ()))
NN = (((1,), (0,)), ((), ()))
TN = (((0,), (0,)), ((), ()))
MIB = 1024 * 1024
SMALL = pl.CostEstimate(flops=1, bytes_accessed=1, transcendentals=0)
ROOM = pltpu.CompilerParams(vmem_limit_bytes=40 * MIB)


def made(shape, dtype):
    return pltpu.HBM(shape, dtype)


def far(*arrays):
    return [pltpu.with_memory_space_constraint(a, pltpu.HBM) for a in arrays]


def dot(a, b, dims=NN, precision=None):
    return lax.dot_general(a, b, dims, precision=precision, preferred_element_type=f32)


def tie(*values):
    return lax.optimization_barrier(values)


def swap(x):
    return lax.ppermute(x, "seq", [(0, 1), (1, 0)])


def via(x, bits):
    count = lax.axis_size("dp")
    return lax.ppermute(x, "dp", [(i, i ^ bits) for i in range(count)])


def upper_half(x):
    return x[: x.shape[0] // 2]


def lower_half(x):
    return x[x.shape[0] // 2 :]


def join_kernel(steps, *refs):
    for k in range(len(refs) - 1):

        @pl.when(pl.program_id(0) // steps == k)
        def _():
            refs[-1][...] = refs[k][...]


def join(*parts):
    rows, width = parts[0].shape
    steps = max(1, rows // 256)
    tile = rows // steps

    def spec(k):
        return pl.BlockSpec((tile, width), lambda t: (jnp.clip(t - k * steps, 0, steps - 1), 0))

    return pl.pallas_call(
        functools.partial(join_kernel, steps),
        grid=(len(parts) * steps,),
        in_specs=[spec(k) for k in range(len(parts))],
        out_specs=pl.BlockSpec((tile, width), lambda t: (t, 0)),
        out_shape=made((len(parts) * rows, width), parts[0].dtype),
        compiler_params=ROOM,
        cost_estimate=SMALL,
        name="join",
    )(*parts)


def fill_kernel(whole_ref, part_ref, out_ref):
    out_ref[...] = part_ref[...]


def fill(target, part):
    rows, width = part.shape
    tile = rows // 2
    return pl.pallas_call(
        fill_kernel,
        grid=(2,),
        in_specs=[pl.BlockSpec(memory_space=pl.ANY), pl.BlockSpec((tile, width), lambda t: (t, 0))],
        out_specs=pl.BlockSpec((tile, width), lambda t: (t + 2, 0)),
        out_shape=made(target.shape, target.dtype),
        input_output_aliases={0: 0},
        compiler_params=ROOM,
        cost_estimate=SMALL,
        name="fill",
    )(target, part)


def half_kernel(x_ref, out_ref):
    out_ref[...] = x_ref[...]


def half_of(x, lower):
    rows, width = x.shape[0] // 4, x.shape[1]
    at = 2 if lower else 0
    return pl.pallas_call(
        half_kernel,
        grid=(2,),
        in_specs=[pl.BlockSpec((rows, width), lambda t: (t + at, 0))],
        out_specs=pl.BlockSpec((rows, width), lambda t: (t, 0)),
        out_shape=made((2 * rows, width), x.dtype),
        compiler_params=ROOM,
        cost_estimate=SMALL,
        name="half",
    )(x)


def diagonal_in(by_x, by_y):
    return via(half_of(by_y, False), 1), via(half_of(by_x, True), 2)


def plus(a, b):
    return (a.astype(f32) + b.astype(f32)).astype(bf16)


def add_half_kernel(a_ref, b_ref, o_ref):
    o_ref[...] = plus(a_ref[...], b_ref[...])


def add_half(x, part, lower):
    rows, width = part.shape
    tile = rows // 2
    at = 2 if lower else 0
    return pl.pallas_call(
        add_half_kernel,
        grid=(2,),
        in_specs=[
            pl.BlockSpec((tile, width), lambda t: (t + at, 0)),
            pl.BlockSpec((tile, width), lambda t: (t, 0)),
        ],
        out_specs=pl.BlockSpec((tile, width), lambda t: (t + at, 0)),
        out_shape=made(x.shape, x.dtype),
        input_output_aliases={0: 0},
        compiler_params=ROOM,
        cost_estimate=SMALL,
        name="add_half",
    )(x, part)


def column_kernel(own_ref, x_ref, y_ref, *outs):
    total = own_ref[...].astype(f32) + x_ref[...].astype(f32) + y_ref[...].astype(f32)
    for k in range(4):

        @pl.when(pl.program_id(0) == k)
        def _():
            if k < 3 or len(outs) == 4:
                outs[k][...] = total.astype(outs[k].dtype)
            else:
                cut = outs[3].shape[0]
                outs[3][...] = total[:cut].astype(bf16)
                outs[4][...] = total[cut:].astype(bf16)


def column_sum(own, from_x, from_y, cut=0):
    rows, width = own.shape[0] // 4, own.shape[1]
    sizes = [rows] * 4 if cut == 0 else [rows] * 3 + [cut, rows - cut]
    block = pl.BlockSpec((rows, width), lambda t: (t, 0))
    mine, *parts = pl.pallas_call(
        column_kernel,
        grid=(4,),
        in_specs=[block] * 3,
        out_specs=[whole((size, width)) for size in sizes],
        out_shape=[made((rows, width), f32)] + [made((size, width), bf16) for size in sizes[1:]],
        compiler_params=ROOM,
        cost_estimate=SMALL,
        name="column_sum",
    )(own, from_x, from_y)
    return mine, parts


def z_sum(mine, parts):
    for part in parts:
        mine = mine + part.astype(f32)
    return mine


def slot_of(offset):
    return (offset & 3) * 4 + (offset >> 2)


def of_first(shape, dim):
    return (lax.broadcasted_iota(jnp.int32, shape, dim) & 32) == 0


def head_sums(x, same):
    high = x.astype(bf16)
    low = (x - high.astype(f32)).astype(bf16)
    return dot(high, same) + dot(low, same)


def same_head():
    same = of_first((PAIR, PAIR), 0) == of_first((PAIR, PAIR), 1)
    return jnp.where(same, 1.0, 0.0).astype(bf16)


def turned_unit(raw, cosine, sine, same):
    turned = raw * cosine + pltpu.roll(raw, HEAD_DIM, 1) * sine
    scale = lax.rsqrt(head_sums(turned * turned, same) + norm_eps)
    return turned * scale, scale


def local_rows(block, half_blocks, rank):
    count = 2 * half_blocks
    return pl.multiple_of(lax.rem(block + half_blocks * rank, count) * BLOCK, BLOCK)


def attend_kernel(
    info, x_ref, a_ref, b_ref, a_other, b_other, cos_ref, sin_ref, qa_ref, ka_ref,
    w_ref, wo_ref, scale_ref, raw_ref, q_ref, k_ref, v_ref, mix_ref, inv_ref,
    q_aug, k_aug,
):
    blocks = x_ref.shape[0] // BLOCK
    rank = info[blocks]
    part = HEAD_DIM // 2

    def assemble(halves):
        for t, ref in enumerate(halves):
            for head in range(2):
                for m in range(4):
                    source = slice(head * ROWS + m * part, head * ROWS + (m + 1) * part)
                    at = t * HEAD_DIM + head * part
                    if m < 3:
                        w_ref[0, m * PAIR + at : m * PAIR + at + part, :] = ref[source, :]
                    else:
                        wo_ref[at : at + part, :] = ref[source, :]
        rows = [
            halves[0][head * ROWS + 4 * part : (head + 1) * ROWS, :PAIR].astype(f32)[:8] for head in range(2)
        ]
        scales = jnp.where(of_first((8, PAIR), 1), rows[0], pltpu.roll(rows[1], 32, 1))
        scale_ref[0] = scales[:1]

    pl.when(rank == 0)(functools.partial(assemble, (a_ref, a_other)))
    pl.when(rank != 0)(functools.partial(assemble, (b_other, b_ref)))

    first = of_first((BLOCK, PAIR), 1)
    tall = 2 * BLOCK if blocks % 2 == 0 else BLOCK
    first_tall = of_first((tall, PAIR), 1)
    same = same_head()

    def project(t, carry):
        rows = pl.ds(pl.multiple_of(t * tall, tall), tall)
        raw = dot(x_ref[rows, :], w_ref[0], NT)
        raw_ref[rows, :] = raw[:, : 2 * PAIR]
        v_ref[rows, :] = raw[:, 2 * PAIR :].astype(bf16)
        cosine, sine = cos_ref[rows, :], sin_ref[rows, :]
        scale = scale_ref[0]
        q = (turned_unit(raw[:, :PAIR], cosine, sine, same)[0] * scale).astype(bf16)
        k = (turned_unit(raw[:, PAIR : 2 * PAIR], cosine, sine, same)[0] * scale).astype(bf16)
        q_ref[rows, :] = q
        k_ref[rows, :] = k
        q8 = q * jnp.asarray(8.0, bf16)
        qa, ka = qa_ref[rows, :], ka_ref[rows, :]
        q_aug[0, rows, :] = jnp.where(first_tall, q8, qa)
        q_aug[1, rows, :] = jnp.where(first_tall, qa, q8)
        k_aug[0, rows, :] = jnp.where(first_tall, k, ka)
        k_aug[1, rows, :] = jnp.where(first_tall, ka, k)
        return carry

    lax.fori_loop(0, blocks * BLOCK // tall, project, 0)

    row = lax.broadcasted_iota(jnp.int32, (BLOCK, BLOCK), 0)
    col = lax.broadcasted_iota(jnp.int32, (BLOCK, BLOCK), 1)
    causal = col <= row

    def query_block(g, carry):
        q_rows = pl.ds(local_rows(g, blocks // 2, rank), BLOCK)
        count = g - info[g] + 1

        def variant(nk):
            mixed = []
            k_rows = [pl.ds(local_rows(g - (nk - 1) + j, blocks // 2, rank), BLOCK) for j in range(nk)]
            for h in range(2):
                q = q_aug[h, q_rows, :]
                lacc = acc = None
                for j in range(nk):
                    p = jnp.exp(dot(q, k_aug[h, k_rows[j], :], NT))
                    if j == nk - 1:
                        p = jnp.where(causal, p, 0.0)
                    part = p[:, :PAIR] + p[:, PAIR:]
                    lacc = part if lacc is None else lacc + part
                    part = dot(p.astype(bf16), v_ref[k_rows[j], :])
                    acc = part if acc is None else acc + part
                inverse = 1.0 / jnp.sum(lacc, axis=1, keepdims=True)
                inv_ref[0, h : h + 1, q_rows] = 1.0 / jnp.sum(lacc.T, axis=0, keepdims=True)
                mixed.append(acc * inverse)
            mix_ref[q_rows, :] = jnp.where(first, mixed[0], mixed[1]).astype(bf16)

        for nk in range(1, 5):
            pl.when(count == nk if nk < 4 else count >= 4)(functools.partial(variant, nk))
        return carry

    lax.fori_loop(0, blocks, query_block, 0)


def whole(shape):
    return pl.BlockSpec(shape, lambda p: (0,) * len(shape))


def attend_forward(info, x_all, parts, cosine, sine, qa, ka):
    tokens, width = x_all.shape
    pairs = 2
    feats = pairs * PAIR
    by_pair = pl.BlockSpec((tokens, PAIR), lambda p: (0, p))
    return pl.pallas_call(
        attend_kernel,
        grid=(pairs,),
        in_specs=[
            pl.BlockSpec(memory_space=pltpu.SMEM),
            whole((tokens, width)),
        ]
        + [pl.BlockSpec((2 * ROWS, width), lambda p: (p, 0))] * 4
        + [
            whole((tokens, PAIR)),
            whole((tokens, PAIR)),
            whole((tokens, PAIR)),
            whole((tokens, PAIR)),
        ],
        out_specs=[
            pl.BlockSpec((1, 3 * PAIR, width), lambda p: (p, 0, 0)),
            pl.BlockSpec((PAIR, width), lambda p: (p, 0)),
            pl.BlockSpec((1, 1, PAIR), lambda p: (p, 0, 0)),
            pl.BlockSpec((tokens, 2 * PAIR), lambda p: (0, p)),
            by_pair,
            by_pair,
            by_pair,
            by_pair,
            pl.BlockSpec((1, 8, tokens), lambda p: (p, 0, 0)),
        ],
        out_shape=[
            made((pairs, 3 * PAIR, width), bf16),
            made((feats, width), bf16),
            made((pairs, 1, PAIR), f32),
            made((tokens, 2 * feats), f32),
            made((tokens, feats), bf16),
            made((tokens, feats), bf16),
            made((tokens, feats), bf16),
            made((tokens, feats), bf16),
            made((pairs, 8, tokens), f32),
        ],
        scratch_shapes=[
            pltpu.VMEM((2, tokens, PAIR), bf16),
            pltpu.VMEM((2, tokens, PAIR), bf16),
        ],
        compiler_params=ROOM,
        cost_estimate=SMALL,
        name="attend_forward",
    )(info, *far(x_all), *parts, *far(cosine, sine, qa, ka))


def attend_back_kernel(
    info, q_ref, k_ref, v_ref, gb_ref, x_ref, wo_ref, mix_ref, inv_ref, raw_ref, cos_ref, sin_ref, scale_ref,
    qa_ref, ka_ref,
    grad_ref, keep_0, keep_1, send_0, send_1,
    q_aug, k_aug, do_h, q_h, kt_h, delta, dq_acc, dk_acc, dv_acc, dw_acc,
):
    blocks = q_ref.shape[0] // BLOCK
    rank = info[blocks]
    first = of_first((BLOCK, PAIR), 1)
    first_rows = of_first((PAIR, BLOCK), 0)
    zero = jnp.zeros((BLOCK, PAIR), bf16)
    eight = jnp.asarray(8.0, bf16)
    same = same_head()

    def prepare(t, carry):
        start = pl.multiple_of(t * BLOCK, BLOCK)
        rows = pl.ds(start, BLOCK)
        q8 = q_ref[rows, :] * eight
        k = k_ref[rows, :]
        qa, ka = qa_ref[rows, :], ka_ref[rows, :]
        q_aug[0, rows, :] = jnp.where(first, q8, qa)
        q_aug[1, rows, :] = jnp.where(first, qa, q8)
        k_aug[0, rows, :] = jnp.where(first, k, ka)
        k_aug[1, rows, :] = jnp.where(first, ka, k)
        q_h[0, rows, :] = jnp.where(first, q8, zero)
        q_h[1, rows, :] = jnp.where(first, zero, q8)
        k_t = (k * eight).astype(f32).T
        kt_h[0, :, rows] = jnp.where(first_rows, k_t, 0.0).astype(bf16)
        kt_h[1, :, rows] = jnp.where(first_rows, 0.0, k_t).astype(bf16)
        grad = dot(gb_ref[rows, :], wo_ref[...], NT).astype(bf16)
        do_h[0, rows, :] = jnp.where(first, grad, zero)
        do_h[1, rows, :] = jnp.where(first, zero, grad)
        inner = (grad.astype(f32) * mix_ref[rows, :].astype(f32)).T
        inner = inner[:HEAD_DIM] + inner[HEAD_DIM:]
        delta[0:1, rows] = jnp.sum(inner[: HEAD_DIM // 2], axis=0, keepdims=True)
        delta[1:2, rows] = jnp.sum(inner[HEAD_DIM // 2 :], axis=0, keepdims=True)
        dk_acc[rows, :] = jnp.zeros((BLOCK, PAIR), f32)
        dv_acc[rows, :] = jnp.zeros((BLOCK, PAIR), f32)
        return carry

    lax.fori_loop(0, blocks, prepare, 0)

    row = lax.broadcasted_iota(jnp.int32, (BLOCK, BLOCK), 0)
    col = lax.broadcasted_iota(jnp.int32, (BLOCK, BLOCK), 1)
    causal = row <= col

    def query_block(g, carry):
        q_rows = pl.ds(local_rows(g, blocks // 2, rank), BLOCK)
        count = g - info[g] + 1

        def variant(nk):
            dq_t = None
            for j in range(nk):
                k_rows = pl.ds(local_rows(g - (nk - 1) + j, blocks // 2, rank), BLOCK)
                dk = dv = None
                for h in range(2):
                    scores = dot(k_aug[h, k_rows, :], q_aug[h, q_rows, :], NT)
                    p = jnp.exp(scores) * inv_ref[0, h : h + 1, q_rows]
                    if j == nk - 1:
                        p = jnp.where(causal, p, 0.0)
                    dp = dot(v_ref[k_rows, :], do_h[h, q_rows, :], NT)
                    ds = (p * (dp - delta[h : h + 1, q_rows])).astype(bf16)
                    dv_part = dot(p.astype(bf16), do_h[h, q_rows, :])
                    dk_part = dot(ds, q_h[h, q_rows, :])
                    dq_part = dot(kt_h[h, :, k_rows], ds)
                    dv = dv_part if dv is None else dv + dv_part
                    dk = dk_part if dk is None else dk + dk_part
                    dq_t = dq_part if dq_t is None else dq_t + dq_part
                dv_acc[k_rows, :] += dv
                dk_acc[k_rows, :] += dk
            dq_acc[q_rows, :] = dq_t.T

        for nk in range(1, 5):
            pl.when(count == nk if nk < 4 else count >= 4)(functools.partial(variant, nk))
        return carry

    lax.fori_loop(0, blocks, query_block, 0)

    tall = 2 * BLOCK if blocks % 2 == 0 else BLOCK

    def unturn(t, total):
        rows = pl.ds(pl.multiple_of(t * tall, tall), tall)
        cosine, sine = cos_ref[rows, :], sin_ref[rows, :]
        scale = scale_ref[0]
        for which, acc in ((0, dq_acc), (1, dk_acc)):
            raw = raw_ref[rows, which * PAIR : (which + 1) * PAIR]
            unit, size = turned_unit(raw, cosine, sine, same)
            grad = acc[rows, :]
            total = total + jnp.sum((grad * unit).reshape(tall // 8, 8, PAIR), axis=0)
            grad_unit = grad * scale
            grad_turned = size * (grad_unit - unit * head_sums(unit * grad_unit, same))
            grad_raw = grad_turned * cosine - pltpu.roll(grad_turned, HEAD_DIM, 1) * sine
            grad_ref[rows, which * PAIR : (which + 1) * PAIR] = grad_raw.astype(bf16)
        grad_ref[rows, 2 * PAIR :] = dv_acc[rows, :].astype(bf16)
        return total

    total = lax.fori_loop(0, blocks * BLOCK // tall, unturn, jnp.zeros((8, PAIR), f32))
    scale_row = jnp.sum(total, axis=0, keepdims=True)

    dw_acc[...] = jnp.zeros_like(dw_acc)

    def row_grads(t, carry):
        rows = pl.ds(pl.multiple_of(t * tall, tall), tall)
        dw_acc[: 3 * PAIR, :] += dot(grad_ref[rows, :], x_ref[rows, :], TN)
        dw_acc[3 * PAIR :, :] += dot(mix_ref[rows, :], gb_ref[rows, :], TN)
        return carry

    lax.fori_loop(0, blocks * BLOCK // tall, row_grads, 0)
    part = HEAD_DIM // 2

    pair = pl.program_id(0)

    def deal(keep, send):
        for half, out in enumerate((keep, send)):
            for head in range(2):
                base = head * ROWS
                for m in range(4):
                    for t in range(2):

                        @pl.when((rank == t) == (half == 0))
                        def _():
                            at = m * PAIR + t * HEAD_DIM + head * part
                            out[base + m * part : base + (m + 1) * part, :] = dw_acc[at : at + part, :].astype(bf16)

                tail = slice(base + 4 * part, base + ROWS)
                out[tail, :] = jnp.zeros((ROWS - 4 * part, out.shape[1]), bf16)
                if half == 0:
                    row = scale_row if head == 0 else pltpu.roll(jnp.broadcast_to(scale_row, (8, PAIR)), 96, 1)[:1]
                    rows = ROWS - 4 * part
                    top = lax.broadcasted_iota(jnp.int32, (rows, PAIR), 0) == 0
                    out[tail, :PAIR] = jnp.where(top, jnp.broadcast_to(row, (rows, PAIR)), 0.0).astype(bf16)

    pl.when(pair == 0)(functools.partial(deal, keep_0, send_0))
    pl.when(pair == 1)(functools.partial(deal, keep_1, send_1))


def attend_backward(info, q, k, v, grad_branch, x, wo, mixture, inverse, raw, cosine, sine, scale, qa, ka):
    tokens, feats = q.shape
    width = x.shape[1]
    pairs = feats // PAIR
    by_pair = pl.BlockSpec((tokens, PAIR), lambda p: (0, p))
    half = pltpu.VMEM((2, tokens, PAIR), bf16)
    acc = pltpu.VMEM((tokens, PAIR), f32)
    return pl.pallas_call(
        attend_back_kernel,
        grid=(pairs,),
        in_specs=[
            pl.BlockSpec(memory_space=pltpu.SMEM),
            by_pair,
            by_pair,
            by_pair,
            whole((tokens, width)),
            whole((tokens, width)),
            pl.BlockSpec((PAIR, width), lambda p: (p, 0)),
            by_pair,
            pl.BlockSpec((1, 8, tokens), lambda p: (p, 0, 0)),
            pl.BlockSpec((tokens, 2 * PAIR), lambda p: (0, p)),
            whole((tokens, PAIR)),
            whole((tokens, PAIR)),
            pl.BlockSpec((1, 1, PAIR), lambda p: (p, 0, 0)),
            whole((tokens, PAIR)),
            whole((tokens, PAIR)),
        ],
        out_specs=[
            pl.BlockSpec((tokens, 3 * PAIR), lambda p: (0, p)),
        ]
        + [whole((2 * ROWS, width))] * 4,
        out_shape=[made((tokens, 3 * feats), bf16)] + [made((2 * ROWS, width), bf16)] * 4,
        scratch_shapes=[
            half,
            half,
            half,
            half,
            pltpu.VMEM((2, PAIR, tokens), bf16),
            pltpu.VMEM((8, tokens), f32),
            acc,
            acc,
            acc,
            pltpu.VMEM((4 * PAIR, width), f32),
        ],
        compiler_params=ROOM,
        cost_estimate=SMALL,
        name="attend_backward",
    )(info, *far(q, k, v, grad_branch, x, wo, mixture, inverse, raw, cosine, sine), scale, *far(qa, ka))


def slot_scale(ref, group):
    return ref[:, 2 * PAIR : 2 * PAIR + 2 * group].astype(f32)[:1]


def scale_specs(width):
    return [pl.BlockSpec((16, width), lambda t, n=n: ((n * ROWS + 2 * HEAD_DIM) // 16, 0)) for n in range(4)]


def up_gate_kernel(h_ref, *refs):
    *w_refs, s_0, s_1, s_2, s_3, ug_ref, product_ref = refs
    group = product_ref.shape[1] // 4
    per = 4 // len(w_refs)
    for k in range(4):
        pair = slice(2 * k * group, 2 * (k + 1) * group)
        at = 2 * (k % per) * group
        both = dot(h_ref[...], w_refs[k // per][at : at + 2 * group, :], NT)
        ug_ref[:, pair] = both.astype(bf16)
        scaled = both * slot_scale((s_0, s_1, s_2, s_3)[k], group)
        gated = scaled[:, group:]
        product = scaled[:, :group] * gated / (1.0 + jnp.exp(-gated))
        product_ref[:, k * group : (k + 1) * group] = product.astype(bf16)


def tile_of(tokens):
    return 512 if tokens % 512 == 0 else 256


def up_gate(hidden, w, scale, before=None):
    tokens, width = hidden.shape
    w = w if isinstance(w, tuple) else (w,)
    units = w[0].shape[0] * len(w) // 2
    tile = tokens // 2
    at = 0 if before is None else 2
    more = [] if before is None else list(before)
    inputs = 5 + len(w)

    def kernel(*refs):
        up_gate_kernel(*refs[:inputs], *refs[inputs + len(more) :])

    return pl.pallas_call(
        kernel,
        grid=(2,),
        in_specs=[
            pl.BlockSpec((tile, width), lambda t: (t, 0)),
        ]
        + [whole(part.shape) for part in w]
        + scale_specs(width)
        + [pl.BlockSpec(memory_space=pl.ANY)] * len(more),
        out_specs=[
            pl.BlockSpec((tile, 2 * units), lambda t: (t + at, 0)),
            pl.BlockSpec((tile, units), lambda t: (t + at, 0)),
        ],
        out_shape=[made((2 * tokens, 2 * units), bf16), made((2 * tokens, units), bf16)],
        input_output_aliases={inputs + n: n for n in range(len(more))},
        compiler_params=ROOM,
        cost_estimate=SMALL,
        name="up_gate",
    )(hidden, *w, *[scale] * 4, *more)


def feed_back_kernel(
    count, grad_ref, h_ref, *rest
):
    w_refs, rest = rest[:count], rest[count:]
    ug_ref, product_ref, s_0, s_1, s_2, s_3, gug_ref, *dws, ug_acc, d_acc, gscale = rest
    group = product_ref.shape[1] // 4
    per_w, per = 4 // count, 4 // len(dws)
    step = pl.program_id(0)

    @pl.when(step == 0)
    def _():
        gscale[...] = jnp.zeros_like(gscale)
        ug_acc[...] = jnp.zeros_like(ug_acc)
        d_acc[...] = jnp.zeros_like(d_acc)

    rows = grad_ref.shape[0] // 8
    d_acc[...] += dot(product_ref[...], grad_ref[...], TN)
    for k in range(4):
        ups = slice(2 * k * group, (2 * k + 1) * group)
        gates = slice((2 * k + 1) * group, (2 * k + 2) * group)
        at = (k % per_w) * group
        grad = dot(grad_ref[...], w_refs[k // per_w][at : at + group, :], NT)
        up = ug_ref[:, ups].astype(f32)
        gate = ug_ref[:, gates].astype(f32)
        scales = slot_scale((s_0, s_1, s_2, s_3)[k], group)
        up_scale, gate_scale = scales[:, :group], scales[:, group:]
        gated = gate * gate_scale
        sig = 1.0 / (1.0 + jnp.exp(-gated))
        silu = gated * sig
        through = grad * silu
        grad_gated = grad * (up * up_scale) * (sig + silu * (1.0 - sig))
        gug_ref[:, ups] = (through * up_scale).astype(bf16)
        gug_ref[:, gates] = (grad_gated * gate_scale).astype(bf16)
        gscale[:, ups] += jnp.sum((through * up).reshape(rows, 8, group), axis=0)
        gscale[:, gates] += jnp.sum((grad_gated * gate).reshape(rows, 8, group), axis=0)
    ug_acc[...] += dot(gug_ref[...], h_ref[...], TN)

    @pl.when(step == pl.num_programs(0) - 1)
    def _():
        top = lax.broadcasted_iota(jnp.int32, (16, 2 * group), 0) == 0
        for k in range(4):
            out, at = dws[k // per], (k % per) * (3 * group + 16)
            out[at : at + 2 * group, :] = ug_acc[2 * k * group : 2 * (k + 1) * group, :].astype(bf16)
            out[at + 2 * group : at + 3 * group, :] = d_acc[k * group : (k + 1) * group, :].astype(bf16)
            sums = jnp.sum(gscale[:, 2 * k * group : 2 * (k + 1) * group], axis=0, keepdims=True)
            tail = slice(at + 3 * group, at + 3 * group + 16)
            out[tail, :] = jnp.zeros((16, out.shape[1]), bf16)
            out[tail, : 2 * group] = jnp.where(top, jnp.broadcast_to(sums, top.shape), 0.0).astype(bf16)


def feed_back(grad, hidden, w, ug, product, scale, pieces=1):
    tokens, width = grad.shape
    w = pieces_of(w)
    units = product.shape[1]
    tile = tile_of(tokens)
    row = pl.BlockSpec((tile, width), lambda t: (t, 0))
    wide = pl.BlockSpec((tile, 2 * units), lambda t: (t, 0))
    rows = (units * 3 + 64) // pieces
    return pl.pallas_call(
        functools.partial(feed_back_kernel, len(w)),
        grid=(tokens // tile,),
        in_specs=[
            row,
            row,
            *[pl.BlockSpec((size, width), lambda t, n=at // size: (n, 0)) for _, at, size in w],
            wide,
            pl.BlockSpec((tile, units), lambda t: (t, 0)),
        ]
        + scale_specs(width),
        out_specs=[wide] + [whole((rows, width))] * pieces,
        out_shape=[made((tokens, 2 * units), bf16)] + [made((rows, width), bf16)] * pieces,
        scratch_shapes=[
            pltpu.VMEM((2 * units, width), f32),
            pltpu.VMEM((units, width), f32),
            pltpu.VMEM((8, 2 * units), f32),
        ],
        compiler_params=ROOM,
        cost_estimate=SMALL,
        name="feed_back",
    )(*far(grad, hidden), *[array for array, _, _ in w], *far(ug, product), *[scale] * 4)


def pieces_of(right):
    right = right if isinstance(right, tuple) else (right,)
    return [p if isinstance(p, tuple) else (p, 0, p.shape[0]) for p in right]


def sum_dots_kernel(lefts, plan, start, tile, *refs):
    arrays = lefts + 1 + max(piece[0] for pieces in plan for piece in pieces)
    has = len(refs) - arrays - 3 - 2 * lefts
    addend = refs[arrays] if has else None
    out, acc, *bufs, sems = refs[arrays + has :]
    rows = out.shape[0]
    copies, used = [], 0
    for n, pieces in enumerate(plan):
        group = [pltpu.make_async_copy(refs[n].at[pl.ds(start, rows), :], bufs[2 * n], sems.at[used])]
        used, to = used + 1, 0
        for index, at, size in pieces:
            source = refs[lefts + index].at[pl.ds(at, size), :]
            group.append(pltpu.make_async_copy(source, bufs[2 * n + 1].at[pl.ds(to, size), :], sems.at[used]))
            used, to = used + 1, to + size
        copies.append(group)
    for group in copies:
        for copy in group:
            copy.start()
    last = lefts - 1
    for n, group in enumerate(copies):
        for copy in group:
            copy.wait()
        for r in range(0, rows, tile):
            here = slice(r, r + tile)
            part = dot(bufs[2 * n][here, :], bufs[2 * n + 1][...])
            if n > 0:
                part = part + acc[here, :]
            elif addend is not None:
                part = part + addend[here, :].astype(f32)
            if n < last:
                acc[here, :] = part
            else:
                out[here, :] = part.astype(out.dtype)


def sum_dots(lefts, rights, start, rows, dtype, addend=None):
    plan, arrays = [], []
    for right in rights:
        pieces = []
        for array, at, size in pieces_of(right):
            known = [n for n, a in enumerate(arrays) if a is array]
            if not known:
                arrays.append(array)
            pieces.append((known[0] if known else len(arrays) - 1, at, size))
        plan.append(pieces)
    width = arrays[0].shape[1]
    bufs = []
    for left in lefts:
        bufs += [pltpu.VMEM((rows, left.shape[1]), bf16), pltpu.VMEM((left.shape[1], width), bf16)]
    copies = len(lefts) + sum(len(pieces) for pieces in plan)
    more = [] if addend is None else [addend]
    far_ref = pl.BlockSpec(memory_space=pltpu.HBM)
    near = pl.BlockSpec(memory_space=pltpu.VMEM)
    return pl.pallas_call(
        functools.partial(sum_dots_kernel, len(lefts), plan, start, 256),
        in_specs=[far_ref] * (len(lefts) + len(arrays)) + [near] * len(more),
        out_specs=near,
        out_shape=made((rows, width), dtype),
        scratch_shapes=[pltpu.VMEM((rows, width), f32), *bufs, pltpu.SemaphoreType.DMA((copies,))],
        compiler_params=ROOM,
        cost_estimate=SMALL,
        name="sum_dots",
    )(*lefts, *arrays, *more)


def alpha_kernel(place, *refs):
    slots, one, two, rows = refs[:HEADS], refs[HEADS], refs[HEADS + 1], refs[HEADS + 2]
    for j in range(HEADS):
        rows[j : j + 1, :] = slots[j][:, PAIR : 2 * PAIR].astype(f32)[:1]
    low = lax.broadcasted_iota(jnp.int32, (1, PAIR), 1) < HEAD_DIM
    for k in range(HEADS // 2):
        pair = []
        for owner in (2 * k, 2 * k + 1):
            slot = slot_of(jnp.bitwise_xor(place[0], owner))
            pair.append(jnp.broadcast_to(rows[pl.ds(slot, 1), :], (8, PAIR)))
        turned = [pltpu.roll(p, HEAD_DIM, 1)[:1] for p in pair]
        lanes = slice(k * PAIR, (k + 1) * PAIR)
        one[:, lanes] = jnp.where(low, pair[0][:1], turned[1])
        two[:, lanes] = jnp.where(low, turned[0], pair[1][:1])


def alpha_rows(place, chunks):
    width = chunks[0].shape[1]
    specs = scale_specs(width)
    return pl.pallas_call(
        alpha_kernel,
        grid=(1,),
        in_specs=[pl.BlockSpec(memory_space=pltpu.SMEM)] + specs * 4,
        out_specs=[whole((1, width))] * 2,
        out_shape=[made((1, width), f32)] * 2,
        scratch_shapes=[pltpu.VMEM((HEADS, PAIR), f32)],
        compiler_params=ROOM,
        cost_estimate=SMALL,
        name="alpha",
    )(place[None].astype(jnp.int32), *(chunk for chunk in chunks for _ in range(4)))


def rms_scale(values):
    return lax.rsqrt(jnp.mean(values * values, axis=-1, keepdims=True) + norm_eps)


def blend_parts(residual, branch, mixing):
    branch_scale = rms_scale(branch)
    unit = branch * branch_scale
    step = unit - residual
    mixed = residual + mixing * step
    mixed_scale = rms_scale(mixed)
    return branch_scale, unit, step, mixed * mixed_scale, mixed_scale


def blend_grads(parts, mixing, grad):
    branch_scale, unit, step, result, mixed_scale = parts
    grad_mixed = mixed_scale * (grad - result * jnp.mean(grad * result, axis=-1, keepdims=True))
    grad_unit = mixing * grad_mixed
    grad_branch = branch_scale * (grad_unit - unit * jnp.mean(unit * grad_unit, axis=-1, keepdims=True))
    return grad_mixed - grad_unit, grad_branch, grad_mixed * step


def add_rows(ref, values):
    @pl.when(pl.program_id(0) == 0)
    def _():
        ref[...] = jnp.zeros_like(ref)

    ref[...] += jnp.sum(values.reshape(values.shape[0] // 8, 8, values.shape[1]), axis=0)


def hidden_kernel(x_ref, own_ref, other_ref, mix_ref, hidden_ref, round_ref, wide_ref):
    branch = own_ref[...] + other_ref[...].astype(f32)
    hidden = blend_parts(x_ref[...].astype(f32), branch, mix_ref[...])[3]
    hidden_ref[...] = hidden
    round_ref[...] = wide_ref[...] = hidden.astype(bf16)


def output_kernel(
    hidden_ref, own_ref, other_ref, mix_ref, cot_ref, out_ref, res_ref, down_ref, wide_ref, gmix_ref
):
    mixing = mix_ref[...]
    parts = blend_parts(hidden_ref[...], own_ref[...] + other_ref[...].astype(f32), mixing)
    out_ref[...] = parts[3]
    grad_res, grad_down, grad_mix = blend_grads(parts, mixing, cot_ref[...].astype(f32))
    res_ref[...] = grad_res
    down_ref[...] = wide_ref[...] = grad_down.astype(bf16)
    add_rows(gmix_ref, grad_mix)


def hidden_back_kernel(
    x_ref, own_ref, other_ref, mix_ref, res_ref, back_ref, from_ref, in_ref, branch_ref, wide_ref, gmix_ref
):
    mixing = mix_ref[...]
    parts = blend_parts(x_ref[...].astype(f32), own_ref[...] + other_ref[...].astype(f32), mixing)
    grad = res_ref[...] + back_ref[...] + from_ref[...].astype(f32)
    grad_res, grad_branch, grad_mix = blend_grads(parts, mixing, grad)
    in_ref[...] = grad_res
    branch_ref[...] = wide_ref[...] = grad_branch.astype(bf16)
    add_rows(gmix_ref, grad_mix)


def rowwise(kernel, name, arrays, floats, reduced=False):
    tokens, width = arrays[0].shape
    tile = 128
    row = pl.BlockSpec((tile, width), lambda t: (t, 0))
    out_shape = [made((tokens, width), f32)] * floats
    out_shape += [made((tokens, width), bf16), made((2 * tokens, width), bf16)]
    out_specs = [row] * (floats + 2)
    if reduced:
        out_shape.append(made((8, width), f32))
        out_specs.append(whole((8, width)))
    return pl.pallas_call(
        kernel,
        grid=(tokens // tile,),
        in_specs=[row if a.shape[0] == tokens else whole((1, width)) for a in arrays],
        out_specs=out_specs,
        out_shape=out_shape,
        compiler_params=ROOM,
        cost_estimate=SMALL,
        name=name,
    )(*(far(a)[0] if a.dtype == f32 and a.shape[0] == tokens else a for a in arrays))


def adam_change(weight, gradient, moment_one, moment_two, renormalize):
    moment_one_new = beta_one * moment_one + (1.0 - beta_one) * gradient
    moment_two_new = beta_two * moment_two + (1.0 - beta_two) * gradient * gradient
    stepped = weight - learn_rate * (moment_one_new / corr_one) / (
        jnp.sqrt(moment_two_new / corr_two) + adam_eps
    )
    if renormalize:
        stepped = stepped * lax.rsqrt(jnp.sum(stepped * stepped, axis=-1, keepdims=True) + norm_eps)
    return stepped - weight


def adam_kernel(w_ref, g_ref, one_ref, two_ref, out_ref):
    out_ref[...] = adam_change(w_ref[...], g_ref[...], one_ref[...], two_ref[...], True)


def adam_rows(weight, gradient, moment_one, moment_two):
    shape = weight.shape
    rows, width = shape[0] * shape[1], shape[2]
    tile = next(t for t in (128, 64, 32, 16, 8) if rows % t == 0)
    block = pl.BlockSpec((tile, width), lambda t: (t, 0))
    return pl.pallas_call(
        adam_kernel,
        grid=(rows // tile,),
        in_specs=[block] * 4,
        out_specs=block,
        out_shape=made((rows, width), f32),
        compiler_params=ROOM,
        cost_estimate=SMALL,
        name="adam",
    )(*far(*(a.reshape(rows, width) for a in (weight, gradient, moment_one, moment_two)))).reshape(shape)


def own_half(x, rank, axis):
    size = x.shape[axis] // 2
    return lax.dynamic_slice_in_dim(x, rank * size, size, axis)


def pick(rank, zero, one):
    return jnp.where(rank == 0, zero, one)


def document_tables(segment_ids, rank, count):
    segments = segment_ids.reshape(-1)
    docs = jnp.arange(8, dtype=jnp.int32)
    begins = jnp.sum((segments[None, :] < docs[:, None]).astype(jnp.int32), axis=1)
    is_doc = segments[:, None] == docs[None, :]
    starts = jnp.sum(jnp.where(is_doc, begins[None, :], 0), axis=1)
    info = jnp.concatenate([starts[::BLOCK] // BLOCK, rank[None].astype(jnp.int32)])
    place = jnp.arange(2 * count, dtype=jnp.int32)

    def arranged(values):
        own = lax.dynamic_slice_in_dim(values, rank * count, count, 0)
        other = lax.dynamic_slice_in_dim(values, (1 - rank) * count, count, 0)
        return jnp.concatenate([own, other], 0)

    positions = arranged(place - starts).astype(f32)
    frequency = jnp.exp(
        jnp.arange(HEAD_DIM // 2, dtype=f32) * (-2.0 * math.log(rope_base) / HEAD_DIM)
    )
    angles = positions[:, None] * jnp.tile(frequency, 4)[None, :]
    cosine = jnp.cos(angles)
    sign = jnp.where(jnp.arange(PAIR) < HEAD_DIM, -1.0, 1.0).astype(f32)
    sine = jnp.sin(angles) * sign[None, :]
    lanes = jnp.arange(PAIR, dtype=jnp.int32)
    lanes = jnp.where(lanes < HEAD_DIM, lanes & 31, 8)
    own_doc = arranged(segments)[:, None] == lanes[None, :]
    query_mark = own_doc.astype(bf16)
    key_mark = jnp.where(own_doc | (lanes >= 8)[None, :], 0.0, -apart).astype(bf16)
    return info, cosine, sine, query_mark, key_mark


def scale_row(qk, alpha, feed, width):
    count = qk.shape[0]
    gap = jnp.zeros((count, HEAD_DIM // 2), f32)
    row = [qk[:, : HEAD_DIM // 2], gap, qk[:, HEAD_DIM // 2 :], gap]
    row += [jnp.broadcast_to(alpha.reshape(1, -1), (count, PAIR)), feed.reshape(count, -1)]
    row = jnp.concatenate(row, 1).astype(bf16)
    return jnp.pad(row[:, None], ((0, 0), (0, 15), (0, width - row.shape[1])))


class Group:
    def __init__(self, tables, x_all, parts):
        self.tables = tables
        info, cosine, sine, query_mark, key_mark = tables
        (self.w, self.wo, self.scale, self.raw, self.q, self.k, self.v, self.mixture, self.inverse) = attend_forward(
            info, x_all, parts, cosine, sine, query_mark, key_mark
        )

    def back(self, grad_branch, x_all):
        info, cosine, sine, query_mark, key_mark = self.tables
        grad_qkv, *rows = attend_backward(
            info, self.q, self.k, self.v, grad_branch, x_all, self.wo, self.mixture, self.inverse, self.raw,
            cosine, sine, self.scale, query_mark, key_mark,
        )
        return grad_qkv, tuple(rows[:2]), tuple(rows[2:])


def local_sixteen(
    tokens,
    segment_ids,
    cotangent,
    attention_weights,
    feed_weights,
    attention_scales,
    feed_scales,
    attention_first,
    attention_second,
    feed_first,
    feed_second,
    attention_scale_first,
    attention_scale_second,
    feed_scale_first,
    feed_scale_second,
):
    count, width = tokens.shape[0] * tokens.shape[1], tokens.shape[-1]
    rank, place = lax.axis_index("seq"), lax.axis_index("dp")
    x = tokens.reshape(count, width)

    part = own_half(attention_weights, rank, 1).astype(bf16)
    rows = part.shape[1]
    body = 4 * rows
    extra = scale_row(attention_scales[0:1], attention_scales[1:], own_half(feed_scales, rank, 1)[None], width)
    block_a = jnp.concatenate([part.reshape(body, width), extra[0]], axis=0)
    feed_part = own_half(feed_weights, rank, 1).astype(bf16)
    units = feed_part.shape[1]
    block_u = feed_part[:2].reshape(2 * units, width)
    block_d = feed_part[2]

    z_a = [via(block_a, 4 * k) for k in (1, 2, 3)]
    x_d, y_d = via(block_d, 1), via(block_d, 2)
    x_all = jnp.concatenate([x, swap(x)], 0)
    tables = document_tables(segment_ids, rank, count)
    block_a, z_a, block_u, x_d, y_d, x_all, tables = tie(block_a, z_a, block_u, x_d, y_d, x_all, tables)

    own_a = join(block_a, *z_a)
    x_a, y_a = via(own_a, 1), via(own_a, 2)
    z_u = [via(block_u, 4), via(block_u, 8)]
    own_a, x_a, y_a, z_u, block_u, y_d, x_all = tie(own_a, x_a, y_a, z_u, block_u, y_d, x_all)

    d_a = diagonal_in(x_a, y_a)
    z_u = z_u + [via(block_u, 12)]
    d_d = via(y_d, 1)
    group_0 = Group(tables, x_all, (own_a, y_a, swap(own_a), swap(y_a)))
    d_a, z_u, block_u, d_d, group_0.mixture, x_all = tie(d_a, z_u, block_u, d_d, group_0.mixture, x_all)

    own_u = join(block_u, *z_u)
    quad = join(block_d, x_d, y_d, d_d)
    own_u, quad = tie(own_u, quad)
    x_u, y_u = via(own_u, 1), via(own_u, 2)
    z_d = [via(quad, 4), via(quad, 8)]
    d_a = join(*d_a)
    group_1 = Group(tables, x_all, (x_a, d_a, swap(x_a), swap(d_a)))
    groups = (group_0, group_1)
    mixtures, wos = [g.mixture for g in groups], [g.wo for g in groups]
    branch_other = sum_dots(mixtures, wos, count, count, bf16)
    branch_own = sum_dots(mixtures, wos, 0, count, f32)
    branch_other, branch_own, x_u, y_u, z_d, d_a = tie(branch_other, branch_own, x_u, y_u, z_d, d_a)

    d_u = diagonal_in(x_u, y_u)
    z_d3 = via(half_of(quad, False), 12)
    alpha = alpha_rows(place, (own_a, x_a, y_a, d_a))
    branch_from = swap(branch_other)
    hidden, hidden_round, hidden_all = rowwise(
        hidden_kernel, "hidden", [x, branch_own, branch_from, alpha[0]], 1
    )
    first_own = up_gate(hidden_round, own_u, own_a)
    first_x = up_gate(hidden_round, x_u, x_a)
    first_y = up_gate(hidden_round, y_u, y_a)
    d_u, z_d3, quad, hidden_round, first_own, first_x, first_y = tie(
        d_u, z_d3, quad, hidden_round, first_own, first_x, first_y
    )
    z_d4 = via(half_of(quad, True), 12)
    hidden_other = swap(hidden_round)
    hidden_all = fill(hidden_all, hidden_other)
    ug_own, product_own = up_gate(hidden_other, own_u, own_a, first_own)
    ug_x, product_x = up_gate(hidden_other, x_u, x_a, first_x)
    ug_y, product_y = up_gate(hidden_other, y_u, y_a, first_y)
    ug_d, product_d = up_gate(hidden_other, d_u, d_a, up_gate(hidden_round, d_u, d_a))
    product_own, product_x, product_y, product_d, hidden_all, z_d4 = tie(
        product_own, product_x, product_y, product_d, hidden_all, z_d4
    )

    own_d, x_d, y_d, d_d = [
        tuple((array, c * units, units) for array in (quad, *z_d)) + (((z_d3, z_d4)[c // 2], (c % 2) * units, units),)
        for c in range(4)
    ]
    products, w_ds = [product_own, product_x, product_y, product_d], [own_d, x_d, y_d, d_d]
    down_other = sum_dots(products, w_ds, count, count, bf16)
    down_own = sum_dots(products, w_ds, 0, count, f32)
    output, grad_hidden_res, grad_down_round, grad_down, grad_alpha_feed = rowwise(
        output_kernel,
        "output",
        [hidden, down_own, swap(down_other), alpha[1], cotangent.reshape(count, width)],
        2,
        True,
    )

    grad_down = fill(grad_down, swap(grad_down_round))
    gug_d, *r_d = feed_back(grad_down, hidden_all, d_d, ug_d, product_d, d_a, 2)
    r_d, grad_down, product_x, product_y, product_own = tie(r_d, grad_down, product_x, product_y, product_own)
    t_d = via(r_d[0], 1), via(r_d[1], 2)
    gug_x, r_x = feed_back(grad_down, hidden_all, x_d, ug_x, product_x, x_a)
    gug_y, r_y = feed_back(grad_down, hidden_all, y_d, ug_y, product_y, y_a)
    gug_own, r_own = feed_back(grad_down, hidden_all, own_d, ug_own, product_own, own_a)
    gugs, w_ugs = [gug_own, gug_x, gug_y, gug_d], [own_u, x_u, y_u, d_u]
    t_d, r_x, r_y, r_own, gugs = tie(t_d, r_x, r_y, r_own, gugs)

    r_x, r_y = add_half(r_x, t_d[1], True), add_half(r_y, t_d[0], False)
    r_x, r_y, gugs = tie(r_x, r_y, gugs)
    v_x, v_y = via(r_x, 1), via(r_y, 2)
    back_other = sum_dots(gugs, w_ugs, count, count, bf16)
    back_from = swap(back_other)
    back_own = sum_dots(gugs, w_ugs, 0, count, f32)
    grad_input_res, grad_branch_round, grad_branch_all, grad_alpha_attend = rowwise(
        hidden_back_kernel,
        "hidden_back",
        [x, branch_own, branch_from, alpha[0], grad_hidden_res, back_own, back_from],
        1,
        True,
    )
    grad_branch_all = fill(grad_branch_all, swap(grad_branch_round))
    grad_alpha = jnp.stack([jnp.sum(grad_alpha_attend, 0), jnp.sum(grad_alpha_feed, 0)])
    alpha_from = via(grad_alpha, 4)
    grad_qkv_1, keep_1, send_1 = group_1.back(grad_branch_all, x_all)
    v_x, v_y, grad_qkv_1, keep_1, send_1, grad_branch_all, alpha_from = tie(
        v_x, v_y, grad_qkv_1, keep_1, send_1, grad_branch_all, alpha_from
    )

    grad_alpha = grad_alpha + alpha_from
    alpha_from = via(grad_alpha, 1)
    feed_mine, feed_parts = column_sum(r_own, v_x, v_y, 112)
    feed_mine, feed_parts, send_1, grad_alpha, alpha_from = tie(feed_mine, feed_parts, send_1, grad_alpha, alpha_from)
    grad_alpha = grad_alpha + alpha_from
    z_feed = [via(feed_parts[0], 4), via(feed_parts[1], 8), via(feed_parts[2], 12)]
    other_1 = swap(send_1[0]), swap(send_1[1])
    a_x = jnp.concatenate([pick(rank, k, o) for k, o in zip(keep_1, other_1)], 0)
    a_d = tuple(pick(rank, o, k) for k, o in zip(keep_1, other_1))
    a_x, a_d, grad_branch_all = tie(a_x, a_d, grad_branch_all)

    t_a = via(a_d[0], 1), via(a_d[1], 2)
    grad_qkv_0, keep_0, send_0 = group_0.back(grad_branch_all, x_all)
    t_a, z_feed, grad_qkv_0, keep_0, send_0 = tie(t_a, z_feed, grad_qkv_0, keep_0, send_0)

    z_rest = via(feed_parts[3], 12)
    other_0 = swap(send_0[0]), swap(send_0[1])
    a_own = jnp.concatenate([pick(rank, k, o) for k, o in zip(keep_0, other_0)], 0)
    a_y = [pick(rank, o, k) for k, o in zip(keep_0, other_0)]
    a_y = jnp.concatenate([plus(a_y[0], t_a[0]), a_y[1]], 0)
    a_x = add_half(a_x, t_a[1], True)
    a_x, a_y, grad_qkv_0, grad_alpha = tie(a_x, a_y, grad_qkv_0, grad_alpha)
    b_x, b_y = via(a_x, 1), via(a_y, 2)
    alpha_from = via(grad_alpha, 2)
    grad_qkvs = [grad_qkv_0, grad_qkv_1]
    w_flats = [g.w.reshape(-1, width) for g in groups]
    input_other = sum_dots(grad_qkvs, w_flats, count, count, bf16)
    input_own = sum_dots(grad_qkvs, w_flats, 0, count, f32, grad_input_res)
    input_other, input_own, b_x, b_y, z_rest, alpha_from = tie(input_other, input_own, b_x, b_y, z_rest, alpha_from)
    z_feed = [z_feed[0], z_feed[1], jnp.concatenate([z_feed[2], z_rest], 0)]
    grad_alpha = grad_alpha + alpha_from
    alpha_from = via(grad_alpha, 8)

    attend_mine, attend_parts = column_sum(a_own, b_x, b_y)
    attend_parts = [via(part, 4 * k) for part, k in zip(attend_parts, (1, 2, 3))]
    input_grad = input_own + swap(input_other).astype(f32)
    total = z_sum(feed_mine, z_feed)
    other = swap(total)
    low, high = pick(rank, total, other), pick(rank, other, total)
    feed_grad = jnp.concatenate([t[: 3 * units].reshape(3, units, width) for t in (low, high)], 1)
    feed_grad_s = jnp.concatenate([t[3 * units, : 2 * units].reshape(2, units) for t in (low, high)], 1)
    feed_change = adam_rows(feed_weights, feed_grad, feed_first, feed_second)
    attend_parts, alpha_from, input_grad, feed_grad, feed_change = tie(
        attend_parts, alpha_from, input_grad, feed_grad, feed_change
    )
    grad_alpha = grad_alpha + alpha_from
    grad_alpha = grad_alpha + swap(grad_alpha)
    own_alpha = lax.dynamic_slice_in_dim(grad_alpha, place * HEAD_DIM, HEAD_DIM, 1)

    total = z_sum(attend_mine, attend_parts)
    other = swap(total)
    low, high = pick(rank, total, other), pick(rank, other, total)
    attend_grad = jnp.concatenate([t[:body].reshape(4, rows, width) for t in (low, high)], 1)
    grad_qk = low[body] + high[body]
    grad_qk = jnp.concatenate([grad_qk[: HEAD_DIM // 2], grad_qk[HEAD_DIM : 3 * HEAD_DIM // 2]], 0)
    attend_grad_s = jnp.concatenate([grad_qk[None], own_alpha], 0)
    return (
        output.reshape(tokens.shape),
        input_grad.reshape(tokens.shape),
        attend_grad,
        feed_grad,
        attend_grad_s,
        feed_grad_s,
        adam_rows(attention_weights, attend_grad, attention_first, attention_second),
        feed_change,
        adam_change(attention_scales, attend_grad_s, attention_scale_first, attention_scale_second, False),
        adam_change(feed_scales, feed_grad_s, feed_scale_first, feed_scale_second, False),
    )


def local_any(
    tokens,
    segment_ids,
    cotangent,
    attention_weights,
    feed_weights,
    attention_scales,
    feed_scales,
    attention_first,
    attention_second,
    feed_first,
    feed_second,
    attention_scale_first,
    attention_scale_second,
    feed_scale_first,
    feed_scale_second,
):
    count, width = tokens.shape[0] * tokens.shape[1], tokens.shape[-1]
    rank = lax.axis_index("seq")
    x = tokens.reshape(count, width)
    x_all = jnp.concatenate([x, swap(x)], axis=0)
    tables = document_tables(segment_ids, rank, count)

    full = lax.all_gather(attention_weights.astype(bf16), "dp", axis=1, tiled=True)
    scales = lax.all_gather(attention_scales.astype(bf16), "dp", axis=1, tiled=True).astype(f32)
    half = width // 2
    alpha = scales[1:]
    mine = lax.dynamic_slice_in_dim(full, rank * half, half, 1)
    mine = jnp.swapaxes(mine.reshape(4, HEADS // 2, 2, HEAD_DIM // 2, width), 0, 1)
    own_scale = lax.dynamic_slice_in_dim(scales[0], rank * half, half, 0).reshape(HEADS // 2, HEAD_DIM)

    groups = []
    for g in range(2):
        heads = slice(4 * g, 4 * g + 4)
        tail = scale_row(own_scale[heads], jnp.zeros((2, HEAD_DIM)), jnp.zeros((4, 2 * PAIR)), width)
        low = jnp.concatenate([mine[heads, :, 0].reshape(4, -1, width), tail], 1).reshape(-1, width)
        high = jnp.concatenate([mine[heads, :, 1].reshape(4, -1, width), tail], 1).reshape(-1, width)
        groups.append(Group(tables, x_all, (low, high, high, low)))

    feed = lax.all_gather(own_half(feed_weights, rank, 1).astype(bf16), "dp", axis=1, tiled=True)
    feed_s = lax.all_gather(own_half(feed_scales, rank, 1).astype(bf16), "dp", axis=1, tiled=True).astype(f32)
    units = feed.shape[1] // 4
    w_ugs, w_ds, feed_scale = [], [], []
    for c in range(4):
        piece = feed[:2, c * units : (c + 1) * units].reshape(2, 4, units // 4, width)
        piece = jnp.swapaxes(piece, 0, 1).reshape(2 * units, width)
        w_ugs.append(piece)
        w_ds.append(feed[2, c * units : (c + 1) * units])
        piece = feed_s[:, c * units : (c + 1) * units].reshape(2, 4, units // 4)
        piece = jnp.swapaxes(piece, 0, 1).reshape(4, units // 2)
        tail = scale_row(jnp.zeros((4, HEAD_DIM)), jnp.zeros((2, HEAD_DIM)), piece, width)
        tail = jnp.concatenate([jnp.zeros((4, 2 * HEAD_DIM, width), bf16), tail], 1)
        feed_scale.append(tail.reshape(-1, width))

    mixtures, wos = [g.mixture for g in groups], [g.wo for g in groups]
    branch_other = sum_dots(mixtures, wos, count, count, bf16)
    branch_own, branch_from = sum_dots(mixtures, wos, 0, count, f32), swap(branch_other)
    hidden, hidden_round, hidden_all = rowwise(
        hidden_kernel, "hidden", [x, branch_own, branch_from, alpha[:1]], 1
    )
    hidden_all = fill(hidden_all, swap(hidden_round))
    hidden_other = hidden_all[count:]
    ugs, products = zip(
        *[up_gate(hidden_other, w, s, up_gate(hidden_round, w, s)) for w, s in zip(w_ugs, feed_scale)]
    )
    down_other = sum_dots(products, w_ds, count, count, bf16)
    down_own = sum_dots(products, w_ds, 0, count, f32)
    output, grad_hidden_res, grad_down_round, grad_down, grad_alpha_feed = rowwise(
        output_kernel,
        "output",
        [hidden, down_own, swap(down_other), alpha[1:], cotangent.reshape(count, width)],
        2,
        True,
    )
    grad_down = fill(grad_down, swap(grad_down_round))
    gugs, chunks = zip(
        *[
            feed_back(grad_down, hidden_all, w, ug, product, s)
            for w, ug, product, s in zip(w_ds, ugs, products, feed_scale)
        ]
    )
    back_other = sum_dots(gugs, w_ugs, count, count, bf16)
    back_own = sum_dots(gugs, w_ugs, 0, count, f32)
    grad_input_res, grad_branch_round, grad_branch_all, grad_alpha_attend = rowwise(
        hidden_back_kernel,
        "hidden_back",
        [x, branch_own, branch_from, alpha[:1], grad_hidden_res, back_own, swap(back_other)],
        1,
        True,
    )
    grad_branch_all = fill(grad_branch_all, swap(grad_branch_round))

    terms, term_scales = [], []
    for chunk in chunks:
        chunk = chunk.reshape(4, -1, width)
        body = chunk[:, : 3 * units // 4].reshape(4, 3, units // 4, width)
        terms.append(jnp.swapaxes(body, 0, 1).reshape(3, units, width))
        piece = chunk[:, 3 * units // 4, : units // 2].astype(f32).reshape(4, 2, units // 4)
        term_scales.append(jnp.swapaxes(piece, 0, 1).reshape(2, units))

    def scattered(values):
        return lax.psum_scatter(values, "dp", scatter_dimension=1, tiled=True)

    def both_halves(total):
        other = swap(total)
        return jnp.concatenate([pick(rank, total, other), pick(rank, other, total)], 1)

    feed_grad = both_halves(scattered(jnp.concatenate(terms, 1)).astype(f32))
    feed_grad_s = both_halves(scattered(jnp.concatenate(term_scales, 1)))

    grad_qkvs, gscales, pieces = [], [], []
    for group in groups:
        grad_qkv, keep, send = group.back(grad_branch_all, x_all)
        keep, send = jnp.concatenate(keep, 0), jnp.concatenate(send, 0)
        halves = jnp.stack([pick(rank, keep, send), pick(rank, send, keep)]).reshape(2, 4, ROWS, width)
        scale = jnp.sum(halves[:, :, 2 * HEAD_DIM].astype(f32), 0)
        scale = jnp.concatenate([scale[:, : HEAD_DIM // 2], scale[:, HEAD_DIM : 3 * HEAD_DIM // 2]], 1)
        halves = halves[:, :, : 2 * HEAD_DIM].reshape(2, 4, 4, HEAD_DIM // 2, width)
        pieces.append(jnp.transpose(halves, (2, 1, 0, 3, 4)).reshape(4, 4 * HEAD_DIM, width))
        grad_qkvs.append(grad_qkv)
        gscales.append(scale.reshape(1, -1))
    w_flats = [g.w.reshape(-1, width) for g in groups]
    input_other = sum_dots(grad_qkvs, w_flats, count, count, bf16)
    input_own = sum_dots(grad_qkvs, w_flats, 0, count, f32)
    input_grad = grad_input_res + input_own + swap(input_other).astype(f32)

    total = jnp.zeros((4, width, width), bf16)
    total = scattered(lax.dynamic_update_slice(total, jnp.concatenate(pieces, 1), (0, rank * half, 0)))
    attend_grad = total.astype(f32) + swap(total.astype(f32))
    qk = jnp.zeros((1, width), f32)
    qk = lax.dynamic_update_slice(qk, jnp.concatenate(gscales, 1), (0, rank * half))
    total = jnp.concatenate(
        [qk, jnp.sum(grad_alpha_attend, 0)[None], jnp.sum(grad_alpha_feed, 0)[None]], 0
    )
    total = scattered(total)
    attend_grad_s = total + swap(total)
    return (
        output.reshape(tokens.shape),
        input_grad.reshape(tokens.shape),
        attend_grad,
        feed_grad,
        attend_grad_s,
        feed_grad_s,
        adam_rows(attention_weights, attend_grad, attention_first, attention_second),
        adam_rows(feed_weights, feed_grad, feed_first, feed_second),
        adam_change(attention_scales, attend_grad_s, attention_scale_first, attention_scale_second, False),
        adam_change(feed_scales, feed_grad_s, feed_scale_first, feed_scale_second, False),
    )


def solution(mesh):
    rows = P("dp", "seq", None)
    matrix = P(None, "dp", None)
    scale = P(None, "dp")
    return jax.shard_map(
        local_sixteen if mesh.shape["dp"] == HEADS else local_any,
        mesh=mesh,
        in_specs=(rows, P("dp", None), rows, matrix, matrix, scale, scale)
        + (matrix,) * 4
        + (scale,) * 4,
        out_specs=(rows, rows, matrix, matrix, scale, scale, matrix, matrix, scale, scale),
        check_vma=False,
    )
```

```python
import functools
import math

import jax
import jax.numpy as jnp
from jax import lax
from jax.experimental import pallas as pl
from jax.experimental.pallas import tpu as pltpu
from jax.sharding import PartitionSpec as P

HEADS = 16
HEAD_DIM = 64
PAIR = 2 * HEAD_DIM
BLOCK = 256
ROWS = 4 * (HEAD_DIM // 2) + 16

norm_eps = 1e-06
rope_base = 10000.0
learn_rate = 0.003
beta_one = 0.9
beta_two = 0.95
adam_eps = 1e-08
corr_one = 1.0 - 0.9**10
corr_two = 1.0 - 0.95**10
apart = 1024.0

bf16 = jnp.bfloat16
f32 = jnp.float32
NT = (((1,), (1,)), ((), ()))
NN = (((1,), (0,)), ((), ()))
TN = (((0,), (0,)), ((), ()))
MIB = 1024 * 1024
SMALL = pl.CostEstimate(flops=1, bytes_accessed=1, transcendentals=0)
ROOM = pltpu.CompilerParams(vmem_limit_bytes=40 * MIB)


def made(shape, dtype):
    return pltpu.HBM(shape, dtype)


def far(*arrays):
    return [pltpu.with_memory_space_constraint(a, pltpu.HBM) for a in arrays]


def dot(a, b, dims=NN, precision=None):
    return lax.dot_general(a, b, dims, precision=precision, preferred_element_type=f32)


def tie(*values):
    return lax.optimization_barrier(values)


def swap(x):
    return lax.ppermute(x, "seq", [(0, 1), (1, 0)])


def via(x, bits):
    count = lax.axis_size("dp")
    return lax.ppermute(x, "dp", [(i, i ^ bits) for i in range(count)])


def upper_half(x):
    return x[: x.shape[0] // 2]


def lower_half(x):
    return x[x.shape[0] // 2 :]


def join_kernel(steps, *refs):
    for k in range(len(refs) - 1):

        @pl.when(pl.program_id(0) // steps == k)
        def _():
            refs[-1][...] = refs[k][...]


def join(*parts):
    rows, width = parts[0].shape
    steps = max(1, rows // 256)
    tile = rows // steps

    def spec(k):
        return pl.BlockSpec((tile, width), lambda t: (jnp.clip(t - k * steps, 0, steps - 1), 0))

    return pl.pallas_call(
        functools.partial(join_kernel, steps),
        grid=(len(parts) * steps,),
        in_specs=[spec(k) for k in range(len(parts))],
        out_specs=pl.BlockSpec((tile, width), lambda t: (t, 0)),
        out_shape=made((len(parts) * rows, width), parts[0].dtype),
        compiler_params=ROOM,
        cost_estimate=SMALL,
        name="join",
    )(*parts)


def fill_kernel(whole_ref, part_ref, out_ref):
    out_ref[...] = part_ref[...]


def fill(target, part):
    rows, width = part.shape
    tile = rows // 2
    return pl.pallas_call(
        fill_kernel,
        grid=(2,),
        in_specs=[pl.BlockSpec(memory_space=pl.ANY), pl.BlockSpec((tile, width), lambda t: (t, 0))],
        out_specs=pl.BlockSpec((tile, width), lambda t: (t + 2, 0)),
        out_shape=made(target.shape, target.dtype),
        input_output_aliases={0: 0},
        compiler_params=ROOM,
        cost_estimate=SMALL,
        name="fill",
    )(target, part)


def half_kernel(x_ref, out_ref):
    out_ref[...] = x_ref[...]


def half_of(x, lower):
    rows, width = x.shape[0] // 4, x.shape[1]
    at = 2 if lower else 0
    return pl.pallas_call(
        half_kernel,
        grid=(2,),
        in_specs=[pl.BlockSpec((rows, width), lambda t: (t + at, 0))],
        out_specs=pl.BlockSpec((rows, width), lambda t: (t, 0)),
        out_shape=made((2 * rows, width), x.dtype),
        compiler_params=ROOM,
        cost_estimate=SMALL,
        name="half",
    )(x)


def diagonal_in(by_x, by_y):
    return via(half_of(by_y, False), 1), via(half_of(by_x, True), 2)


def plus(a, b):
    return (a.astype(f32) + b.astype(f32)).astype(bf16)


def add_half_kernel(a_ref, b_ref, o_ref):
    o_ref[...] = plus(a_ref[...], b_ref[...])


def add_half(x, part, lower):
    rows, width = part.shape
    tile = rows // 2
    at = 2 if lower else 0
    return pl.pallas_call(
        add_half_kernel,
        grid=(2,),
        in_specs=[
            pl.BlockSpec((tile, width), lambda t: (t + at, 0)),
            pl.BlockSpec((tile, width), lambda t: (t, 0)),
        ],
        out_specs=pl.BlockSpec((tile, width), lambda t: (t + at, 0)),
        out_shape=made(x.shape, x.dtype),
        input_output_aliases={0: 0},
        compiler_params=ROOM,
        cost_estimate=SMALL,
        name="add_half",
    )(x, part)


def column_kernel(own_ref, x_ref, y_ref, *outs):
    total = own_ref[...].astype(f32) + x_ref[...].astype(f32) + y_ref[...].astype(f32)
    for k in range(4):

        @pl.when(pl.program_id(0) == k)
        def _():
            if k < 3 or len(outs) == 4:
                outs[k][...] = total.astype(outs[k].dtype)
            else:
                cut = outs[3].shape[0]
                outs[3][...] = total[:cut].astype(bf16)
                outs[4][...] = total[cut:].astype(bf16)


def column_sum(own, from_x, from_y, cut=0):
    rows, width = own.shape[0] // 4, own.shape[1]
    sizes = [rows] * 4 if cut == 0 else [rows] * 3 + [cut, rows - cut]
    block = pl.BlockSpec((rows, width), lambda t: (t, 0))
    mine, *parts = pl.pallas_call(
        column_kernel,
        grid=(4,),
        in_specs=[block] * 3,
        out_specs=[whole((size, width)) for size in sizes],
        out_shape=[made((rows, width), f32)] + [made((size, width), bf16) for size in sizes[1:]],
        compiler_params=ROOM,
        cost_estimate=SMALL,
        name="column_sum",
    )(own, from_x, from_y)
    return mine, parts


def z_sum(mine, parts):
    for part in parts:
        mine = mine + part.astype(f32)
    return mine


def slot_of(offset):
    return (offset & 3) * 4 + (offset >> 2)


def of_first(shape, dim):
    return (lax.broadcasted_iota(jnp.int32, shape, dim) & 32) == 0


def head_sums(x, same):
    high = x.astype(bf16)
    low = (x - high.astype(f32)).astype(bf16)
    return dot(high, same) + dot(low, same)


def same_head():
    same = of_first((PAIR, PAIR), 0) == of_first((PAIR, PAIR), 1)
    return jnp.where(same, 1.0, 0.0).astype(bf16)


def turned_unit(raw, cosine, sine, same):
    turned = raw * cosine + pltpu.roll(raw, HEAD_DIM, 1) * sine
    scale = lax.rsqrt(head_sums(turned * turned, same) + norm_eps)
    return turned * scale, scale


def local_rows(block, half_blocks, rank):
    count = 2 * half_blocks
    return pl.multiple_of(lax.rem(block + half_blocks * rank, count) * BLOCK, BLOCK)


def attend_kernel(
    info, x_ref, a_ref, b_ref, a_other, b_other, cos_ref, sin_ref, qa_ref, ka_ref,
    w_ref, wo_ref, scale_ref, raw_ref, q_ref, k_ref, v_ref, mix_ref, inv_ref,
    q_aug, k_aug,
):
    blocks = x_ref.shape[0] // BLOCK
    rank = info[blocks]
    part = HEAD_DIM // 2

    def assemble(halves):
        for t, ref in enumerate(halves):
            for head in range(2):
                for m in range(4):
                    source = slice(head * ROWS + m * part, head * ROWS + (m + 1) * part)
                    at = t * HEAD_DIM + head * part
                    if m < 3:
                        w_ref[0, m * PAIR + at : m * PAIR + at + part, :] = ref[source, :]
                    else:
                        wo_ref[at : at + part, :] = ref[source, :]
        rows = [
            halves[0][head * ROWS + 4 * part : (head + 1) * ROWS, :PAIR].astype(f32)[:8] for head in range(2)
        ]
        scales = jnp.where(of_first((8, PAIR), 1), rows[0], pltpu.roll(rows[1], 32, 1))
        scale_ref[0] = scales[:1]

    pl.when(rank == 0)(functools.partial(assemble, (a_ref, a_other)))
    pl.when(rank != 0)(functools.partial(assemble, (b_other, b_ref)))

    first = of_first((BLOCK, PAIR), 1)
    tall = 2 * BLOCK if blocks % 2 == 0 else BLOCK
    first_tall = of_first((tall, PAIR), 1)
    same = same_head()

    def project(t, carry):
        rows = pl.ds(pl.multiple_of(t * tall, tall), tall)
        raw = dot(x_ref[rows, :], w_ref[0], NT)
        raw_ref[rows, :] = raw[:, : 2 * PAIR]
        v_ref[rows, :] = raw[:, 2 * PAIR :].astype(bf16)
        cosine, sine = cos_ref[rows, :], sin_ref[rows, :]
        scale = scale_ref[0]
        q = (turned_unit(raw[:, :PAIR], cosine, sine, same)[0] * scale).astype(bf16)
        k = (turned_unit(raw[:, PAIR : 2 * PAIR], cosine, sine, same)[0] * scale).astype(bf16)
        q_ref[rows, :] = q
        k_ref[rows, :] = k
        q8 = q * jnp.asarray(8.0, bf16)
        qa, ka = qa_ref[rows, :], ka_ref[rows, :]
        q_aug[0, rows, :] = jnp.where(first_tall, q8, qa)
        q_aug[1, rows, :] = jnp.where(first_tall, qa, q8)
        k_aug[0, rows, :] = jnp.where(first_tall, k, ka)
        k_aug[1, rows, :] = jnp.where(first_tall, ka, k)
        return carry

    lax.fori_loop(0, blocks * BLOCK // tall, project, 0)

    row = lax.broadcasted_iota(jnp.int32, (BLOCK, BLOCK), 0)
    col = lax.broadcasted_iota(jnp.int32, (BLOCK, BLOCK), 1)
    causal = col <= row

    def query_block(g, carry):
        q_rows = pl.ds(local_rows(g, blocks // 2, rank), BLOCK)
        count = g - info[g] + 1

        def variant(nk):
            mixed = []
            k_rows = [pl.ds(local_rows(g - (nk - 1) + j, blocks // 2, rank), BLOCK) for j in range(nk)]
            for h in range(2):
                q = q_aug[h, q_rows, :]
                lacc = acc = None
                for j in range(nk):
                    p = jnp.exp(dot(q, k_aug[h, k_rows[j], :], NT))
                    if j == nk - 1:
                        p = jnp.where(causal, p, 0.0)
                    part = p[:, :PAIR] + p[:, PAIR:]
                    lacc = part if lacc is None else lacc + part
                    part = dot(p.astype(bf16), v_ref[k_rows[j], :])
                    acc = part if acc is None else acc + part
                inverse = 1.0 / jnp.sum(lacc, axis=1, keepdims=True)
                inv_ref[0, h : h + 1, q_rows] = 1.0 / jnp.sum(lacc.T, axis=0, keepdims=True)
                mixed.append(acc * inverse)
            mix_ref[q_rows, :] = jnp.where(first, mixed[0], mixed[1]).astype(bf16)

        for nk in range(1, 5):
            pl.when(count == nk if nk < 4 else count >= 4)(functools.partial(variant, nk))
        return carry

    lax.fori_loop(0, blocks, query_block, 0)


def whole(shape):
    return pl.BlockSpec(shape, lambda p: (0,) * len(shape))


def attend_forward(info, x_all, parts, cosine, sine, qa, ka):
    tokens, width = x_all.shape
    pairs = 2
    feats = pairs * PAIR
    by_pair = pl.BlockSpec((tokens, PAIR), lambda p: (0, p))
    return pl.pallas_call(
        attend_kernel,
        grid=(pairs,),
        in_specs=[
            pl.BlockSpec(memory_space=pltpu.SMEM),
            whole((tokens, width)),
        ]
        + [pl.BlockSpec((2 * ROWS, width), lambda p: (p, 0))] * 4
        + [
            whole((tokens, PAIR)),
            whole((tokens, PAIR)),
            whole((tokens, PAIR)),
            whole((tokens, PAIR)),
        ],
        out_specs=[
            pl.BlockSpec((1, 3 * PAIR, width), lambda p: (p, 0, 0)),
            pl.BlockSpec((PAIR, width), lambda p: (p, 0)),
            pl.BlockSpec((1, 1, PAIR), lambda p: (p, 0, 0)),
            pl.BlockSpec((tokens, 2 * PAIR), lambda p: (0, p)),
            by_pair,
            by_pair,
            by_pair,
            by_pair,
            pl.BlockSpec((1, 8, tokens), lambda p: (p, 0, 0)),
        ],
        out_shape=[
            made((pairs, 3 * PAIR, width), bf16),
            made((feats, width), bf16),
            made((pairs, 1, PAIR), f32),
            made((tokens, 2 * feats), f32),
            made((tokens, feats), bf16),
            made((tokens, feats), bf16),
            made((tokens, feats), bf16),
            made((tokens, feats), bf16),
            made((pairs, 8, tokens), f32),
        ],
        scratch_shapes=[
            pltpu.VMEM((2, tokens, PAIR), bf16),
            pltpu.VMEM((2, tokens, PAIR), bf16),
        ],
        compiler_params=ROOM,
        cost_estimate=SMALL,
        name="attend_forward",
    )(info, *far(x_all), *parts, *far(cosine, sine, qa, ka))


def attend_back_kernel(
    info, q_ref, k_ref, v_ref, gb_ref, x_ref, wo_ref, mix_ref, inv_ref, raw_ref, cos_ref, sin_ref, scale_ref,
    qa_ref, ka_ref,
    grad_ref, keep_0, keep_1, send_0, send_1,
    q_aug, k_aug, do_h, q_h, kt_h, delta, dq_acc, dk_acc, dv_acc, dw_acc,
):
    blocks = q_ref.shape[0] // BLOCK
    rank = info[blocks]
    first = of_first((BLOCK, PAIR), 1)
    first_rows = of_first((PAIR, BLOCK), 0)
    zero = jnp.zeros((BLOCK, PAIR), bf16)
    eight = jnp.asarray(8.0, bf16)
    same = same_head()

    def prepare(t, carry):
        start = pl.multiple_of(t * BLOCK, BLOCK)
        rows = pl.ds(start, BLOCK)
        q8 = q_ref[rows, :] * eight
        k = k_ref[rows, :]
        qa, ka = qa_ref[rows, :], ka_ref[rows, :]
        q_aug[0, rows, :] = jnp.where(first, q8, qa)
        q_aug[1, rows, :] = jnp.where(first, qa, q8)
        k_aug[0, rows, :] = jnp.where(first, k, ka)
        k_aug[1, rows, :] = jnp.where(first, ka, k)
        q_h[0, rows, :] = jnp.where(first, q8, zero)
        q_h[1, rows, :] = jnp.where(first, zero, q8)
        k_t = (k * eight).astype(f32).T
        kt_h[0, :, rows] = jnp.where(first_rows, k_t, 0.0).astype(bf16)
        kt_h[1, :, rows] = jnp.where(first_rows, 0.0, k_t).astype(bf16)
        grad = dot(gb_ref[rows, :], wo_ref[...], NT).astype(bf16)
        do_h[0, rows, :] = jnp.where(first, grad, zero)
        do_h[1, rows, :] = jnp.where(first, zero, grad)
        inner = (grad.astype(f32) * mix_ref[rows, :].astype(f32)).T
        inner = inner[:HEAD_DIM] + inner[HEAD_DIM:]
        delta[0:1, rows] = jnp.sum(inner[: HEAD_DIM // 2], axis=0, keepdims=True)
        delta[1:2, rows] = jnp.sum(inner[HEAD_DIM // 2 :], axis=0, keepdims=True)
        dk_acc[rows, :] = jnp.zeros((BLOCK, PAIR), f32)
        dv_acc[rows, :] = jnp.zeros((BLOCK, PAIR), f32)
        return carry

    lax.fori_loop(0, blocks, prepare, 0)

    row = lax.broadcasted_iota(jnp.int32, (BLOCK, BLOCK), 0)
    col = lax.broadcasted_iota(jnp.int32, (BLOCK, BLOCK), 1)
    causal = row <= col

    def query_block(g, carry):
        q_rows = pl.ds(local_rows(g, blocks // 2, rank), BLOCK)
        count = g - info[g] + 1

        def variant(nk):
            dq_t = None
            for j in range(nk):
                k_rows = pl.ds(local_rows(g - (nk - 1) + j, blocks // 2, rank), BLOCK)
                dk = dv = None
                for h in range(2):
                    scores = dot(k_aug[h, k_rows, :], q_aug[h, q_rows, :], NT)
                    p = jnp.exp(scores) * inv_ref[0, h : h + 1, q_rows]
                    if j == nk - 1:
                        p = jnp.where(causal, p, 0.0)
                    dp = dot(v_ref[k_rows, :], do_h[h, q_rows, :], NT)
                    ds = (p * (dp - delta[h : h + 1, q_rows])).astype(bf16)
                    dv_part = dot(p.astype(bf16), do_h[h, q_rows, :])
                    dk_part = dot(ds, q_h[h, q_rows, :])
                    dq_part = dot(kt_h[h, :, k_rows], ds)
                    dv = dv_part if dv is None else dv + dv_part
                    dk = dk_part if dk is None else dk + dk_part
                    dq_t = dq_part if dq_t is None else dq_t + dq_part
                dv_acc[k_rows, :] += dv
                dk_acc[k_rows, :] += dk
            dq_acc[q_rows, :] = dq_t.T

        for nk in range(1, 5):
            pl.when(count == nk if nk < 4 else count >= 4)(functools.partial(variant, nk))
        return carry

    lax.fori_loop(0, blocks, query_block, 0)

    tall = 2 * BLOCK if blocks % 2 == 0 else BLOCK

    def unturn(t, total):
        rows = pl.ds(pl.multiple_of(t * tall, tall), tall)
        cosine, sine = cos_ref[rows, :], sin_ref[rows, :]
        scale = scale_ref[0]
        for which, acc in ((0, dq_acc), (1, dk_acc)):
            raw = raw_ref[rows, which * PAIR : (which + 1) * PAIR]
            unit, size = turned_unit(raw, cosine, sine, same)
            grad = acc[rows, :]
            total = total + jnp.sum((grad * unit).reshape(tall // 8, 8, PAIR), axis=0)
            grad_unit = grad * scale
            grad_turned = size * (grad_unit - unit * head_sums(unit * grad_unit, same))
            grad_raw = grad_turned * cosine - pltpu.roll(grad_turned, HEAD_DIM, 1) * sine
            grad_ref[rows, which * PAIR : (which + 1) * PAIR] = grad_raw.astype(bf16)
        grad_ref[rows, 2 * PAIR :] = dv_acc[rows, :].astype(bf16)
        return total

    total = lax.fori_loop(0, blocks * BLOCK // tall, unturn, jnp.zeros((8, PAIR), f32))
    scale_row = jnp.sum(total, axis=0, keepdims=True)

    dw_acc[...] = jnp.zeros_like(dw_acc)

    def row_grads(t, carry):
        rows = pl.ds(pl.multiple_of(t * tall, tall), tall)
        dw_acc[: 3 * PAIR, :] += dot(grad_ref[rows, :], x_ref[rows, :], TN)
        dw_acc[3 * PAIR :, :] += dot(mix_ref[rows, :], gb_ref[rows, :], TN)
        return carry

    lax.fori_loop(0, blocks * BLOCK // tall, row_grads, 0)
    part = HEAD_DIM // 2

    pair = pl.program_id(0)

    def deal(keep, send):
        for half, out in enumerate((keep, send)):
            for head in range(2):
                base = head * ROWS
                for m in range(4):
                    for t in range(2):

                        @pl.when((rank == t) == (half == 0))
                        def _():
                            at = m * PAIR + t * HEAD_DIM + head * part
                            out[base + m * part : base + (m + 1) * part, :] = dw_acc[at : at + part, :].astype(bf16)

                tail = slice(base + 4 * part, base + ROWS)
                out[tail, :] = jnp.zeros((ROWS - 4 * part, out.shape[1]), bf16)
                if half == 0:
                    row = scale_row if head == 0 else pltpu.roll(jnp.broadcast_to(scale_row, (8, PAIR)), 96, 1)[:1]
                    rows = ROWS - 4 * part
                    top = lax.broadcasted_iota(jnp.int32, (rows, PAIR), 0) == 0
                    out[tail, :PAIR] = jnp.where(top, jnp.broadcast_to(row, (rows, PAIR)), 0.0).astype(bf16)

    pl.when(pair == 0)(functools.partial(deal, keep_0, send_0))
    pl.when(pair == 1)(functools.partial(deal, keep_1, send_1))


def attend_backward(info, q, k, v, grad_branch, x, wo, mixture, inverse, raw, cosine, sine, scale, qa, ka):
    tokens, feats = q.shape
    width = x.shape[1]
    pairs = feats // PAIR
    by_pair = pl.BlockSpec((tokens, PAIR), lambda p: (0, p))
    half = pltpu.VMEM((2, tokens, PAIR), bf16)
    acc = pltpu.VMEM((tokens, PAIR), f32)
    return pl.pallas_call(
        attend_back_kernel,
        grid=(pairs,),
        in_specs=[
            pl.BlockSpec(memory_space=pltpu.SMEM),
            by_pair,
            by_pair,
            by_pair,
            whole((tokens, width)),
            whole((tokens, width)),
            pl.BlockSpec((PAIR, width), lambda p: (p, 0)),
            by_pair,
            pl.BlockSpec((1, 8, tokens), lambda p: (p, 0, 0)),
            pl.BlockSpec((tokens, 2 * PAIR), lambda p: (0, p)),
            whole((tokens, PAIR)),
            whole((tokens, PAIR)),
            pl.BlockSpec((1, 1, PAIR), lambda p: (p, 0, 0)),
            whole((tokens, PAIR)),
            whole((tokens, PAIR)),
        ],
        out_specs=[
            pl.BlockSpec((tokens, 3 * PAIR), lambda p: (0, p)),
        ]
        + [whole((2 * ROWS, width))] * 4,
        out_shape=[made((tokens, 3 * feats), bf16)] + [made((2 * ROWS, width), bf16)] * 4,
        scratch_shapes=[
            half,
            half,
            half,
            half,
            pltpu.VMEM((2, PAIR, tokens), bf16),
            pltpu.VMEM((8, tokens), f32),
            acc,
            acc,
            acc,
            pltpu.VMEM((4 * PAIR, width), f32),
        ],
        compiler_params=ROOM,
        cost_estimate=SMALL,
        name="attend_backward",
    )(info, *far(q, k, v, grad_branch, x, wo, mixture, inverse, raw, cosine, sine), scale, *far(qa, ka))


def slot_scale(ref, group):
    return ref[:, 2 * PAIR : 2 * PAIR + 2 * group].astype(f32)[:1]


def scale_specs(width):
    return [pl.BlockSpec((16, width), lambda t, n=n: ((n * ROWS + 2 * HEAD_DIM) // 16, 0)) for n in range(4)]


def up_gate_kernel(h_ref, *refs):
    *w_refs, s_0, s_1, s_2, s_3, ug_ref, product_ref = refs
    group = product_ref.shape[1] // 4
    per = 4 // len(w_refs)
    for k in range(4):
        pair = slice(2 * k * group, 2 * (k + 1) * group)
        at = 2 * (k % per) * group
        both = dot(h_ref[...], w_refs[k // per][at : at + 2 * group, :], NT)
        ug_ref[:, pair] = both.astype(bf16)
        scaled = both * slot_scale((s_0, s_1, s_2, s_3)[k], group)
        gated = scaled[:, group:]
        product = scaled[:, :group] * gated / (1.0 + jnp.exp(-gated))
        product_ref[:, k * group : (k + 1) * group] = product.astype(bf16)


def tile_of(tokens):
    return 512 if tokens % 512 == 0 else 256


def up_gate(hidden, w, scale, before=None):
    tokens, width = hidden.shape
    w = w if isinstance(w, tuple) else (w,)
    units = w[0].shape[0] * len(w) // 2
    tile = tokens // 2
    at = 0 if before is None else 2
    more = [] if before is None else list(before)
    inputs = 5 + len(w)

    def kernel(*refs):
        up_gate_kernel(*refs[:inputs], *refs[inputs + len(more) :])

    return pl.pallas_call(
        kernel,
        grid=(2,),
        in_specs=[
            pl.BlockSpec((tile, width), lambda t: (t, 0)),
        ]
        + [whole(part.shape) for part in w]
        + scale_specs(width)
        + [pl.BlockSpec(memory_space=pl.ANY)] * len(more),
        out_specs=[
            pl.BlockSpec((tile, 2 * units), lambda t: (t + at, 0)),
            pl.BlockSpec((tile, units), lambda t: (t + at, 0)),
        ],
        out_shape=[made((2 * tokens, 2 * units), bf16), made((2 * tokens, units), bf16)],
        input_output_aliases={inputs + n: n for n in range(len(more))},
        compiler_params=ROOM,
        cost_estimate=SMALL,
        name="up_gate",
    )(hidden, *w, *[scale] * 4, *more)


def feed_back_kernel(
    count, grad_ref, h_ref, *rest
):
    w_refs, rest = rest[:count], rest[count:]
    ug_ref, product_ref, s_0, s_1, s_2, s_3, gug_ref, *dws, ug_acc, d_acc, gscale = rest
    group = product_ref.shape[1] // 4
    per_w, per = 4 // count, 4 // len(dws)
    step = pl.program_id(0)

    @pl.when(step == 0)
    def _():
        gscale[...] = jnp.zeros_like(gscale)
        ug_acc[...] = jnp.zeros_like(ug_acc)
        d_acc[...] = jnp.zeros_like(d_acc)

    rows = grad_ref.shape[0] // 8
    d_acc[...] += dot(product_ref[...], grad_ref[...], TN)
    for k in range(4):
        ups = slice(2 * k * group, (2 * k + 1) * group)
        gates = slice((2 * k + 1) * group, (2 * k + 2) * group)
        at = (k % per_w) * group
        grad = dot(grad_ref[...], w_refs[k // per_w][at : at + group, :], NT)
        up = ug_ref[:, ups].astype(f32)
        gate = ug_ref[:, gates].astype(f32)
        scales = slot_scale((s_0, s_1, s_2, s_3)[k], group)
        up_scale, gate_scale = scales[:, :group], scales[:, group:]
        gated = gate * gate_scale
        sig = 1.0 / (1.0 + jnp.exp(-gated))
        silu = gated * sig
        through = grad * silu
        grad_gated = grad * (up * up_scale) * (sig + silu * (1.0 - sig))
        gug_ref[:, ups] = (through * up_scale).astype(bf16)
        gug_ref[:, gates] = (grad_gated * gate_scale).astype(bf16)
        gscale[:, ups] += jnp.sum((through * up).reshape(rows, 8, group), axis=0)
        gscale[:, gates] += jnp.sum((grad_gated * gate).reshape(rows, 8, group), axis=0)
    ug_acc[...] += dot(gug_ref[...], h_ref[...], TN)

    @pl.when(step == pl.num_programs(0) - 1)
    def _():
        top = lax.broadcasted_iota(jnp.int32, (16, 2 * group), 0) == 0
        for k in range(4):
            out, at = dws[k // per], (k % per) * (3 * group + 16)
            out[at : at + 2 * group, :] = ug_acc[2 * k * group : 2 * (k + 1) * group, :].astype(bf16)
            out[at + 2 * group : at + 3 * group, :] = d_acc[k * group : (k + 1) * group, :].astype(bf16)
            sums = jnp.sum(gscale[:, 2 * k * group : 2 * (k + 1) * group], axis=0, keepdims=True)
            tail = slice(at + 3 * group, at + 3 * group + 16)
            out[tail, :] = jnp.zeros((16, out.shape[1]), bf16)
            out[tail, : 2 * group] = jnp.where(top, jnp.broadcast_to(sums, top.shape), 0.0).astype(bf16)


def feed_back(grad, hidden, w, ug, product, scale, pieces=1):
    tokens, width = grad.shape
    w = pieces_of(w)
    units = product.shape[1]
    tile = tile_of(tokens)
    row = pl.BlockSpec((tile, width), lambda t: (t, 0))
    wide = pl.BlockSpec((tile, 2 * units), lambda t: (t, 0))
    rows = (units * 3 + 64) // pieces
    return pl.pallas_call(
        functools.partial(feed_back_kernel, len(w)),
        grid=(tokens // tile,),
        in_specs=[
            row,
            row,
            *[pl.BlockSpec((size, width), lambda t, n=at // size: (n, 0)) for _, at, size in w],
            wide,
            pl.BlockSpec((tile, units), lambda t: (t, 0)),
        ]
        + scale_specs(width),
        out_specs=[wide] + [whole((rows, width))] * pieces,
        out_shape=[made((tokens, 2 * units), bf16)] + [made((rows, width), bf16)] * pieces,
        scratch_shapes=[
            pltpu.VMEM((2 * units, width), f32),
            pltpu.VMEM((units, width), f32),
            pltpu.VMEM((8, 2 * units), f32),
        ],
        compiler_params=ROOM,
        cost_estimate=SMALL,
        name="feed_back",
    )(*far(grad, hidden), *[array for array, _, _ in w], *far(ug, product), *[scale] * 4)


def pieces_of(right):
    right = right if isinstance(right, tuple) else (right,)
    return [p if isinstance(p, tuple) else (p, 0, p.shape[0]) for p in right]


def sum_dots_kernel(lefts, plan, start, tile, *refs):
    arrays = lefts + 1 + max(piece[0] for pieces in plan for piece in pieces)
    has = len(refs) - arrays - 3 - 2 * lefts
    addend = refs[arrays] if has else None
    out, acc, *bufs, sems = refs[arrays + has :]
    rows = out.shape[0]
    copies, used = [], 0
    for n, pieces in enumerate(plan):
        group = [pltpu.make_async_copy(refs[n].at[pl.ds(start, rows), :], bufs[2 * n], sems.at[used])]
        used, to = used + 1, 0
        for index, at, size in pieces:
            source = refs[lefts + index].at[pl.ds(at, size), :]
            group.append(pltpu.make_async_copy(source, bufs[2 * n + 1].at[pl.ds(to, size), :], sems.at[used]))
            used, to = used + 1, to + size
        copies.append(group)
    for group in copies:
        for copy in group:
            copy.start()
    last = lefts - 1
    for n, group in enumerate(copies):
        for copy in group:
            copy.wait()
        for r in range(0, rows, tile):
            here = slice(r, r + tile)
            part = dot(bufs[2 * n][here, :], bufs[2 * n + 1][...])
            if n > 0:
                part = part + acc[here, :]
            elif addend is not None:
                part = part + addend[here, :].astype(f32)
            if n < last:
                acc[here, :] = part
            else:
                out[here, :] = part.astype(out.dtype)


def sum_dots(lefts, rights, start, rows, dtype, addend=None):
    plan, arrays = [], []
    for right in rights:
        pieces = []
        for array, at, size in pieces_of(right):
            known = [n for n, a in enumerate(arrays) if a is array]
            if not known:
                arrays.append(array)
            pieces.append((known[0] if known else len(arrays) - 1, at, size))
        plan.append(pieces)
    width = arrays[0].shape[1]
    bufs = []
    for left in lefts:
        bufs += [pltpu.VMEM((rows, left.shape[1]), bf16), pltpu.VMEM((left.shape[1], width), bf16)]
    copies = len(lefts) + sum(len(pieces) for pieces in plan)
    more = [] if addend is None else [addend]
    far_ref = pl.BlockSpec(memory_space=pltpu.HBM)
    near = pl.BlockSpec(memory_space=pltpu.VMEM)
    return pl.pallas_call(
        functools.partial(sum_dots_kernel, len(lefts), plan, start, 256),
        in_specs=[far_ref] * (len(lefts) + len(arrays)) + [near] * len(more),
        out_specs=near,
        out_shape=made((rows, width), dtype),
        scratch_shapes=[pltpu.VMEM((rows, width), f32), *bufs, pltpu.SemaphoreType.DMA((copies,))],
        compiler_params=ROOM,
        cost_estimate=SMALL,
        name="sum_dots",
    )(*lefts, *arrays, *more)


def alpha_kernel(place, *refs):
    slots, one, two, rows = refs[:HEADS], refs[HEADS], refs[HEADS + 1], refs[HEADS + 2]
    for j in range(HEADS):
        rows[j : j + 1, :] = slots[j][:, PAIR : 2 * PAIR].astype(f32)[:1]
    low = lax.broadcasted_iota(jnp.int32, (1, PAIR), 1) < HEAD_DIM
    for k in range(HEADS // 2):
        pair = []
        for owner in (2 * k, 2 * k + 1):
            slot = slot_of(jnp.bitwise_xor(place[0], owner))
            pair.append(jnp.broadcast_to(rows[pl.ds(slot, 1), :], (8, PAIR)))
        turned = [pltpu.roll(p, HEAD_DIM, 1)[:1] for p in pair]
        lanes = slice(k * PAIR, (k + 1) * PAIR)
        one[:, lanes] = jnp.where(low, pair[0][:1], turned[1])
        two[:, lanes] = jnp.where(low, turned[0], pair[1][:1])


def alpha_rows(place, chunks):
    width = chunks[0].shape[1]
    specs = scale_specs(width)
    return pl.pallas_call(
        alpha_kernel,
        grid=(1,),
        in_specs=[pl.BlockSpec(memory_space=pltpu.SMEM)] + specs * 4,
        out_specs=[whole((1, width))] * 2,
        out_shape=[made((1, width), f32)] * 2,
        scratch_shapes=[pltpu.VMEM((HEADS, PAIR), f32)],
        compiler_params=ROOM,
        cost_estimate=SMALL,
        name="alpha",
    )(place[None].astype(jnp.int32), *(chunk for chunk in chunks for _ in range(4)))


def rms_scale(values):
    return lax.rsqrt(jnp.mean(values * values, axis=-1, keepdims=True) + norm_eps)


def blend_parts(residual, branch, mixing):
    branch_scale = rms_scale(branch)
    unit = branch * branch_scale
    step = unit - residual
    mixed = residual + mixing * step
    mixed_scale = rms_scale(mixed)
    return branch_scale, unit, step, mixed * mixed_scale, mixed_scale


def blend_grads(parts, mixing, grad):
    branch_scale, unit, step, result, mixed_scale = parts
    grad_mixed = mixed_scale * (grad - result * jnp.mean(grad * result, axis=-1, keepdims=True))
    grad_unit = mixing * grad_mixed
    grad_branch = branch_scale * (grad_unit - unit * jnp.mean(unit * grad_unit, axis=-1, keepdims=True))
    return grad_mixed - grad_unit, grad_branch, grad_mixed * step


def add_rows(ref, values):
    @pl.when(pl.program_id(0) == 0)
    def _():
        ref[...] = jnp.zeros_like(ref)

    ref[...] += jnp.sum(values.reshape(values.shape[0] // 8, 8, values.shape[1]), axis=0)


def hidden_kernel(x_ref, own_ref, other_ref, mix_ref, hidden_ref, round_ref, wide_ref):
    branch = own_ref[...] + other_ref[...].astype(f32)
    hidden = blend_parts(x_ref[...].astype(f32), branch, mix_ref[...])[3]
    hidden_ref[...] = hidden
    round_ref[...] = wide_ref[...] = hidden.astype(bf16)


def output_kernel(
    hidden_ref, own_ref, other_ref, mix_ref, cot_ref, out_ref, res_ref, down_ref, wide_ref, gmix_ref
):
    mixing = mix_ref[...]
    parts = blend_parts(hidden_ref[...], own_ref[...] + other_ref[...].astype(f32), mixing)
    out_ref[...] = parts[3]
    grad_res, grad_down, grad_mix = blend_grads(parts, mixing, cot_ref[...].astype(f32))
    res_ref[...] = grad_res
    down_ref[...] = wide_ref[...] = grad_down.astype(bf16)
    add_rows(gmix_ref, grad_mix)


def hidden_back_kernel(
    x_ref, own_ref, other_ref, mix_ref, res_ref, back_ref, from_ref, in_ref, branch_ref, wide_ref, gmix_ref
):
    mixing = mix_ref[...]
    parts = blend_parts(x_ref[...].astype(f32), own_ref[...] + other_ref[...].astype(f32), mixing)
    grad = res_ref[...] + back_ref[...] + from_ref[...].astype(f32)
    grad_res, grad_branch, grad_mix = blend_grads(parts, mixing, grad)
    in_ref[...] = grad_res
    branch_ref[...] = wide_ref[...] = grad_branch.astype(bf16)
    add_rows(gmix_ref, grad_mix)


def rowwise(kernel, name, arrays, floats, reduced=False):
    tokens, width = arrays[0].shape
    tile = 128
    row = pl.BlockSpec((tile, width), lambda t: (t, 0))
    out_shape = [made((tokens, width), f32)] * floats
    out_shape += [made((tokens, width), bf16), made((2 * tokens, width), bf16)]
    out_specs = [row] * (floats + 2)
    if reduced:
        out_shape.append(made((8, width), f32))
        out_specs.append(whole((8, width)))
    return pl.pallas_call(
        kernel,
        grid=(tokens // tile,),
        in_specs=[row if a.shape[0] == tokens else whole((1, width)) for a in arrays],
        out_specs=out_specs,
        out_shape=out_shape,
        compiler_params=ROOM,
        cost_estimate=SMALL,
        name=name,
    )(*(far(a)[0] if a.dtype == f32 and a.shape[0] == tokens else a for a in arrays))


def adam_change(weight, gradient, moment_one, moment_two, renormalize):
    moment_one_new = beta_one * moment_one + (1.0 - beta_one) * gradient
    moment_two_new = beta_two * moment_two + (1.0 - beta_two) * gradient * gradient
    stepped = weight - learn_rate * (moment_one_new / corr_one) / (
        jnp.sqrt(moment_two_new / corr_two) + adam_eps
    )
    if renormalize:
        stepped = stepped * lax.rsqrt(jnp.sum(stepped * stepped, axis=-1, keepdims=True) + norm_eps)
    return stepped - weight


def adam_kernel(w_ref, g_ref, one_ref, two_ref, out_ref):
    out_ref[...] = adam_change(w_ref[...], g_ref[...], one_ref[...], two_ref[...], True)


def adam_rows(weight, gradient, moment_one, moment_two):
    shape = weight.shape
    rows, width = shape[0] * shape[1], shape[2]
    tile = next(t for t in (128, 64, 32, 16, 8) if rows % t == 0)
    block = pl.BlockSpec((tile, width), lambda t: (t, 0))
    return pl.pallas_call(
        adam_kernel,
        grid=(rows // tile,),
        in_specs=[block] * 4,
        out_specs=block,
        out_shape=made((rows, width), f32),
        compiler_params=ROOM,
        cost_estimate=SMALL,
        name="adam",
    )(*far(*(a.reshape(rows, width) for a in (weight, gradient, moment_one, moment_two)))).reshape(shape)


def own_half(x, rank, axis):
    size = x.shape[axis] // 2
    return lax.dynamic_slice_in_dim(x, rank * size, size, axis)


def pick(rank, zero, one):
    return jnp.where(rank == 0, zero, one)


def document_tables(segment_ids, rank, count):
    segments = segment_ids.reshape(-1)
    docs = jnp.arange(8, dtype=jnp.int32)
    begins = jnp.sum((segments[None, :] < docs[:, None]).astype(jnp.int32), axis=1)
    is_doc = segments[:, None] == docs[None, :]
    starts = jnp.sum(jnp.where(is_doc, begins[None, :], 0), axis=1)
    info = jnp.concatenate([starts[::BLOCK] // BLOCK, rank[None].astype(jnp.int32)])
    place = jnp.arange(2 * count, dtype=jnp.int32)

    def arranged(values):
        own = lax.dynamic_slice_in_dim(values, rank * count, count, 0)
        other = lax.dynamic_slice_in_dim(values, (1 - rank) * count, count, 0)
        return jnp.concatenate([own, other], 0)

    positions = arranged(place - starts).astype(f32)
    frequency = jnp.exp(
        jnp.arange(HEAD_DIM // 2, dtype=f32) * (-2.0 * math.log(rope_base) / HEAD_DIM)
    )
    angles = positions[:, None] * jnp.tile(frequency, 4)[None, :]
    cosine = jnp.cos(angles)
    sign = jnp.where(jnp.arange(PAIR) < HEAD_DIM, -1.0, 1.0).astype(f32)
    sine = jnp.sin(angles) * sign[None, :]
    lanes = jnp.arange(PAIR, dtype=jnp.int32)
    lanes = jnp.where(lanes < HEAD_DIM, lanes & 31, 8)
    own_doc = arranged(segments)[:, None] == lanes[None, :]
    query_mark = own_doc.astype(bf16)
    key_mark = jnp.where(own_doc | (lanes >= 8)[None, :], 0.0, -apart).astype(bf16)
    return info, cosine, sine, query_mark, key_mark


def scale_row(qk, alpha, feed, width):
    count = qk.shape[0]
    gap = jnp.zeros((count, HEAD_DIM // 2), f32)
    row = [qk[:, : HEAD_DIM // 2], gap, qk[:, HEAD_DIM // 2 :], gap]
    row += [jnp.broadcast_to(alpha.reshape(1, -1), (count, PAIR)), feed.reshape(count, -1)]
    row = jnp.concatenate(row, 1).astype(bf16)
    return jnp.pad(row[:, None], ((0, 0), (0, 15), (0, width - row.shape[1])))


class Group:
    def __init__(self, tables, x_all, parts):
        self.tables = tables
        info, cosine, sine, query_mark, key_mark = tables
        (self.w, self.wo, self.scale, self.raw, self.q, self.k, self.v, self.mixture, self.inverse) = attend_forward(
            info, x_all, parts, cosine, sine, query_mark, key_mark
        )

    def back(self, grad_branch, x_all):
        info, cosine, sine, query_mark, key_mark = self.tables
        grad_qkv, *rows = attend_backward(
            info, self.q, self.k, self.v, grad_branch, x_all, self.wo, self.mixture, self.inverse, self.raw,
            cosine, sine, self.scale, query_mark, key_mark,
        )
        return grad_qkv, tuple(rows[:2]), tuple(rows[2:])


def local_sixteen(
    tokens,
    segment_ids,
    cotangent,
    attention_weights,
    feed_weights,
    attention_scales,
    feed_scales,
    attention_first,
    attention_second,
    feed_first,
    feed_second,
    attention_scale_first,
    attention_scale_second,
    feed_scale_first,
    feed_scale_second,
):
    count, width = tokens.shape[0] * tokens.shape[1], tokens.shape[-1]
    rank, place = lax.axis_index("seq"), lax.axis_index("dp")
    x = tokens.reshape(count, width)

    part = own_half(attention_weights, rank, 1).astype(bf16)
    rows = part.shape[1]
    body = 4 * rows
    extra = scale_row(attention_scales[0:1], attention_scales[1:], own_half(feed_scales, rank, 1)[None], width)
    block_a = jnp.concatenate([part.reshape(body, width), extra[0]], axis=0)
    feed_part = own_half(feed_weights, rank, 1).astype(bf16)
    units = feed_part.shape[1]
    block_u = feed_part[:2].reshape(2 * units, width)
    block_d = feed_part[2]

    z_a = [via(block_a, 4 * k) for k in (1, 2, 3)]
    x_d, y_d = via(block_d, 1), via(block_d, 2)
    x_all = jnp.concatenate([x, swap(x)], 0)
    tables = document_tables(segment_ids, rank, count)
    block_a, z_a, block_u, x_d, y_d, x_all, tables = tie(block_a, z_a, block_u, x_d, y_d, x_all, tables)

    own_a = join(block_a, *z_a)
    x_a, y_a = via(own_a, 1), via(own_a, 2)
    z_u = [via(block_u, 4), via(block_u, 8)]
    own_a, x_a, y_a, z_u, block_u, y_d, x_all = tie(own_a, x_a, y_a, z_u, block_u, y_d, x_all)

    d_a = diagonal_in(x_a, y_a)
    z_u = z_u + [via(block_u, 12)]
    d_d = via(y_d, 1)
    group_0 = Group(tables, x_all, (own_a, y_a, swap(own_a), swap(y_a)))
    d_a, z_u, block_u, d_d, group_0.mixture, x_all = tie(d_a, z_u, block_u, d_d, group_0.mixture, x_all)

    own_u = join(block_u, *z_u)
    quad = join(block_d, x_d, y_d, d_d)
    own_u, quad = tie(own_u, quad)
    x_u, y_u = via(own_u, 1), via(own_u, 2)
    z_d = [via(quad, 4), via(quad, 8)]
    d_a = join(*d_a)
    group_1 = Group(tables, x_all, (x_a, d_a, swap(x_a), swap(d_a)))
    groups = (group_0, group_1)
    mixtures, wos = [g.mixture for g in groups], [g.wo for g in groups]
    branch_other = sum_dots(mixtures, wos, count, count, bf16)
    branch_own = sum_dots(mixtures, wos, 0, count, f32)
    branch_other, branch_own, x_u, y_u, z_d, d_a = tie(branch_other, branch_own, x_u, y_u, z_d, d_a)

    d_u = diagonal_in(x_u, y_u)
    z_d3 = via(half_of(quad, False), 12)
    alpha = alpha_rows(place, (own_a, x_a, y_a, d_a))
    branch_from = swap(branch_other)
    hidden, hidden_round, hidden_all = rowwise(
        hidden_kernel, "hidden", [x, branch_own, branch_from, alpha[0]], 1
    )
    first_own = up_gate(hidden_round, own_u, own_a)
    first_x = up_gate(hidden_round, x_u, x_a)
    first_y = up_gate(hidden_round, y_u, y_a)
    d_u, z_d3, quad, hidden_round, first_own, first_x, first_y = tie(
        d_u, z_d3, quad, hidden_round, first_own, first_x, first_y
    )
    z_d4 = via(half_of(quad, True), 12)
    hidden_other = swap(hidden_round)
    hidden_all = fill(hidden_all, hidden_other)
    ug_own, product_own = up_gate(hidden_other, own_u, own_a, first_own)
    ug_x, product_x = up_gate(hidden_other, x_u, x_a, first_x)
    ug_y, product_y = up_gate(hidden_other, y_u, y_a, first_y)
    ug_d, product_d = up_gate(hidden_other, d_u, d_a, up_gate(hidden_round, d_u, d_a))
    product_own, product_x, product_y, product_d, hidden_all, z_d4 = tie(
        product_own, product_x, product_y, product_d, hidden_all, z_d4
    )

    own_d, x_d, y_d, d_d = [
        tuple((array, c * units, units) for array in (quad, *z_d)) + (((z_d3, z_d4)[c // 2], (c % 2) * units, units),)
        for c in range(4)
    ]
    products, w_ds = [product_own, product_x, product_y, product_d], [own_d, x_d, y_d, d_d]
    down_other = sum_dots(products, w_ds, count, count, bf16)
    down_own = sum_dots(products, w_ds, 0, count, f32)
    output, grad_hidden_res, grad_down_round, grad_down, grad_alpha_feed = rowwise(
        output_kernel,
        "output",
        [hidden, down_own, swap(down_other), alpha[1], cotangent.reshape(count, width)],
        2,
        True,
    )

    grad_down = fill(grad_down, swap(grad_down_round))
    gug_d, *r_d = feed_back(grad_down, hidden_all, d_d, ug_d, product_d, d_a, 2)
    r_d, grad_down, product_x, product_y, product_own = tie(r_d, grad_down, product_x, product_y, product_own)
    t_d = via(r_d[0], 1), via(r_d[1], 2)
    gug_x, r_x = feed_back(grad_down, hidden_all, x_d, ug_x, product_x, x_a)
    gug_y, r_y = feed_back(grad_down, hidden_all, y_d, ug_y, product_y, y_a)
    gug_own, r_own = feed_back(grad_down, hidden_all, own_d, ug_own, product_own, own_a)
    gugs, w_ugs = [gug_own, gug_x, gug_y, gug_d], [own_u, x_u, y_u, d_u]
    t_d, r_x, r_y, r_own, gugs = tie(t_d, r_x, r_y, r_own, gugs)

    r_x, r_y = add_half(r_x, t_d[1], True), add_half(r_y, t_d[0], False)
    r_x, r_y, gugs = tie(r_x, r_y, gugs)
    v_x, v_y = via(r_x, 1), via(r_y, 2)
    back_other = sum_dots(gugs, w_ugs, count, count, bf16)
    back_from = swap(back_other)
    back_own = sum_dots(gugs, w_ugs, 0, count, f32)
    grad_input_res, grad_branch_round, grad_branch_all, grad_alpha_attend = rowwise(
        hidden_back_kernel,
        "hidden_back",
        [x, branch_own, branch_from, alpha[0], grad_hidden_res, back_own, back_from],
        1,
        True,
    )
    grad_branch_all = fill(grad_branch_all, swap(grad_branch_round))
    grad_alpha = jnp.stack([jnp.sum(grad_alpha_attend, 0), jnp.sum(grad_alpha_feed, 0)])
    alpha_from = via(grad_alpha, 4)
    grad_qkv_1, keep_1, send_1 = group_1.back(grad_branch_all, x_all)
    v_x, v_y, grad_qkv_1, keep_1, send_1, grad_branch_all, alpha_from = tie(
        v_x, v_y, grad_qkv_1, keep_1, send_1, grad_branch_all, alpha_from
    )

    grad_alpha = grad_alpha + alpha_from
    alpha_from = via(grad_alpha, 1)
    feed_mine, feed_parts = column_sum(r_own, v_x, v_y, 112)
    feed_mine, feed_parts, send_1, grad_alpha, alpha_from = tie(feed_mine, feed_parts, send_1, grad_alpha, alpha_from)
    grad_alpha = grad_alpha + alpha_from
    z_feed = [via(feed_parts[0], 4), via(feed_parts[1], 8), via(feed_parts[2], 12)]
    other_1 = swap(send_1[0]), swap(send_1[1])
    a_x = jnp.concatenate([pick(rank, k, o) for k, o in zip(keep_1, other_1)], 0)
    a_d = tuple(pick(rank, o, k) for k, o in zip(keep_1, other_1))
    a_x, a_d, grad_branch_all = tie(a_x, a_d, grad_branch_all)

    t_a = via(a_d[0], 1), via(a_d[1], 2)
    grad_qkv_0, keep_0, send_0 = group_0.back(grad_branch_all, x_all)
    t_a, z_feed, grad_qkv_0, keep_0, send_0 = tie(t_a, z_feed, grad_qkv_0, keep_0, send_0)

    z_rest = via(feed_parts[3], 12)
    other_0 = swap(send_0[0]), swap(send_0[1])
    a_own = jnp.concatenate([pick(rank, k, o) for k, o in zip(keep_0, other_0)], 0)
    a_y = [pick(rank, o, k) for k, o in zip(keep_0, other_0)]
    a_y = jnp.concatenate([plus(a_y[0], t_a[0]), a_y[1]], 0)
    a_x = add_half(a_x, t_a[1], True)
    a_x, a_y, grad_qkv_0, grad_alpha = tie(a_x, a_y, grad_qkv_0, grad_alpha)
    b_x, b_y = via(a_x, 1), via(a_y, 2)
    alpha_from = via(grad_alpha, 2)
    grad_qkvs = [grad_qkv_0, grad_qkv_1]
    w_flats = [g.w.reshape(-1, width) for g in groups]
    input_other = sum_dots(grad_qkvs, w_flats, count, count, bf16)
    input_own = sum_dots(grad_qkvs, w_flats, 0, count, f32, grad_input_res)
    input_other, input_own, b_x, b_y, z_rest, alpha_from = tie(input_other, input_own, b_x, b_y, z_rest, alpha_from)
    z_feed = [z_feed[0], z_feed[1], jnp.concatenate([z_feed[2], z_rest], 0)]
    grad_alpha = grad_alpha + alpha_from

    attend_mine, attend_parts = column_sum(a_own, b_x, b_y)
    attend_mine, attend_parts, grad_alpha = tie(attend_mine, attend_parts, grad_alpha)
    alpha_from = via(grad_alpha, 8)
    attend_parts = [via(part, 4 * k) for part, k in zip(attend_parts, (1, 2, 3))]
    input_grad = input_own + swap(input_other).astype(f32)
    total = z_sum(feed_mine, z_feed)
    other = swap(total)
    low, high = pick(rank, total, other), pick(rank, other, total)
    feed_grad = jnp.concatenate([t[: 3 * units].reshape(3, units, width) for t in (low, high)], 1)
    feed_grad_s = jnp.concatenate([t[3 * units, : 2 * units].reshape(2, units) for t in (low, high)], 1)
    feed_change = adam_rows(feed_weights, feed_grad, feed_first, feed_second)
    attend_parts, alpha_from, input_grad, feed_grad, feed_change = tie(
        attend_parts, alpha_from, input_grad, feed_grad, feed_change
    )
    grad_alpha = grad_alpha + alpha_from
    grad_alpha = grad_alpha + swap(grad_alpha)
    own_alpha = lax.dynamic_slice_in_dim(grad_alpha, place * HEAD_DIM, HEAD_DIM, 1)

    total = z_sum(attend_mine, attend_parts)
    other = swap(total)
    low, high = pick(rank, total, other), pick(rank, other, total)
    attend_grad = jnp.concatenate([t[:body].reshape(4, rows, width) for t in (low, high)], 1)
    grad_qk = low[body] + high[body]
    grad_qk = jnp.concatenate([grad_qk[: HEAD_DIM // 2], grad_qk[HEAD_DIM : 3 * HEAD_DIM // 2]], 0)
    attend_grad_s = jnp.concatenate([grad_qk[None], own_alpha], 0)
    return (
        output.reshape(tokens.shape),
        input_grad.reshape(tokens.shape),
        attend_grad,
        feed_grad,
        attend_grad_s,
        feed_grad_s,
        adam_rows(attention_weights, attend_grad, attention_first, attention_second),
        feed_change,
        adam_change(attention_scales, attend_grad_s, attention_scale_first, attention_scale_second, False),
        adam_change(feed_scales, feed_grad_s, feed_scale_first, feed_scale_second, False),
    )


def local_any(
    tokens,
    segment_ids,
    cotangent,
    attention_weights,
    feed_weights,
    attention_scales,
    feed_scales,
    attention_first,
    attention_second,
    feed_first,
    feed_second,
    attention_scale_first,
    attention_scale_second,
    feed_scale_first,
    feed_scale_second,
):
    count, width = tokens.shape[0] * tokens.shape[1], tokens.shape[-1]
    rank = lax.axis_index("seq")
    x = tokens.reshape(count, width)
    x_all = jnp.concatenate([x, swap(x)], axis=0)
    tables = document_tables(segment_ids, rank, count)

    full = lax.all_gather(attention_weights.astype(bf16), "dp", axis=1, tiled=True)
    scales = lax.all_gather(attention_scales.astype(bf16), "dp", axis=1, tiled=True).astype(f32)
    half = width // 2
    alpha = scales[1:]
    mine = lax.dynamic_slice_in_dim(full, rank * half, half, 1)
    mine = jnp.swapaxes(mine.reshape(4, HEADS // 2, 2, HEAD_DIM // 2, width), 0, 1)
    own_scale = lax.dynamic_slice_in_dim(scales[0], rank * half, half, 0).reshape(HEADS // 2, HEAD_DIM)

    groups = []
    for g in range(2):
        heads = slice(4 * g, 4 * g + 4)
        tail = scale_row(own_scale[heads], jnp.zeros((2, HEAD_DIM)), jnp.zeros((4, 2 * PAIR)), width)
        low = jnp.concatenate([mine[heads, :, 0].reshape(4, -1, width), tail], 1).reshape(-1, width)
        high = jnp.concatenate([mine[heads, :, 1].reshape(4, -1, width), tail], 1).reshape(-1, width)
        groups.append(Group(tables, x_all, (low, high, high, low)))

    feed = lax.all_gather(own_half(feed_weights, rank, 1).astype(bf16), "dp", axis=1, tiled=True)
    feed_s = lax.all_gather(own_half(feed_scales, rank, 1).astype(bf16), "dp", axis=1, tiled=True).astype(f32)
    units = feed.shape[1] // 4
    w_ugs, w_ds, feed_scale = [], [], []
    for c in range(4):
        piece = feed[:2, c * units : (c + 1) * units].reshape(2, 4, units // 4, width)
        piece = jnp.swapaxes(piece, 0, 1).reshape(2 * units, width)
        w_ugs.append(piece)
        w_ds.append(feed[2, c * units : (c + 1) * units])
        piece = feed_s[:, c * units : (c + 1) * units].reshape(2, 4, units // 4)
        piece = jnp.swapaxes(piece, 0, 1).reshape(4, units // 2)
        tail = scale_row(jnp.zeros((4, HEAD_DIM)), jnp.zeros((2, HEAD_DIM)), piece, width)
        tail = jnp.concatenate([jnp.zeros((4, 2 * HEAD_DIM, width), bf16), tail], 1)
        feed_scale.append(tail.reshape(-1, width))

    mixtures, wos = [g.mixture for g in groups], [g.wo for g in groups]
    branch_other = sum_dots(mixtures, wos, count, count, bf16)
    branch_own, branch_from = sum_dots(mixtures, wos, 0, count, f32), swap(branch_other)
    hidden, hidden_round, hidden_all = rowwise(
        hidden_kernel, "hidden", [x, branch_own, branch_from, alpha[:1]], 1
    )
    hidden_all = fill(hidden_all, swap(hidden_round))
    hidden_other = hidden_all[count:]
    ugs, products = zip(
        *[up_gate(hidden_other, w, s, up_gate(hidden_round, w, s)) for w, s in zip(w_ugs, feed_scale)]
    )
    down_other = sum_dots(products, w_ds, count, count, bf16)
    down_own = sum_dots(products, w_ds, 0, count, f32)
    output, grad_hidden_res, grad_down_round, grad_down, grad_alpha_feed = rowwise(
        output_kernel,
        "output",
        [hidden, down_own, swap(down_other), alpha[1:], cotangent.reshape(count, width)],
        2,
        True,
    )
    grad_down = fill(grad_down, swap(grad_down_round))
    gugs, chunks = zip(
        *[
            feed_back(grad_down, hidden_all, w, ug, product, s)
            for w, ug, product, s in zip(w_ds, ugs, products, feed_scale)
        ]
    )
    back_other = sum_dots(gugs, w_ugs, count, count, bf16)
    back_own = sum_dots(gugs, w_ugs, 0, count, f32)
    grad_input_res, grad_branch_round, grad_branch_all, grad_alpha_attend = rowwise(
        hidden_back_kernel,
        "hidden_back",
        [x, branch_own, branch_from, alpha[:1], grad_hidden_res, back_own, swap(back_other)],
        1,
        True,
    )
    grad_branch_all = fill(grad_branch_all, swap(grad_branch_round))

    terms, term_scales = [], []
    for chunk in chunks:
        chunk = chunk.reshape(4, -1, width)
        body = chunk[:, : 3 * units // 4].reshape(4, 3, units // 4, width)
        terms.append(jnp.swapaxes(body, 0, 1).reshape(3, units, width))
        piece = chunk[:, 3 * units // 4, : units // 2].astype(f32).reshape(4, 2, units // 4)
        term_scales.append(jnp.swapaxes(piece, 0, 1).reshape(2, units))

    def scattered(values):
        return lax.psum_scatter(values, "dp", scatter_dimension=1, tiled=True)

    def both_halves(total):
        other = swap(total)
        return jnp.concatenate([pick(rank, total, other), pick(rank, other, total)], 1)

    feed_grad = both_halves(scattered(jnp.concatenate(terms, 1)).astype(f32))
    feed_grad_s = both_halves(scattered(jnp.concatenate(term_scales, 1)))

    grad_qkvs, gscales, pieces = [], [], []
    for group in groups:
        grad_qkv, keep, send = group.back(grad_branch_all, x_all)
        keep, send = jnp.concatenate(keep, 0), jnp.concatenate(send, 0)
        halves = jnp.stack([pick(rank, keep, send), pick(rank, send, keep)]).reshape(2, 4, ROWS, width)
        scale = jnp.sum(halves[:, :, 2 * HEAD_DIM].astype(f32), 0)
        scale = jnp.concatenate([scale[:, : HEAD_DIM // 2], scale[:, HEAD_DIM : 3 * HEAD_DIM // 2]], 1)
        halves = halves[:, :, : 2 * HEAD_DIM].reshape(2, 4, 4, HEAD_DIM // 2, width)
        pieces.append(jnp.transpose(halves, (2, 1, 0, 3, 4)).reshape(4, 4 * HEAD_DIM, width))
        grad_qkvs.append(grad_qkv)
        gscales.append(scale.reshape(1, -1))
    w_flats = [g.w.reshape(-1, width) for g in groups]
    input_other = sum_dots(grad_qkvs, w_flats, count, count, bf16)
    input_own = sum_dots(grad_qkvs, w_flats, 0, count, f32)
    input_grad = grad_input_res + input_own + swap(input_other).astype(f32)

    total = jnp.zeros((4, width, width), bf16)
    total = scattered(lax.dynamic_update_slice(total, jnp.concatenate(pieces, 1), (0, rank * half, 0)))
    attend_grad = total.astype(f32) + swap(total.astype(f32))
    qk = jnp.zeros((1, width), f32)
    qk = lax.dynamic_update_slice(qk, jnp.concatenate(gscales, 1), (0, rank * half))
    total = jnp.concatenate(
        [qk, jnp.sum(grad_alpha_attend, 0)[None], jnp.sum(grad_alpha_feed, 0)[None]], 0
    )
    total = scattered(total)
    attend_grad_s = total + swap(total)
    return (
        output.reshape(tokens.shape),
        input_grad.reshape(tokens.shape),
        attend_grad,
        feed_grad,
        attend_grad_s,
        feed_grad_s,
        adam_rows(attention_weights, attend_grad, attention_first, attention_second),
        adam_rows(feed_weights, feed_grad, feed_first, feed_second),
        adam_change(attention_scales, attend_grad_s, attention_scale_first, attention_scale_second, False),
        adam_change(feed_scales, feed_grad_s, feed_scale_first, feed_scale_second, False),
    )


def solution(mesh):
    rows = P("dp", "seq", None)
    matrix = P(None, "dp", None)
    scale = P(None, "dp")
    return jax.shard_map(
        local_sixteen if mesh.shape["dp"] == HEADS else local_any,
        mesh=mesh,
        in_specs=(rows, P("dp", None), rows, matrix, matrix, scale, scale)
        + (matrix,) * 4
        + (scale,) * 4,
        out_specs=(rows, rows, matrix, matrix, scale, scale, matrix, matrix, scale, scale),
        check_vma=False,
    )
```
